32 devices in a mesh: dp: 2 (over core), row: 4 (over z), col: 4 (over y, x).
Axes of the slice: x: 2, y: 2, z: 4, core: 2. Of those that a mesh axis runs over, the one named last changes fastest.
Arguments:
- tokens: bfloat16 [1024, 8192], P('col', ('dp', 'row')), may hold values from -6.5 to 6.5
- w_qkv: bfloat16 [1024, 3, 1024], P('col', None, 'row'), may hold values from -0.1875 to 0.1875
- b_qv: bfloat16 [2, 1024], P(None, 'row'), may hold values from -0.59765625 to 0.59765625
- w_out: bfloat16 [1024, 1024], P('row', 'col'), may hold values from -1.5 to 1.5
- b_out: bfloat16 [1024], P('col'), may hold values from -2 to 2
- norm1_gain: bfloat16 [1024], P('col'), may hold values from 0.25 to 1.75
- norm1_shift: bfloat16 [1024], P('col'), may hold values from -2 to 2
- w_up: bfloat16 [1024, 4096], P('col', 'row'), may hold values from -0.1875 to 0.1875
- b_up: bfloat16 [4096], P('row'), may hold values from -3 to 3
- w_down: bfloat16 [4096, 1024], P('row', 'col'), may hold values from -0.09375 to 0.09375
- b_down: bfloat16 [1024], P('col'), may hold values from -2 to 2
- norm2_gain: bfloat16 [1024], P('col'), may hold values from 0.25 to 1.75
- norm2_shift: bfloat16 [1024], P('col'), may hold values from -2 to 2
- cotangent: bfloat16 [1024, 8192], P('col', ('dp', 'row')), may hold values from -6 to 6
Outputs:
- out: bfloat16 [1024, 8192], P('col', ('dp', 'row'))
- grad_tokens: float32 [1024, 8192], P('col', ('dp', 'row'))
- grad_w_qkv: float32 [1024, 3, 1024], P('col', None, 'row')
- grad_b_qv: float32 [2, 1024], P(None, 'row')
- grad_w_out: float32 [1024, 1024], P('row', 'col')
- grad_b_out: float32 [1024], P('col')
- grad_norm1_gain: float32 [1024], P('col')
- grad_norm1_shift: float32 [1024], P('col')
- grad_w_up: float32 [1024, 4096], P('col', 'row')
- grad_b_up: float32 [4096], P('row')
- grad_w_down: float32 [4096, 1024], P('row', 'col')
- grad_b_down: float32 [1024], P('col')
- grad_norm2_gain: float32 [1024], P('col')
- grad_norm2_shift: float32 [1024], P('col')
The draws below stay inside these ranges and needn't reach their ends.
All inputs are finite; a program needn't handle non-finite values.
Results may differ from the reference program's by a relative error of at most 0.014.
Values may be sent and summed in bfloat16 or wider, within the bound.
No kernel may reach another device: no remote copies, remote signals or barrier semaphores. Data moves between devices by JAX's collectives and lax.ppermute only.
A program may use at most 256 MiB of HBM per device.

```python
import jax
import jax.numpy as jnp
from jax import lax

D = 1024
HEADS = 16
HEAD_DIM = 64
FF = 4096
SEQ = 1024
TOKENS = 8192


def draw_tokens(key, part):
    key = jax.random.fold_in(key, 11)
    profile = jnp.exp(jnp.log(0.6) + jnp.log(3.0) * jnp.arange(D, dtype=jnp.float32) / (D - 1))
    base = jax.random.truncated_normal(key, -3.5, 3.5, (D, TOKENS), jnp.float32)
    return (base * profile[:, None]).astype(jnp.bfloat16)


def steps_of(key, dims, cuts, least, largest):
    gain, own = 1.0, jax.random.fold_in(key, 6)
    for dim, blocks in cuts:
        draws = jnp.exp(jax.random.uniform(jax.random.fold_in(own, dim), (blocks,), jnp.float32, least / len(cuts), largest / len(cuts)))
        gain = gain * jnp.repeat(draws, dims[dim] // blocks).reshape([-1 if axis == dim else 1 for axis in range(len(dims))])
    return gain


def noise(key, shape, width, reach, shards=(), held_as=jnp.bfloat16):
    factor_of = steps_of(key, shape, shards, -0.22, 0.18) if shards else 1.0
    entries = jax.random.normal(key, shape, jnp.float32) * width * factor_of
    return jnp.minimum(jnp.maximum(entries, -reach), reach).astype(held_as)


def setup_inputs(seed: int = 0) -> dict:
    splits = jax.random.split(jax.random.key(seed), 15)
    tokens = draw_tokens(jax.random.fold_in(splits[14], 71), 0)
    w_qkv = noise(splits[1], (D, 3, D), D ** -0.5, 0.1875, ((0, 4), (2, 4)))
    b_qv = noise(splits[2], (2, D), 0.1, 0.59765625, ((1, 4),))
    w_out = noise(splits[3], (D, D), (max(D // 64, 1)) ** -0.5, 1.5, ((0, 4), (1, 4)))
    b_out = noise(splits[4], (D,), 0.3, 2.0, ((0, 4),))
    norm1_gain = jnp.clip(1.0 + 0.15 * jax.random.normal(splits[5], (D,), jnp.float32), 0.25, 1.75).astype(jnp.bfloat16)
    norm1_shift = noise(splits[6], (D,), 0.3, 2.0, ((0, 4),))
    w_up = noise(splits[7], (D, FF), D ** -0.5, 0.1875, ((0, 4), (1, 4)))
    b_up = noise(splits[8], (FF,), 0.5, 3.0, ((0, 4),))
    w_down = noise(splits[9], (FF, D), FF ** -0.5, 0.09375, ((0, 4), (1, 4)))
    b_down = noise(splits[10], (D,), 0.3, 2.0, ((0, 4),))
    norm2_gain = jnp.clip(1.0 + 0.15 * jax.random.normal(splits[11], (D,), jnp.float32), 0.25, 1.75).astype(jnp.bfloat16)
    norm2_shift = noise(splits[12], (D,), 0.3, 2.0, ((0, 4),))
    cotangent = noise(splits[13], (D, TOKENS), 1.0, 6.0, ((0, 4), (1, 8)))
    return dict(tokens=tokens, w_qkv=w_qkv, b_qv=b_qv, w_out=w_out, b_out=b_out, norm1_gain=norm1_gain, norm1_shift=norm1_shift, w_up=w_up, b_up=b_up, w_down=w_down, b_down=b_down, norm2_gain=norm2_gain, norm2_shift=norm2_shift, cotangent=cotangent)


@jax.custom_vjp
def low(v):
    return lax.optimization_barrier(v.astype(jnp.bfloat16)).astype(jnp.float32)

@jax.custom_vjp
def low_back(v):
    return v

def low_keep(v):
    return (low(v), None)

def low_pass(kept, grad):
    return (grad,)

def back_keep(v):
    return (v, None)

def back_low(kept, grad):
    return (low(grad),)
low.defvjp(low_keep, low_pass)
low_back.defvjp(back_keep, back_low)
norm_eps = 1e-05

def product(first_mat, second_mat):
    return jnp.dot(first_mat, second_mat, precision=lax.Precision.HIGHEST, preferred_element_type=jnp.float32)

def layer_norm(residual, gain_vec, shift_vec):
    mean_rows = lax.optimization_barrier(jnp.mean(residual, axis=-1, keepdims=True))
    spread = lax.optimization_barrier(jnp.mean(residual * residual, axis=-1, keepdims=True)) - mean_rows * mean_rows
    return (residual - mean_rows) * lax.rsqrt(spread + norm_eps) * gain_vec + shift_vec

def attend(queries, key_rows, value_rows):
    scores = low_back(jnp.einsum('qhd,khd->hqk', queries, key_rows, precision=lax.Precision.HIGHEST))
    weights = low(jax.nn.softmax(scores, axis=-1))
    return jnp.einsum('hqk,khd->qhd', weights, value_rows, precision=lax.Precision.HIGHEST)

def encoder_layer(inputs, w_qkv, b_qv, w_out, b_out, norm1_gain, norm1_shift, w_up, b_up, w_down, b_down, norm2_gain, norm2_shift):
    projected = product(low(inputs), w_qkv.reshape(D, 3 * D)).reshape(SEQ, 3, D)
    queries = low_back(low((projected[:, 0] + b_qv[0]) * HEAD_DIM ** (-0.5)))
    key_rows = low_back(low(projected[:, 1]))
    value_rows = low_back(low(projected[:, 2] + b_qv[1]))
    attended = jax.checkpoint(attend)(queries.reshape(SEQ, HEADS, HEAD_DIM), key_rows.reshape(SEQ, HEADS, HEAD_DIM), value_rows.reshape(SEQ, HEADS, HEAD_DIM))
    attended = low_back(low(attended.reshape(SEQ, D)))
    attn_out = low_back(product(attended, w_out)) + b_out
    normed_a = layer_norm(inputs + attn_out, norm1_gain, norm1_shift)
    pre_act = low_back(product(low(normed_a), w_up) + b_up)
    hidden = low(jax.nn.gelu(pre_act, approximate=False))
    branch_out = low_back(product(hidden, w_down)) + b_down
    return layer_norm(normed_a + branch_out, norm2_gain, norm2_shift)

def reference(tokens, w_qkv, b_qv, w_out, b_out, norm1_gain, norm1_shift, w_up, b_up, w_down, b_down, norm2_gain, norm2_shift, cotangent):
    params = (w_qkv.astype(jnp.float32), b_qv.astype(jnp.float32), w_out.astype(jnp.float32), b_out.astype(jnp.float32), norm1_gain.astype(jnp.float32), norm1_shift.astype(jnp.float32), w_up.astype(jnp.float32), b_up.astype(jnp.float32), w_down.astype(jnp.float32), b_down.astype(jnp.float32), norm2_gain.astype(jnp.float32), norm2_shift.astype(jnp.float32))
    inputs = tokens.astype(jnp.float32).T.reshape(TOKENS // SEQ, SEQ, D)
    cotangents = cotangent.astype(jnp.float32).T.reshape(TOKENS // SEQ, SEQ, D)
    zero_sums = tuple((jnp.zeros(param.shape, jnp.float32) for param in params))

    def one_sequence(totals, pieces):
        seq_in, seq_cot = pieces
        result, pullback = jax.vjp(encoder_layer, seq_in, *params)
        gradients = pullback(seq_cot)
        return (tuple((left_sum + new_sum for left_sum, new_sum in zip(totals, gradients[1:]))), (result, gradients[0]))
    totals, (outputs, grad_inputs) = lax.scan(one_sequence, zero_sums, (inputs, cotangents))
    return (outputs.reshape(TOKENS, D).T.astype(jnp.bfloat16), grad_inputs.reshape(TOKENS, D).T, totals[0], totals[1], totals[2], totals[3], totals[4], totals[5], totals[6], totals[7], totals[8], totals[9], totals[10], totals[11])
```

```python
import jax
import jax.numpy as jnp
from jax import lax
from jax.experimental import pallas as pl
from jax.experimental.pallas import tpu as pltpu
from jax.sharding import Mesh
from jax.sharding import PartitionSpec as P

D = 1024
HEAD_DIM = 64
SEQ = 1024


norm_eps = 1e-05


def matmul(first_mat, second_mat):
    return jnp.dot(first_mat, second_mat, preferred_element_type=jnp.float32)


def against(first_mat, second_mat):
    return lax.dot_general(
        first_mat, second_mat, (((1,), (1,)), ((), ())), preferred_element_type=jnp.float32
    )


def inner_rows(first_mat, second_mat):
    return lax.dot_general(
        first_mat, second_mat, (((0,), (0,)), ((), ())), preferred_element_type=jnp.float32
    )


def by_row(values):
    return lax.all_gather(values, "row", axis=0, tiled=True)


def by_col(values):
    return lax.all_gather(values, "col", axis=0, tiled=True)


def reduce_col(source, weight, transposed):
    row_count = source.shape[0] // lax.axis_size("col")

    def partial_value(row_start, row_num):
        return against(source, weight) if transposed else matmul(source, weight)

    return lax.psum_scatter(
        partial_value(jnp.int32(0), row_count * lax.axis_size("col")),
        "col",
        scatter_dimension=0,
        tiled=True,
    )


def reduce_row(source, weight, transposed):
    row_count = source.shape[0] // lax.axis_size("row")

    def partial_value(row_start, row_num):
        return against(source, weight) if transposed else matmul(source, weight)

    return lax.psum_scatter(
        partial_value(jnp.int32(0), row_count * lax.axis_size("row")),
        "row",
        scatter_dimension=0,
        tiled=True,
    )


def feature_totals(first_terms, second_terms):
    return lax.psum((jnp.sum(first_terms, axis=1), jnp.sum(second_terms, axis=1)), "col")


def norm_forward(residual, gain_vec, shift_vec):
    totals = feature_totals(residual, residual * residual)
    mean_rows = totals[0][:, None] / D
    spread = totals[1][:, None] / D - mean_rows * mean_rows
    scale_rows = lax.rsqrt(spread + norm_eps)
    normed = (residual - mean_rows) * scale_rows
    return (normed * gain_vec + shift_vec, normed, scale_rows)


def norm_backward(grad_in, normed, scale_rows, gain_vec):
    scaled = grad_in * gain_vec
    totals = feature_totals(scaled, scaled * normed)
    grad_resid = scale_rows * (scaled - totals[0][:, None] / D - normed * (totals[1][:, None] / D))
    return (grad_resid, jnp.sum(grad_in * normed, axis=0), jnp.sum(grad_in, axis=0))


def gelu_exact(values):
    return jax.nn.gelu(values, approximate=False)


def by_heads(values, head_count):
    seq_count = values.shape[0] // SEQ
    return values.reshape(seq_count, SEQ, head_count, HEAD_DIM)


def attention_forward(queries, key_seq, value_seq):
    block_len = min(512, SEQ)
    outputs = []
    log_parts = []
    for offset in range(0, SEQ, block_len):
        query_block = queries[:, offset : offset + block_len]
        scores = jnp.einsum(
            "nqhd,nkhd->nhqk", query_block, key_seq, preferred_element_type=jnp.float32
        )
        row_max = jnp.max(scores, axis=-1, keepdims=True)
        exp_scores = jnp.exp(scores - row_max)
        denom = jnp.sum(exp_scores, axis=-1, keepdims=True)
        probs_low = (exp_scores / denom).astype(jnp.bfloat16)
        outputs.append(
            jnp.einsum("nhqk,nkhd->nqhd", probs_low, value_seq, preferred_element_type=jnp.float32)
        )
        log_parts.append(row_max + jnp.log(denom))
    attended = jnp.concatenate(outputs, axis=1)
    rows_here = attended.shape[0] * SEQ
    return (
        attended.reshape(rows_here, -1).astype(jnp.bfloat16),
        jnp.concatenate(log_parts, axis=2),
    )


def attention_backward(queries, key_seq, value_seq, grad_seq, log_norm):
    block_len = min(512, SEQ)
    grad_query_parts = []
    grad_key = jnp.zeros(key_seq.shape, jnp.float32)
    grad_value = jnp.zeros(value_seq.shape, jnp.float32)
    for offset in range(0, SEQ, block_len):
        query_block = queries[:, offset : offset + block_len]
        grad_block = grad_seq[:, offset : offset + block_len]
        scores = jnp.einsum(
            "nqhd,nkhd->nhqk", query_block, key_seq, preferred_element_type=jnp.float32
        )
        probs = jnp.exp(scores - log_norm[:, :, offset : offset + block_len])
        grad_probs = jnp.einsum(
            "nqhd,nkhd->nhqk", grad_block, value_seq, preferred_element_type=jnp.float32
        )
        row_delta = jnp.sum(grad_probs * probs, axis=-1, keepdims=True)
        grad_scores = (probs * (grad_probs - row_delta)).astype(jnp.bfloat16)
        grad_query_parts.append(
            jnp.einsum("nhqk,nkhd->nqhd", grad_scores, key_seq, preferred_element_type=jnp.float32)
        )
        grad_key = grad_key + jnp.einsum(
            "nhqk,nqhd->nkhd", grad_scores, query_block, preferred_element_type=jnp.float32
        )
        grad_value = grad_value + jnp.einsum(
            "nhqk,nqhd->nkhd",
            probs.astype(jnp.bfloat16),
            grad_block,
            preferred_element_type=jnp.float32,
        )
    grad_query = jnp.concatenate(grad_query_parts, axis=1)
    rows_here = grad_query.shape[0] * SEQ
    return (
        grad_query.reshape(rows_here, -1).astype(jnp.bfloat16),
        grad_key.reshape(rows_here, -1).astype(jnp.bfloat16),
        grad_value.reshape(rows_here, -1).astype(jnp.bfloat16),
    )


def shards(
    tokens,
    w_qkv,
    b_qv,
    w_out,
    b_out,
    norm1_gain,
    norm1_shift,
    w_up,
    b_up,
    w_down,
    b_down,
    norm2_gain,
    norm2_shift,
    cotangent,
):
    token_major = tokens.T
    width_col = token_major.shape[1]
    width_row = w_out.shape[0]
    qkv_weight = w_qkv.reshape(width_col, 3 * width_row)
    query_scale = HEAD_DIM ** (-0.5)
    head_count = width_row // HEAD_DIM
    gathered_in = by_row(token_major)
    projected = reduce_col(gathered_in, qkv_weight, False).reshape(-1, 3, width_row)
    queries = ((projected[:, 0] + b_qv[0]) * query_scale).astype(jnp.bfloat16)
    key_rows = projected[:, 1].astype(jnp.bfloat16)
    value_rows = (projected[:, 2] + b_qv[1]).astype(jnp.bfloat16)
    query_seq = by_heads(queries, head_count)
    key_seq = by_heads(key_rows, head_count)
    value_seq = by_heads(value_rows, head_count)
    attended, log_norm = attention_forward(query_seq, key_seq, value_seq)
    gathered_att = by_col(attended)
    attn_out = reduce_row(gathered_att, w_out, False) + b_out
    residual1 = token_major.astype(jnp.float32) + attn_out
    normed_a, normed1, scale1 = norm_forward(residual1, norm1_gain, norm1_shift)
    low_a = normed_a.astype(jnp.bfloat16)
    gathered_a = by_row(low_a)
    pre_act = reduce_col(gathered_a, w_up, False) + b_up
    hidden, gelu_pull = jax.vjp(gelu_exact, pre_act)
    hidden_low = hidden.astype(jnp.bfloat16)
    gathered_h = by_col(hidden_low)
    branch_out = reduce_row(gathered_h, w_down, False)
    residual2 = normed_a + branch_out + b_down
    result, normed2, scale2 = norm_forward(residual2, norm2_gain, norm2_shift)
    grad_out = cotangent.T.astype(jnp.float32)
    grad_r2, gain2_part, shift2_part = norm_backward(grad_out, normed2, scale2, norm2_gain)
    down_bias_part = jnp.sum(grad_r2, axis=0)
    grad_branch = grad_r2.astype(jnp.bfloat16)
    gathered_df = by_row(grad_branch)
    down_grad = inner_rows(gathered_h, gathered_df)
    grad_hidden = reduce_col(gathered_df, w_down, True)
    grad_pre = gelu_pull(grad_hidden)[0].astype(jnp.bfloat16)
    gathered_dz = by_col(grad_pre)
    up_grad = inner_rows(gathered_a, gathered_dz)
    up_bias_grad = jnp.sum(gathered_dz, axis=0, dtype=jnp.float32)
    grad_a_ff = reduce_row(gathered_dz, w_up, True)
    grad_a = grad_r2 + grad_a_ff
    grad_r1, gain1_part, shift1_part = norm_backward(grad_a, normed1, scale1, norm1_gain)
    out_bias_part = jnp.sum(grad_r1, axis=0)
    gathered_datt = by_row(grad_r1.astype(jnp.bfloat16))
    out_grad = inner_rows(gathered_att, gathered_datt)
    grad_attended = reduce_col(gathered_datt, w_out, True).astype(jnp.bfloat16)
    grad_seq = by_heads(grad_attended, head_count)
    grad_query, grad_key, grad_value = attention_backward(
        query_seq, key_seq, value_seq, grad_seq, log_norm
    )
    grad_proj = jnp.stack([grad_query * query_scale, grad_key, grad_value], axis=1).reshape(
        -1, 3 * width_row
    )
    gathered_dqkv = by_col(grad_proj)
    qkv_grad = inner_rows(gathered_in, gathered_dqkv).reshape(width_col, 3, width_row)
    bias_rows = jnp.sum(gathered_dqkv, axis=0, dtype=jnp.float32).reshape(3, width_row)
    qv_bias_grad = jnp.stack([bias_rows[0], bias_rows[2]])
    grad_input = reduce_row(gathered_dqkv, qkv_weight, True) + grad_r1
    norm_sums = lax.psum(
        (gain1_part, shift1_part, gain2_part, shift2_part, out_bias_part, down_bias_part),
        ("dp", "row"),
    )
    weight_sums = lax.psum(
        (qkv_grad, qv_bias_grad, out_grad, up_grad, up_bias_grad, down_grad), "dp"
    )
    return (
        result.astype(jnp.bfloat16).T,
        grad_input.T,
        weight_sums[0],
        weight_sums[1],
        weight_sums[2],
        norm_sums[4],
        norm_sums[0],
        norm_sums[1],
        weight_sums[3],
        weight_sums[4],
        weight_sums[5],
        norm_sums[5],
        norm_sums[2],
        norm_sums[3],
    )


BF = jnp.bfloat16
F32 = jnp.float32
PAIR = ((0, 1), (1, 0))
VMEM_BYTES = 48 * 1024 * 1024


def flip(values, axis_name):
    return lax.ppermute(values, axis_name, PAIR)


def shift(values, axis_name, step):
    size = lax.axis_size(axis_name)
    return lax.ppermute(values, axis_name, [(i, (i + step) % size) for i in range(size)])


def in_order(index, mine, other, axis):
    first = jnp.where(index == 0, mine, other)
    second = jnp.where(index == 0, other, mine)
    return jnp.concatenate([first, second], axis)


def four_in_order(low_bit, high_bit, parts, axis):
    low = [jnp.where(low_bit == 0, parts[i], parts[i ^ 1]) for i in range(4)]
    full = [jnp.where(high_bit == 0, low[i], low[i ^ 2]) for i in range(4)]
    return jnp.concatenate(full, axis)


def cut(values, index, size, axis):
    return lax.dynamic_slice_in_dim(values, index * size, size, axis)


def attend_kernel(qkv_ref, out_ref, norm_ref):
    key_t = qkv_ref[0, 1].T
    value = qkv_ref[0, 2]
    step = 256
    for start in range(0, SEQ, step):
        here = slice(start, start + step)
        scores = matmul(key_t, qkv_ref[0, 0, :, here])
        top = jnp.max(scores, axis=0, keepdims=True)
        weights = jnp.exp(scores - top)
        denom = jnp.sum(weights, axis=0, keepdims=True)
        low = (weights * (1.0 / denom)).astype(BF)
        out_ref[0, :, here] = matmul(value, low).astype(BF)
        norm_ref[0, :, here] = top + jnp.log(denom)


def attend(qkv):
    heads = qkv.shape[0]
    return pl.pallas_call(
        attend_kernel,
        grid=(heads,),
        in_specs=[pl.BlockSpec((1, 3, HEAD_DIM, SEQ), lambda h: (h, 0, 0, 0))],
        out_specs=[
            pl.BlockSpec((1, HEAD_DIM, SEQ), lambda h: (h, 0, 0)),
            pl.BlockSpec((1, 1, SEQ), lambda h: (h, 0, 0)),
        ],
        out_shape=[
            jax.ShapeDtypeStruct((heads, HEAD_DIM, SEQ), BF),
            jax.ShapeDtypeStruct((heads, 1, SEQ), F32),
        ],
        compiler_params=pltpu.CompilerParams(vmem_limit_bytes=VMEM_BYTES),
        name="attend",
    )(qkv)


def attend_back_kernel(qkv_ref, grad_ref, norm_ref, out_ref):
    key = qkv_ref[0, 1]
    key_t = key.T
    value_t = qkv_ref[0, 2].T
    step = 256
    grad_key = jnp.zeros((SEQ, HEAD_DIM), F32)
    grad_value = jnp.zeros((SEQ, HEAD_DIM), F32)
    for start in range(0, SEQ, step):
        here = slice(start, start + step)
        query = qkv_ref[0, 0, :, here]
        grad = grad_ref[0, :, here]
        probs = jnp.exp(matmul(key_t, query) - norm_ref[0, :, here])
        grad_probs = matmul(value_t, grad)
        delta = jnp.sum(grad_probs * probs, axis=0, keepdims=True)
        grad_scores = (probs * (grad_probs - delta)).astype(BF)
        grad_query = matmul(key, grad_scores).astype(BF)
        out_ref[0, 0, :, here] = (grad_query.astype(F32) * HEAD_DIM**-0.5).astype(BF)
        grad_key = grad_key + matmul(grad_scores, query.T)
        grad_value = grad_value + matmul(probs.astype(BF), grad.T)
    out_ref[0, 1] = grad_key.T.astype(BF)
    out_ref[0, 2] = grad_value.T.astype(BF)


def attend_back(qkv, grad, log_norm):
    heads = qkv.shape[0]
    return pl.pallas_call(
        attend_back_kernel,
        grid=(heads,),
        in_specs=[
            pl.BlockSpec((1, 3, HEAD_DIM, SEQ), lambda h: (h, 0, 0, 0)),
            pl.BlockSpec((1, HEAD_DIM, SEQ), lambda h: (h, 0, 0)),
            pl.BlockSpec((1, 1, SEQ), lambda h: (h, 0, 0)),
        ],
        out_specs=pl.BlockSpec((1, 3, HEAD_DIM, SEQ), lambda h: (h, 0, 0, 0)),
        out_shape=jax.ShapeDtypeStruct(qkv.shape, BF),
        compiler_params=pltpu.CompilerParams(vmem_limit_bytes=VMEM_BYTES),
        name="attend_back",
    )(qkv, grad, log_norm)


def norm_rows(residual, gain_vec, shift_vec):
    mean_rows = jnp.mean(residual, axis=1, keepdims=True)
    spread = jnp.mean(residual * residual, axis=1, keepdims=True) - mean_rows * mean_rows
    scale_rows = lax.rsqrt(spread + norm_eps)
    normed = (residual - mean_rows) * scale_rows
    return normed * gain_vec + shift_vec, normed, scale_rows


def norm_rows_back(grad_in, normed, scale_rows, gain_vec):
    scaled = grad_in * gain_vec
    first = jnp.mean(scaled, axis=1, keepdims=True)
    second = jnp.mean(scaled * normed, axis=1, keepdims=True)
    grad_resid = scale_rows * (scaled - first - normed * second)
    return grad_resid, jnp.sum(grad_in * normed, axis=0), jnp.sum(grad_in, axis=0)


def gather_pair(own):
    far = flip(own, "t")
    near = flip(own, "dp")
    return jnp.concatenate([own, near]), jnp.concatenate([far, flip(far, "dp")])


def sum_pair(near_part, far_part, rows):
    far_sum = far_part[:rows].astype(F32) + flip(far_part[rows:].astype(BF), "dp").astype(F32)
    sent = flip(far_sum.astype(BF), "t")
    return near_part[:rows] + flip(near_part[rows:].astype(BF), "dp").astype(F32) + sent.astype(F32)


def gather_rows(payload):
    size = lax.axis_size("row")
    return jnp.stack([payload] + [shift(payload, "row", step) for step in range(1, size)])


def reduce_weights(grads, u_index):
    size, _, width = grads.shape
    half = width // 2
    sent = flip(cut(grads, 1 - u_index, half, 2).astype(BF), "u")
    both = cut(grads, u_index, half, 2).astype(F32) + sent.astype(F32)
    total = both[0]
    for step in range(1, size):
        total = total + shift(both[step].astype(BF), "row", -step).astype(F32)
    return total


def spread_weights(total, t_index, core):
    half = total.shape[1] // 2
    mine = cut(total, t_index, half, 1)
    other = flip(cut(total, 1 - t_index, half, 1).astype(BF), "t")
    near = jnp.stack([mine.astype(BF), other])
    far = flip(near, "dp")
    return [mine, far[0].astype(F32), other.astype(F32), far[1].astype(F32)]


def fast_shards(
    tokens,
    w_qkv,
    b_qv,
    w_out,
    b_out,
    norm1_gain,
    norm1_shift,
    w_up,
    b_up,
    w_down,
    b_down,
    norm2_gain,
    norm2_shift,
    cotangent,
):
    core, chip = lax.axis_index("dp"), lax.axis_index("t")
    u_index, row = lax.axis_index("u"), lax.axis_index("row")
    rows = lax.axis_size("row")
    quarter = 2 * chip + core
    other_quarter = 2 * (1 - chip) + core
    feats = tokens.shape[0]
    own_rows = SEQ // 4
    swap_cores = [(2 * d + u, 2 * u + d) for d in range(2) for u in range(2)]
    scale = HEAD_DIM**-0.5

    tokens_here = lax.ppermute(tokens, ("dp", "u"), swap_cores)
    tokens_far = flip(tokens_here, "t")
    tokens_near = flip(tokens_here, "dp")
    tokens_both = flip(tokens_far, "dp")
    x_t = four_in_order(chip, core, [tokens_here, tokens_far, tokens_near, tokens_both], 0)

    qkv_local = w_qkv.transpose(1, 2, 0).reshape(3, 4, -1, feats)
    out_local = w_out.reshape(4, -1, feats)
    up_local = w_up.T.reshape(4, -1, feats)
    down_local = w_down.reshape(4, -1, feats)
    head_rows = qkv_local.shape[2]
    qkv_rows, out_rows, ff_rows = 3 * head_rows, out_local.shape[1], up_local.shape[1]

    def pick_qkv(index):
        return lax.dynamic_index_in_dim(qkv_local, index, 1, False).reshape(qkv_rows, feats)

    def pick(array, index):
        return lax.dynamic_index_in_dim(array, index, 0, False)

    vectors = jnp.stack([b_out, norm1_gain, norm1_shift, b_down, norm2_gain, norm2_shift])
    vectors = jnp.pad(vectors, ((0, 2), (0, 0)))
    attn_keep = jnp.concatenate([pick_qkv(quarter), vectors, pick(out_local, quarter)])
    attn_send = jnp.concatenate([pick_qkv(other_quarter), vectors, pick(out_local, other_quarter)])
    attn_both = in_order(chip, attn_keep, flip(attn_send, "t"), 1)
    ff_keep = jnp.concatenate([pick(up_local, quarter), pick(down_local, quarter)])
    ff_send = jnp.concatenate([pick(up_local, other_quarter), pick(down_local, other_quarter)])
    ff_both = in_order(chip, ff_keep, flip(ff_send, "t"), 1)
    width = attn_both.shape[1]

    qv_own = pick(b_qv.reshape(2, 4, -1).transpose(1, 0, 2), quarter).reshape(-1)
    up_own = pick(b_up.reshape(4, -1), quarter)
    biases = jnp.pad(jnp.concatenate([qv_own, up_own]), (0, width - qv_own.size - up_own.size))
    biases = jnp.pad(biases[None], ((0, 7), (0, 0)))
    qkv_gathered = gather_rows(jnp.concatenate([attn_both[:qkv_rows], biases]))
    vectors_both = attn_both[qkv_rows : qkv_rows + 8]
    sent = jnp.concatenate([qkv_gathered[:, :qkv_rows].reshape(-1, width), vectors_both])
    qkv_full = in_order(u_index, sent, flip(sent, "u"), 1)
    qkv_full, vec = qkv_full[: rows * qkv_rows], qkv_full[rows * qkv_rows :].astype(F32)
    bias_rows = qkv_gathered[:, qkv_rows].astype(F32)
    bias_q, bias_v = bias_rows[:, :head_rows], bias_rows[:, head_rows : 2 * head_rows]
    bias_up = bias_rows[:, 2 * head_rows : 2 * head_rows + ff_rows].reshape(1, -1)

    def gather_weight(payload):
        gathered = gather_rows(payload).reshape(-1, width)
        return in_order(u_index, gathered, flip(gathered, "u"), 1)

    out_full = gather_weight(attn_both[qkv_rows + 8 :])
    up_full = gather_weight(ff_both[:ff_rows])
    down_full = gather_weight(ff_both[ff_rows:])

    projected = matmul(qkv_full, x_t).reshape(rows, 3, head_rows, SEQ)
    qkv = jnp.stack(
        [
            (projected[:, 0] + bias_q[:, :, None]) * scale,
            projected[:, 1],
            projected[:, 2] + bias_v[:, :, None],
        ],
        axis=1,
    ).astype(BF)
    attended, log_norm = attend(qkv)
    attended = attended.reshape(rows * head_rows, SEQ)
    attended = jnp.concatenate([cut(attended, quarter ^ j, own_rows, 1) for j in range(4)], 1)
    half = SEQ // 2
    far_out = inner_rows(attended[:, half:], out_full)
    near_out = inner_rows(attended[:, :half], out_full)
    attn_out = sum_pair(near_out, far_out, own_rows) + vec[0]
    residual1 = cut(x_t, quarter, own_rows, 1).T.astype(F32) + attn_out
    normed_a, normed1, scale1 = norm_rows(residual1, vec[1], vec[2])

    near_a, far_a = gather_pair(normed_a.astype(BF))

    def up(rows_in):
        pre = against(rows_in, up_full) + bias_up
        cdf = 0.5 * (1.0 + lax.erf(pre * (0.5**0.5)))
        slope = cdf + pre * (jnp.exp(-0.5 * pre * pre) * 0.3989422804014327)
        return (pre * cdf).astype(BF), slope

    hidden_near, slope_near = up(near_a)
    hidden_far, slope_far = up(far_a)
    far_branch = matmul(hidden_far, down_full)
    near_branch = matmul(hidden_near, down_full)
    residual2 = normed_a + sum_pair(near_branch, far_branch, own_rows) + vec[3]
    result, normed2, scale2 = norm_rows(residual2, vec[4], vec[5])

    cot = lax.ppermute(cotangent, ("dp", "u"), swap_cores)
    cot_parts = [cut(cot, quarter ^ j, own_rows, 1) for j in range(4)]
    cot_far = flip(jnp.stack([cot_parts[2], cot_parts[3]]), "t")
    cot_mine = jnp.stack([cot_parts[0], cot_far[0]])
    cot_near = flip(jnp.stack([cot_parts[1], cot_far[1]]), "dp")
    grad_out = four_in_order(chip, core, [cot_mine[0], cot_mine[1], cot_near[0], cot_near[1]], 0)
    grad_out = grad_out.T.astype(F32)
    grad_r2, gain2_part, shift2_part = norm_rows_back(grad_out, normed2, scale2, vec[4])
    down_bias_part = jnp.sum(grad_r2, axis=0)

    near_g, far_g = gather_pair(grad_r2.astype(BF))
    grad_pre_near = (against(near_g, down_full) * slope_near).astype(BF)
    grad_pre_far = (against(far_g, down_full) * slope_far).astype(BF)
    far_back = matmul(grad_pre_far, up_full)
    near_back = matmul(grad_pre_near, up_full)
    grad_a = grad_r2 + sum_pair(near_back, far_back, own_rows)
    grad_r1, gain1_part, shift1_part = norm_rows_back(grad_a, normed1, scale1, vec[1])
    out_bias_part = jnp.sum(grad_r1, axis=0)

    hidden_all = jnp.concatenate([hidden_near, hidden_far])
    g_all = jnp.concatenate([near_g, far_g])
    a_all = jnp.concatenate([near_a, far_a])
    grad_pre_all = jnp.concatenate([grad_pre_near, grad_pre_far])
    down_grad = inner_rows(hidden_all, g_all).reshape(rows, ff_rows, -1)
    up_grad = inner_rows(grad_pre_all, a_all).reshape(rows, ff_rows, -1)
    up_bias = jnp.sum(grad_pre_all, axis=0, dtype=F32).reshape(rows, 1, ff_rows)
    up_bias = jnp.tile(up_bias, (1, 1, up_grad.shape[2] // ff_rows))
    up_grad = jnp.concatenate([up_grad, jnp.pad(up_bias, ((0, 0), (0, 7), (0, 0)))], 1)
    down_total = reduce_weights(down_grad, u_index)
    up_total = reduce_weights(up_grad, u_index)

    def in_tokens(values):
        parts = [values[:, j * own_rows : (j + 1) * own_rows] for j in range(4)]
        return four_in_order(core, chip, parts, 1)

    near_d, far_d = gather_pair(grad_r1.astype(BF))
    d_all = jnp.concatenate([near_d, far_d])
    grad_att = in_tokens(against(out_full, d_all).astype(BF)).reshape(rows, HEAD_DIM, SEQ)
    out_grad = matmul(attended, d_all).reshape(rows, out_rows, -1)
    grad_proj = attend_back(qkv, grad_att, log_norm).reshape(rows * qkv_rows, SEQ)

    block = feats
    own_block, near_block = 2 * core + chip, 2 * (1 - core) + chip
    far_block, both_block = 2 * core + 1 - chip, 2 * (1 - core) + 1 - chip

    def back_to(index):
        return inner_rows(cut(qkv_full, index, block, 1), grad_proj)

    far_in = back_to(far_block) + flip(back_to(both_block).astype(BF), "dp").astype(F32)
    far_in = flip(far_in.astype(BF), "t")
    near_in = back_to(own_block) + flip(back_to(near_block).astype(BF), "dp").astype(F32)
    passed = in_tokens(cut(d_all, own_block, block, 1).T)
    grad_in = near_in + far_in.astype(F32) + passed.astype(F32)
    grad_tokens = lax.ppermute(grad_in.astype(BF), ("dp", "u"), swap_cores).astype(F32)

    qkv_grad = against(grad_proj, x_t).reshape(rows, qkv_rows, -1)
    proj_sums = jnp.sum(grad_proj.reshape(rows, 3, head_rows, SEQ), axis=3, dtype=F32)
    qv_bias = jnp.concatenate([proj_sums[:, 0], proj_sums[:, 2]], 1)[:, None]
    qv_bias = jnp.tile(qv_bias, (1, 1, qkv_grad.shape[2] // qv_bias.shape[2]))
    norm_part = jnp.stack(
        [out_bias_part, gain1_part, shift1_part, down_bias_part, gain2_part, shift2_part]
    )
    norm_part = jnp.broadcast_to(norm_part, (rows, *norm_part.shape))
    extra = jnp.pad(jnp.concatenate([norm_part, qv_bias], 1), ((0, 0), (0, 1), (0, 0)))
    qkv_total = reduce_weights(jnp.concatenate([qkv_grad, extra], 1), u_index)
    out_total = reduce_weights(out_grad, u_index)

    ff_parts = spread_weights(jnp.concatenate([down_total, up_total]), chip, core)
    attn_parts = spread_weights(jnp.concatenate([out_total, qkv_total]), chip, core)

    def quarters(parts, start, stop):
        picked = [part[start:stop] for part in parts]
        return four_in_order(core, chip, [p[None] for p in picked], 0)

    down_out = quarters(ff_parts, 0, ff_rows).reshape(4 * ff_rows, -1)
    up_out = quarters(ff_parts, ff_rows, 2 * ff_rows).reshape(4 * ff_rows, -1).T
    up_bias_out = quarters(ff_parts, 2 * ff_rows, 2 * ff_rows + 1)[:, 0, :ff_rows].reshape(-1)
    out_out = quarters(attn_parts, 0, out_rows).reshape(4 * out_rows, -1)
    qkv_out = quarters(attn_parts, out_rows, out_rows + qkv_rows)
    qkv_out = qkv_out.reshape(4, 3, head_rows, -1).transpose(3, 1, 0, 2).reshape(feats, 3, -1)
    first_extra = out_rows + qkv_rows
    norm_out = sum(part[first_extra : first_extra + 6] for part in attn_parts)
    qv_out = quarters(attn_parts, first_extra + 6, first_extra + 7)[:, 0, : 2 * head_rows]
    qv_out = qv_out.reshape(4, 2, head_rows).transpose(1, 0, 2).reshape(2, -1)

    result_t = result.astype(BF).T.reshape(2, 2, feats, own_rows)
    result_here = lax.dynamic_index_in_dim(result_t, chip, 1, False)
    result_far = flip(lax.dynamic_index_in_dim(result_t, 1 - chip, 1, False), "t")
    result_pair = jnp.stack([result_here, result_far])
    result_own = lax.dynamic_index_in_dim(result_pair, core, 1, False)
    result_near = flip(lax.dynamic_index_in_dim(result_pair, 1 - core, 1, False), "dp")
    result_parts = [result_own[0], result_near[0], result_own[1], result_near[1]]
    result_seq = four_in_order(core, chip, result_parts, 1)
    result_out = lax.ppermute(result_seq, ("dp", "u"), swap_cores)
    return (
        result_out,
        grad_tokens,
        qkv_out,
        qv_out,
        out_out,
        norm_out[0],
        norm_out[1],
        norm_out[2],
        up_out,
        up_bias_out,
        down_out,
        norm_out[3],
        norm_out[4],
        norm_out[5],
    )


def solution(mesh):
    sizes = dict(mesh.shape)
    grouped = sizes["dp"] == 2 and sizes["col"] == 4 and D % (4 * sizes["row"] * HEAD_DIM) == 0
    if grouped:
        devices = mesh.devices.reshape(sizes["dp"], sizes["row"], 2, 2)
        inner_mesh, col, body = Mesh(devices, ("dp", "row", "u", "t")), ("u", "t"), fast_shards
    else:
        inner_mesh, col, body = mesh, "col", shards
    tokens_spec = P(col, ("dp", "row"))
    return jax.shard_map(
        body,
        mesh=inner_mesh,
        in_specs=(
            tokens_spec,
            P(col, None, "row"),
            P(None, "row"),
            P("row", col),
            P(col),
            P(col),
            P(col),
            P(col, "row"),
            P("row"),
            P("row", col),
            P(col),
            P(col),
            P(col),
            tokens_spec,
        ),
        out_specs=(
            tokens_spec,
            tokens_spec,
            P(col, None, "row"),
            P(None, "row"),
            P("row", col),
            P(col),
            P(col),
            P(col),
            P(col, "row"),
            P("row"),
            P("row", col),
            P(col),
            P(col),
            P(col),
        ),
        check_vma=False,
    )
```

```python
import jax
import jax.numpy as jnp
from jax import lax
from jax.experimental import pallas as pl
from jax.experimental.pallas import tpu as pltpu
from jax.sharding import Mesh
from jax.sharding import PartitionSpec as P

D = 1024
HEAD_DIM = 64
SEQ = 1024


norm_eps = 1e-05


def matmul(first_mat, second_mat):
    return jnp.dot(first_mat, second_mat, preferred_element_type=jnp.float32)


def against(first_mat, second_mat):
    return lax.dot_general(
        first_mat, second_mat, (((1,), (1,)), ((), ())), preferred_element_type=jnp.float32
    )


def inner_rows(first_mat, second_mat):
    return lax.dot_general(
        first_mat, second_mat, (((0,), (0,)), ((), ())), preferred_element_type=jnp.float32
    )


def by_row(values):
    return lax.all_gather(values, "row", axis=0, tiled=True)


def by_col(values):
    return lax.all_gather(values, "col", axis=0, tiled=True)


def reduce_col(source, weight, transposed):
    row_count = source.shape[0] // lax.axis_size("col")

    def partial_value(row_start, row_num):
        return against(source, weight) if transposed else matmul(source, weight)

    return lax.psum_scatter(
        partial_value(jnp.int32(0), row_count * lax.axis_size("col")),
        "col",
        scatter_dimension=0,
        tiled=True,
    )


def reduce_row(source, weight, transposed):
    row_count = source.shape[0] // lax.axis_size("row")

    def partial_value(row_start, row_num):
        return against(source, weight) if transposed else matmul(source, weight)

    return lax.psum_scatter(
        partial_value(jnp.int32(0), row_count * lax.axis_size("row")),
        "row",
        scatter_dimension=0,
        tiled=True,
    )


def feature_totals(first_terms, second_terms):
    return lax.psum((jnp.sum(first_terms, axis=1), jnp.sum(second_terms, axis=1)), "col")


def norm_forward(residual, gain_vec, shift_vec):
    totals = feature_totals(residual, residual * residual)
    mean_rows = totals[0][:, None] / D
    spread = totals[1][:, None] / D - mean_rows * mean_rows
    scale_rows = lax.rsqrt(spread + norm_eps)
    normed = (residual - mean_rows) * scale_rows
    return (normed * gain_vec + shift_vec, normed, scale_rows)


def norm_backward(grad_in, normed, scale_rows, gain_vec):
    scaled = grad_in * gain_vec
    totals = feature_totals(scaled, scaled * normed)
    grad_resid = scale_rows * (scaled - totals[0][:, None] / D - normed * (totals[1][:, None] / D))
    return (grad_resid, jnp.sum(grad_in * normed, axis=0), jnp.sum(grad_in, axis=0))


def gelu_exact(values):
    return jax.nn.gelu(values, approximate=False)


def by_heads(values, head_count):
    seq_count = values.shape[0] // SEQ
    return values.reshape(seq_count, SEQ, head_count, HEAD_DIM)


def attention_forward(queries, key_seq, value_seq):
    block_len = min(512, SEQ)
    outputs = []
    log_parts = []
    for offset in range(0, SEQ, block_len):
        query_block = queries[:, offset : offset + block_len]
        scores = jnp.einsum(
            "nqhd,nkhd->nhqk", query_block, key_seq, preferred_element_type=jnp.float32
        )
        row_max = jnp.max(scores, axis=-1, keepdims=True)
        exp_scores = jnp.exp(scores - row_max)
        denom = jnp.sum(exp_scores, axis=-1, keepdims=True)
        probs_low = (exp_scores / denom).astype(jnp.bfloat16)
        outputs.append(
            jnp.einsum("nhqk,nkhd->nqhd", probs_low, value_seq, preferred_element_type=jnp.float32)
        )
        log_parts.append(row_max + jnp.log(denom))
    attended = jnp.concatenate(outputs, axis=1)
    rows_here = attended.shape[0] * SEQ
    return (
        attended.reshape(rows_here, -1).astype(jnp.bfloat16),
        jnp.concatenate(log_parts, axis=2),
    )


def attention_backward(queries, key_seq, value_seq, grad_seq, log_norm):
    block_len = min(512, SEQ)
    grad_query_parts = []
    grad_key = jnp.zeros(key_seq.shape, jnp.float32)
    grad_value = jnp.zeros(value_seq.shape, jnp.float32)
    for offset in range(0, SEQ, block_len):
        query_block = queries[:, offset : offset + block_len]
        grad_block = grad_seq[:, offset : offset + block_len]
        scores = jnp.einsum(
            "nqhd,nkhd->nhqk", query_block, key_seq, preferred_element_type=jnp.float32
        )
        probs = jnp.exp(scores - log_norm[:, :, offset : offset + block_len])
        grad_probs = jnp.einsum(
            "nqhd,nkhd->nhqk", grad_block, value_seq, preferred_element_type=jnp.float32
        )
        row_delta = jnp.sum(grad_probs * probs, axis=-1, keepdims=True)
        grad_scores = (probs * (grad_probs - row_delta)).astype(jnp.bfloat16)
        grad_query_parts.append(
            jnp.einsum("nhqk,nkhd->nqhd", grad_scores, key_seq, preferred_element_type=jnp.float32)
        )
        grad_key = grad_key + jnp.einsum(
            "nhqk,nqhd->nkhd", grad_scores, query_block, preferred_element_type=jnp.float32
        )
        grad_value = grad_value + jnp.einsum(
            "nhqk,nqhd->nkhd",
            probs.astype(jnp.bfloat16),
            grad_block,
            preferred_element_type=jnp.float32,
        )
    grad_query = jnp.concatenate(grad_query_parts, axis=1)
    rows_here = grad_query.shape[0] * SEQ
    return (
        grad_query.reshape(rows_here, -1).astype(jnp.bfloat16),
        grad_key.reshape(rows_here, -1).astype(jnp.bfloat16),
        grad_value.reshape(rows_here, -1).astype(jnp.bfloat16),
    )


def shards(
    tokens,
    w_qkv,
    b_qv,
    w_out,
    b_out,
    norm1_gain,
    norm1_shift,
    w_up,
    b_up,
    w_down,
    b_down,
    norm2_gain,
    norm2_shift,
    cotangent,
):
    token_major = tokens.T
    width_col = token_major.shape[1]
    width_row = w_out.shape[0]
    qkv_weight = w_qkv.reshape(width_col, 3 * width_row)
    query_scale = HEAD_DIM ** (-0.5)
    head_count = width_row // HEAD_DIM
    gathered_in = by_row(token_major)
    projected = reduce_col(gathered_in, qkv_weight, False).reshape(-1, 3, width_row)
    queries = ((projected[:, 0] + b_qv[0]) * query_scale).astype(jnp.bfloat16)
    key_rows = projected[:, 1].astype(jnp.bfloat16)
    value_rows = (projected[:, 2] + b_qv[1]).astype(jnp.bfloat16)
    query_seq = by_heads(queries, head_count)
    key_seq = by_heads(key_rows, head_count)
    value_seq = by_heads(value_rows, head_count)
    attended, log_norm = attention_forward(query_seq, key_seq, value_seq)
    gathered_att = by_col(attended)
    attn_out = reduce_row(gathered_att, w_out, False) + b_out
    residual1 = token_major.astype(jnp.float32) + attn_out
    normed_a, normed1, scale1 = norm_forward(residual1, norm1_gain, norm1_shift)
    low_a = normed_a.astype(jnp.bfloat16)
    gathered_a = by_row(low_a)
    pre_act = reduce_col(gathered_a, w_up, False) + b_up
    hidden, gelu_pull = jax.vjp(gelu_exact, pre_act)
    hidden_low = hidden.astype(jnp.bfloat16)
    gathered_h = by_col(hidden_low)
    branch_out = reduce_row(gathered_h, w_down, False)
    residual2 = normed_a + branch_out + b_down
    result, normed2, scale2 = norm_forward(residual2, norm2_gain, norm2_shift)
    grad_out = cotangent.T.astype(jnp.float32)
    grad_r2, gain2_part, shift2_part = norm_backward(grad_out, normed2, scale2, norm2_gain)
    down_bias_part = jnp.sum(grad_r2, axis=0)
    grad_branch = grad_r2.astype(jnp.bfloat16)
    gathered_df = by_row(grad_branch)
    down_grad = inner_rows(gathered_h, gathered_df)
    grad_hidden = reduce_col(gathered_df, w_down, True)
    grad_pre = gelu_pull(grad_hidden)[0].astype(jnp.bfloat16)
    gathered_dz = by_col(grad_pre)
    up_grad = inner_rows(gathered_a, gathered_dz)
    up_bias_grad = jnp.sum(gathered_dz, axis=0, dtype=jnp.float32)
    grad_a_ff = reduce_row(gathered_dz, w_up, True)
    grad_a = grad_r2 + grad_a_ff
    grad_r1, gain1_part, shift1_part = norm_backward(grad_a, normed1, scale1, norm1_gain)
    out_bias_part = jnp.sum(grad_r1, axis=0)
    gathered_datt = by_row(grad_r1.astype(jnp.bfloat16))
    out_grad = inner_rows(gathered_att, gathered_datt)
    grad_attended = reduce_col(gathered_datt, w_out, True).astype(jnp.bfloat16)
    grad_seq = by_heads(grad_attended, head_count)
    grad_query, grad_key, grad_value = attention_backward(
        query_seq, key_seq, value_seq, grad_seq, log_norm
    )
    grad_proj = jnp.stack([grad_query * query_scale, grad_key, grad_value], axis=1).reshape(
        -1, 3 * width_row
    )
    gathered_dqkv = by_col(grad_proj)
    qkv_grad = inner_rows(gathered_in, gathered_dqkv).reshape(width_col, 3, width_row)
    bias_rows = jnp.sum(gathered_dqkv, axis=0, dtype=jnp.float32).reshape(3, width_row)
    qv_bias_grad = jnp.stack([bias_rows[0], bias_rows[2]])
    grad_input = reduce_row(gathered_dqkv, qkv_weight, True) + grad_r1
    norm_sums = lax.psum(
        (gain1_part, shift1_part, gain2_part, shift2_part, out_bias_part, down_bias_part),
        ("dp", "row"),
    )
    weight_sums = lax.psum(
        (qkv_grad, qv_bias_grad, out_grad, up_grad, up_bias_grad, down_grad), "dp"
    )
    return (
        result.astype(jnp.bfloat16).T,
        grad_input.T,
        weight_sums[0],
        weight_sums[1],
        weight_sums[2],
        norm_sums[4],
        norm_sums[0],
        norm_sums[1],
        weight_sums[3],
        weight_sums[4],
        weight_sums[5],
        norm_sums[5],
        norm_sums[2],
        norm_sums[3],
    )


BF = jnp.bfloat16
F32 = jnp.float32
PAIR = ((0, 1), (1, 0))
MEBIBYTE = 1024 * 1024
BLOCK = 256


def flip(values, axis_name):
    return lax.ppermute(values, axis_name, PAIR)


def shift(values, axis_name, step):
    size = lax.axis_size(axis_name)
    return lax.ppermute(values, axis_name, [(i, (i + step) % size) for i in range(size)])


def in_order(index, mine, other, axis):
    first = jnp.where(index == 0, mine, other)
    second = jnp.where(index == 0, other, mine)
    return jnp.concatenate([first, second], axis)


def four_in_order(low_bit, high_bit, parts, axis):
    low = [jnp.where(low_bit == 0, parts[i], parts[i ^ 1]) for i in range(4)]
    full = [jnp.where(high_bit == 0, low[i], low[i ^ 2]) for i in range(4)]
    return jnp.concatenate(full, axis)


def cut(values, index, size, axis):
    return lax.dynamic_slice_in_dim(values, index * size, size, axis)


def after(values, *earlier):
    return lax.optimization_barrier((values, earlier))[0]


def part(index, size):
    return pl.ds(pl.multiple_of(index * size, size), size)


def kernel_call(kernel, name, outs, places, *inputs, grid=1, specs=None, out_specs=None, scratch=(), vmem=16):
    return pl.pallas_call(
        kernel,
        grid_spec=pltpu.PrefetchScalarGridSpec(
            num_scalar_prefetch=1,
            grid=(grid,),
            in_specs=[fixed(x.shape) for x in inputs] if specs is None else specs,
            out_specs=[fixed(shape) for shape, _ in outs] if out_specs is None else out_specs,
            scratch_shapes=list(scratch),
        ),
        out_shape=[jax.ShapeDtypeStruct(shape, dtype) for shape, dtype in outs],
        compiler_params=pltpu.CompilerParams(vmem_limit_bytes=vmem * MEBIBYTE),
        cost_estimate=pl.CostEstimate(flops=1, bytes_accessed=1, transcendentals=0),
        name=name,
    )(places, *inputs)


def fixed(shape):
    return pl.BlockSpec(shape, lambda step, places: (0,) * len(shape))


def stepped(shape, axis):
    return pl.BlockSpec(
        shape, lambda step, places: tuple(step if i == axis else 0 for i in range(len(shape)))
    )


def prepare_attn_kernel(places, w_qkv, b_qv, w_out, *refs):
    vectors, (keep, send, turned) = refs[:-3], refs[-3:]
    head = turned.shape[1] // 4
    for piece in range(3):
        turned[piece] = w_qkv[piece].T
    for ref, quarter in ((keep, places[0]), (send, places[1])):
        for piece in range(3):
            ref[piece * head : (piece + 1) * head] = turned[piece, part(quarter, head), :]
        bias = b_qv[...].astype(F32)
        own = sum(
            jnp.where(quarter == q, bias[:, q * head : (q + 1) * head], 0.0) for q in range(4)
        )
        line = jnp.concatenate([own[0:1], own[1:2]], 1)
        line = jnp.concatenate([line, jnp.zeros((1, keep.shape[1] - 2 * head), F32)], 1)
        rows = [jnp.broadcast_to(line, (8, keep.shape[1]))]
        rows += [vector[...].astype(F32).reshape(1, -1) for vector in vectors]
        rows += [jnp.zeros((2, keep.shape[1]), F32)]
        ref[3 * head : 3 * head + 16] = jnp.concatenate(rows, 0).astype(BF)
        ref[3 * head + 16 :] = w_out[part(quarter, head), :]


def prepare_ff_kernel(places, w_up, w_down, keep, send):
    for ref, quarter in ((keep, places[0]), (send, places[1])):
        ref[:BLOCK] = w_up[:, part(quarter, BLOCK)].T
        ref[BLOCK:] = w_down[part(quarter, BLOCK), :]


def attend_kernel(places, x00, x01, x10, x11, own, far, qkv_ref, out_ref, norm_ref, *weight_refs):
    head_rows = qkv_ref.shape[2]
    total = None
    for side, pair in ((0, (x00, x01)), (1, (x10, x11))):
        mine = (places[3] ^ side) == places[2]
        for end, x in enumerate(pair):
            weight = jnp.where(mine, own[0, end, : 3 * head_rows], far[0, end, : 3 * head_rows])
            weight_refs[2 * side + end][0] = weight
            piece = matmul(weight, x[...])
            total = piece if total is None else total + piece
    bias = own[0, 0, 3 * head_rows : 3 * head_rows + 8].astype(F32)[0:1, : 2 * head_rows]
    bias = jnp.broadcast_to(bias, (2 * head_rows, 2 * head_rows)).T
    query = (total[:head_rows] + bias[:head_rows, 0:1]) * HEAD_DIM**-0.5
    qkv_ref[0, 0] = query.astype(BF)
    key = total[head_rows : 2 * head_rows].astype(BF)
    qkv_ref[0, 1] = key
    value = (total[2 * head_rows :] + bias[head_rows:, 0:1]).astype(BF)
    qkv_ref[0, 2] = value
    key_t = key.T
    for start in range(0, SEQ, BLOCK):
        here = slice(start, start + BLOCK)
        scores = matmul(key_t, qkv_ref[0, 0, :, here])
        top = jnp.max(scores, axis=0, keepdims=True)
        weights = jnp.exp(scores - top)
        denom = jnp.sum(weights, axis=0, keepdims=True)
        out_ref[0, :, here] = matmul(value, weights.astype(BF)) * (1.0 / denom)
        norm_ref[0, :, here] = top + jnp.log(denom)


def turn_kernel(places, *refs):
    for ref, out_ref in zip(refs[:4], refs[4:]):
        out_ref[...] = ref[...].T


def out_far_kernel(places, attended, mixed, other, own_ref, send_ref, full_ref, low_ref):
    heads, head_rows, _ = attended.shape
    half = other.shape[2]
    low_ref[...] = attended[...].astype(BF)
    for head in range(heads):
        source = lax.rem(places[5] - head + heads, heads)
        rows = slice(head * head_rows, (head + 1) * head_rows)
        full_ref[rows, part(places[2], half)] = mixed[source, 8 : 8 + head_rows, :]
        full_ref[rows, part(1 - places[2], half)] = other[source, 8:, :]
    out_block(places, 3, low_ref, full_ref, send_ref)
    out_block(places, 2, low_ref, full_ref, own_ref)


def out_near_kernel(places, attended, full_ref, own_ref, send_ref):
    out_block(places, 1, attended, full_ref, send_ref)
    out_block(places, 0, attended, full_ref, own_ref)


def out_block(places, step, attended, full_ref, out_ref):
    rows = attended[:, :, part(places[0] ^ step, BLOCK)].reshape(-1, BLOCK)
    out_ref[...] = inner_rows(rows, full_ref[...]).astype(out_ref.dtype)


def norm1_kernel(places, near, core, got, x00, x01, x10, x11, vec, a_ref, low_ref, normed_ref, scale_ref):
    for side, pair in ((0, (x00, x01)), (1, (x10, x11))):
        for end, x in enumerate(pair):
            block = 2 * (places[3] ^ side) + (places[4] ^ end)
            a_ref[:, part(block, BLOCK)] = x[...].T.astype(F32)
    residual = a_ref[...] + (near[...] + core[...].astype(F32) + got[...].astype(F32) + vec[0:1])
    mean_rows = jnp.mean(residual, axis=1, keepdims=True)
    spread = jnp.mean(residual * residual, axis=1, keepdims=True) - mean_rows * mean_rows
    scale_rows = lax.rsqrt(spread + norm_eps)
    normed = (residual - mean_rows) * scale_rows
    values = normed * vec[1:2] + vec[2:3]
    a_ref[...] = values
    low_ref[...] = values.astype(BF)
    normed_ref[...] = normed
    scale_ref[...] = scale_rows


def back_of_norm(grad_in, normed, scale_rows, gain_vec):
    scaled = grad_in * gain_vec
    first = jnp.mean(scaled, axis=1, keepdims=True)
    second = jnp.mean(scaled * normed, axis=1, keepdims=True)
    return scale_rows * (scaled - first - normed * second)


def add_sums(sums_ref, *arrays):
    @pl.when(pl.program_id(0) == 0)
    def _():
        sums_ref[...] = jnp.zeros_like(sums_ref)

    for index, values in enumerate(arrays):
        sums_ref[index : index + 1] += jnp.sum(values, axis=0, keepdims=True)


def norm2_kernel(places, near, core, got, a_ref, c0, c1, c2, c3, vec, here_ref, send_ref, grad_ref, low_ref, sums_ref):
    for index, piece in enumerate((c0, c1, c2, c3)):
        block = 2 * (places[3] ^ (index >> 1)) + (places[4] ^ (index & 1))
        grad_ref[:, part(block, BLOCK)] = piece[...].T.astype(F32)
    branch = near[...] + core[...].astype(F32) + got[...].astype(F32) + vec[3:4]
    residual = a_ref[...] + branch
    mean_rows = jnp.mean(residual, axis=1, keepdims=True)
    spread = jnp.mean(residual * residual, axis=1, keepdims=True) - mean_rows * mean_rows
    scale_rows = lax.rsqrt(spread + norm_eps)
    normed = (residual - mean_rows) * scale_rows
    grad_out = grad_ref[...]
    grad = back_of_norm(grad_out, normed, scale_rows, vec[4:5])
    add_sums(sums_ref, grad, grad_out * normed, grad_out)
    grad_ref[...] = normed * vec[4:5] + vec[5:6]
    for side in range(2):
        for end, ref in ((0, here_ref), (1, send_ref)):
            block = 2 * (places[3] ^ side) + (places[4] ^ end)
            ref[side] = grad_ref[:, part(block, BLOCK)].T.astype(BF)
    grad_ref[...] = grad
    low_ref[...] = grad.astype(BF)


def norm1_back_kernel(places, near, core, got, grad2, normed_ref, scale_ref, vec, sums2, low_ref, sums_ref):
    grad_in = grad2[...] + (near[...] + core[...].astype(F32) + got[...].astype(F32))
    normed = normed_ref[...]
    grad = back_of_norm(grad_in, normed, scale_ref[...], vec[1:2])
    add_sums(sums_ref, grad, grad_in * normed, grad_in)
    sums_ref[3:6] = sums2[0:3]
    low_ref[...] = grad.astype(BF)


def weight_grad_kernel(places, left_near, left_far, r0, r1, r2, r3, mine_ref, sent_ref, right):
    half = mine_ref.shape[2]

    @pl.when(pl.program_id(0) == 0)
    def _():
        for index, rows in enumerate((r0, r1, r2, r3)):
            here = slice(index * BLOCK, (index + 1) * BLOCK)
            right[0, here] = rows[:, part(places[2], half)]
            right[1, here] = rows[:, part(1 - places[2], half)]

    left = jnp.concatenate([left_near[...], left_far[...]], 0)
    sent_ref[0, :BLOCK] = inner_rows(left, right[1]).astype(BF)
    mine_ref[0, :BLOCK] = inner_rows(left, right[0]).astype(BF)
    if mine_ref.shape[1] > BLOCK:
        sums = jnp.sum(left.astype(F32), axis=0, keepdims=True)
        sums = jnp.broadcast_to(jnp.concatenate([sums, sums], 1), (8, half)).astype(BF)
        sent_ref[0, BLOCK:] = sums
        mine_ref[0, BLOCK:] = sums


def out_back_kernel(places, d0, d1, d2, d3, full_ref, attended, grad_ref, mine_ref, sent_ref):
    heads, head_rows, _ = attended.shape
    blocks = (d0, d1, d2, d3)
    left = []
    for step, rows in enumerate(blocks):
        here = part(places[0] ^ step, BLOCK)
        grad = against(full_ref[...], rows[...]).astype(BF)
        grad_ref[:, :, here] = grad.reshape(heads, head_rows, BLOCK)
        left.append(attended[:, :, here].reshape(-1, BLOCK))
    width = mine_ref.shape[3]
    for ref, side in ((sent_ref, 1 - places[2]), (mine_ref, places[2])):
        for end in range(2):
            columns = part(2 * side + (places[4] ^ end), width)
            total = None
            for piece, rows in zip(left, blocks):
                product = matmul(piece, rows[:, columns])
                total = product if total is None else total + product
            ref[:, end] = total.astype(BF).reshape(heads, head_rows, width)


def attend_back_kernel(
    places, qkv_ref, grad_ref, norm_ref, attended, x00, x01, x10, x11, sums, out_ref, mine_ref, sent_ref, probs_low, scores_low
):
    head_rows = qkv_ref.shape[2]
    key = qkv_ref[0, 1]
    key_t = key.T
    value_t = qkv_ref[0, 2].T
    for start in range(0, SEQ, BLOCK):
        here = slice(start, start + BLOCK)
        grad = grad_ref[0, :, here]
        probs = jnp.exp(matmul(key_t, qkv_ref[0, 0, :, here]) - norm_ref[0, :, here])
        delta = jnp.sum(grad.astype(F32) * attended[0, :, here], axis=0, keepdims=True)
        grad_scores = (probs * (matmul(value_t, grad) - delta)).astype(BF)
        probs_low[:, here] = probs.astype(BF)
        scores_low[:, here] = grad_scores
        grad_query = matmul(key, grad_scores).astype(BF)
        out_ref[0, :head_rows, here] = (grad_query.astype(F32) * HEAD_DIM**-0.5).astype(BF)
    grad_key = matmul(scores_low[...], qkv_ref[0, 0].T)
    out_ref[0, head_rows : 2 * head_rows] = grad_key.T.astype(BF)
    grad_value = matmul(probs_low[...], grad_ref[0].T)
    out_ref[0, 2 * head_rows :] = grad_value.T.astype(BF)
    left = out_ref[0]
    bias = jnp.sum(left.astype(F32), axis=1, keepdims=True)
    bias = jnp.concatenate([bias[:head_rows], bias[2 * head_rows :]], 0)
    bias = jnp.broadcast_to(bias, (2 * head_rows, 2 * head_rows)).T[:8]
    bias = jnp.concatenate([bias, jnp.zeros((8, BLOCK - 2 * head_rows), F32)], 1)
    rows = 3 * head_rows
    for side, pair in ((0, (x00, x01)), (1, (x10, x11))):
        mine = (places[3] ^ side) == places[2]
        for end, x in enumerate(pair):
            weight = matmul(left, x[...]).astype(BF)
            block = sums[:, part(2 * (places[3] ^ side) + (places[4] ^ end), BLOCK)]
            extra = jnp.concatenate([block, bias], 0).astype(BF)

            @pl.when(mine)
            def _():
                mine_ref[0, end, :rows] = weight
                mine_ref[0, end, rows:] = extra

            @pl.when(jnp.logical_not(mine))
            def _():
                sent_ref[0, end, :rows] = weight
                sent_ref[0, end, rows:] = extra


def both_halves(mine, got, out_mine, out_got, head, place):
    sums = mine[head].astype(F32) + got[head].astype(F32)
    outs = out_mine[place].astype(F32) + out_got[place].astype(F32)
    return jnp.concatenate([sums, outs], 1)


def late_sum_kernel(places, mine, got, out_mine, out_got, *sums):
    for head, ref in enumerate(sums):
        place = head + out_mine.shape[0] - len(sums)
        ref[...] = both_halves(mine, got, out_mine, out_got, head, place).astype(BF)


def early_sum_kernel(places, mine, got, out_mine, out_got, own_ref, *sums):
    own_ref[...] = both_halves(mine, got, out_mine, out_got, 0, 0)
    for head, ref in enumerate(sums):
        ref[...] = both_halves(mine, got, out_mine, out_got, head + 1, head + 1).astype(BF)


def last_sum_kernel(places, own_ref, *refs):
    total = own_ref[...]
    for ref in refs[:-2]:
        total = total + ref[...].astype(F32)
    refs[-2][...] = total[0].astype(BF)
    refs[-1][...] = total[1].astype(BF)


def input_near_kernel(places, weight_own, weight_send, grads, d0, d1, d2, d3, own_ref, send_ref):
    heads, rows, _ = grads.shape
    right = grads[...].reshape(heads * rows, SEQ)
    send_ref[...] = inner_rows(weight_send[...].reshape(heads * rows, -1), right).astype(BF)
    own_ref[...] = inner_rows(weight_own[...].reshape(heads * rows, -1), right)
    block = 2 * places[3] + places[4]
    for step, d in enumerate((d0, d1, d2, d3)):
        here = part(places[0] ^ step, BLOCK)
        own_ref[:, here] += d[:, part(block, BLOCK)].T.astype(F32)


def last_attn_kernel(places, p0, p1, p2, p3, qkv_out, qv_out, norm_out, out_out, turned):
    parts = (p0, p1, p2, p3)
    head = turned.shape[0] // 4
    for piece in range(3):
        for step, ref in enumerate(parts):
            turned[part(places[0] ^ step, head), :] = ref[piece * head : (piece + 1) * head].astype(F32)
        qkv_out[piece] = turned[...].T
    extra = [ref[3 * head : 3 * head + 16].astype(F32) for ref in parts]
    norm_out[...] = extra[0][:8] + extra[1][:8] + extra[2][:8] + extra[3][:8]
    lines = [[], []]
    for quarter in range(4):
        line = sum(
            jnp.where((places[0] ^ step) == quarter, extra[step][8:9], 0.0) for step in range(4)
        )
        lines[0].append(line[:, :head])
        lines[1].append(line[:, head : 2 * head])
    qv_out[...] = jnp.concatenate([jnp.concatenate(line, 1) for line in lines], 0)
    for step, ref in enumerate(parts):
        out_out[part(places[0] ^ step, head), :] = ref[3 * head + 16 :].astype(F32)


def last_up_kernel(places, p0, p1, p2, p3, up_out, bias_out):
    for step, ref in enumerate((p0, p1, p2, p3)):
        quarter = places[0] ^ step
        up_out[:, part(quarter, BLOCK)] = ref[:BLOCK].astype(F32).T
        bias_out[:, part(quarter, BLOCK)] = ref[BLOCK:].astype(F32)[0:1]


def last_down_kernel(places, p0, p1, p2, p3, down_out):
    for step, ref in enumerate((p0, p1, p2, p3)):
        down_out[part(places[0] ^ step, BLOCK), :] = ref[...].astype(F32)


def to_far_chip(own, send):
    return (own + flip(send, "dp").astype(F32)).astype(BF)


def gather_rows(payload):
    size = lax.axis_size("row")
    return jnp.stack([payload] + [shift(payload, "row", step) for step in range(1, size)])


def gather_blocks(payload):
    return lax.all_gather(payload, "row", axis=0)


def reduce_blocks(both):
    return lax.psum_scatter(both.astype(BF), "row", scatter_dimension=0)


def spread_weights(mine, other):
    near = jnp.stack([mine, flip(other, "t")])
    far = flip(near, "dp")
    return near[0], far[0], near[1], far[1]


def fast_shards(
    tokens,
    w_qkv,
    b_qv,
    w_out,
    b_out,
    norm1_gain,
    norm1_shift,
    w_up,
    b_up,
    w_down,
    b_down,
    norm2_gain,
    norm2_shift,
    cotangent,
):
    core, chip = lax.axis_index("dp"), lax.axis_index("t")
    u_index, row = lax.axis_index("u"), lax.axis_index("row")
    rows = lax.axis_size("row")
    quarter = 2 * chip + core
    other_quarter = 2 * (1 - chip) + core
    places = jnp.stack([quarter, other_quarter, u_index, core, chip, row]).astype(jnp.int32)
    feats = tokens.shape[0]
    width = 4 * feats
    half = 2 * feats
    own_rows = SEQ // 4
    swap_cores = [(2 * d + u, 2 * u + d) for d in range(2) for u in range(2)]
    head_rows = w_out.shape[0] // 4
    qkv_rows, out_rows, ff_rows = 3 * head_rows, head_rows, w_down.shape[0] // 4

    x00 = lax.ppermute(tokens, ("dp", "u"), swap_cores)

    attn_rows = qkv_rows + 16 + out_rows
    attn_keep, attn_send = kernel_call(
        prepare_attn_kernel,
        "prepare_attn",
        [((attn_rows, feats), BF)] * 2,
        places,
        w_qkv.transpose(1, 0, 2),
        b_qv,
        w_out,
        b_out,
        norm1_gain,
        norm1_shift,
        b_down,
        norm2_gain,
        norm2_shift,
        scratch=[pltpu.VMEM((3, 4 * head_rows, feats), BF)],
        vmem=60,
    )
    attn_got = flip(attn_send, "t")
    ff_keep, ff_send = kernel_call(
        prepare_ff_kernel, "prepare_ff", [((2 * ff_rows, feats), BF)] * 2, places, after(w_up, attn_send), w_down, vmem=60
    )
    ff_got = flip(ff_send, "t")
    attn_got = after(attn_got, x00)
    cot = lax.ppermute(after(cotangent, x00), ("dp", "u"), swap_cores)
    x01 = flip(x00, "t")
    x10, x11 = flip(x00, "dp"), flip(x01, "dp")
    cot = after(cot, x01)
    cot_parts = [cut(cot, quarter ^ j, own_rows, 1) for j in range(4)]
    cot_far = flip(jnp.stack([cot_parts[2], cot_parts[3]]), "t")
    cot_near = flip(jnp.stack([cot_parts[1], cot_far[1]]), "dp")

    qkv_part = jnp.stack([attn_keep[: qkv_rows + 8], attn_got[: qkv_rows + 8]])
    qkv_part, ff_got = lax.optimization_barrier((qkv_part, ff_got))
    qkv_own = gather_rows(qkv_part)
    attn_both = in_order(chip, attn_keep[qkv_rows + 8 :], attn_got[qkv_rows + 8 :], 1)
    ff_both = in_order(chip, ff_keep, ff_got, 1)
    up_bias = lax.dynamic_index_in_dim(b_up.reshape(4, -1), quarter, 0, True)
    up_bias = jnp.pad(up_bias, ((0, 7), (0, half - ff_rows)))
    down_both = in_order(u_index, ff_both[ff_rows:], flip(ff_both[ff_rows:], "u"), 1)
    mixed = gather_blocks(jnp.concatenate([attn_both, ff_both[:ff_rows], up_bias]))
    down_full = gather_blocks(down_both).reshape(rows * ff_rows, width)
    qkv_far = flip(after(qkv_own, x01, down_both), "u")

    x_blocks = (x00, x01, x10, x11)
    qkv, attended, log_norm, *weight = kernel_call(
        attend_kernel,
        "attend",
        [
            ((rows, 3, head_rows, SEQ), BF),
            ((rows, head_rows, SEQ), F32),
            ((rows, 1, SEQ), F32),
        ]
        + [((rows, qkv_rows, feats), BF)] * 4,
        places,
        *x_blocks,
        qkv_own,
        qkv_far,
        grid=rows,
        specs=[fixed((feats, SEQ))] * 4 + [stepped((1, 2, qkv_rows + 8, feats), 0)] * 2,
        out_specs=[
            stepped((1, 3, head_rows, SEQ), 0),
            stepped((1, head_rows, SEQ), 0),
            stepped((1, 1, SEQ), 0),
        ]
        + [stepped((1, qkv_rows, feats), 0)] * 4,
        vmem=28,
    )
    mixed = after(mixed, qkv_far, cot_near)
    vec_rows = 8 + out_rows
    out_other = flip(mixed[:, :vec_rows], "u")
    up_own = mixed[:, vec_rows : vec_rows + ff_rows]
    up_far = flip(after(up_own, out_other), "u")
    bias_up = mixed[:, vec_rows + ff_rows, :ff_rows].reshape(1, -1).astype(F32)
    vec = in_order(u_index, mixed[0, :8], out_other[0, :8], 1).astype(F32)
    up_full = in_order(
        u_index, up_own.reshape(rows * ff_rows, half), up_far.reshape(rows * ff_rows, half), 1
    )

    row_block = (own_rows, width)
    pair_outs = [(row_block, F32), (row_block, BF)]
    far_own, far_send, out_full, low_attended = kernel_call(
        out_far_kernel,
        "out_far",
        pair_outs + [((rows * head_rows, width), BF), (attended.shape, BF)],
        places,
        attended,
        mixed,
        out_other,
        specs=[fixed(attended.shape), fixed((rows, vec_rows, half)), fixed(out_other.shape)],
    )
    sent = to_far_chip(far_own, far_send)
    near_attended = after(low_attended, sent)
    got = flip(sent, "t")
    near_own, near_send = kernel_call(
        out_near_kernel, "out_near", pair_outs, places, near_attended, out_full
    )
    token_rows = kernel_call(
        turn_kernel, "turn", [((SEQ, feats), BF)] * 4, places, *after(x_blocks, near_own)
    )
    near_got = flip(near_send, "dp")
    got = after(got, near_got, token_rows)
    chunk = own_rows // 2
    row_chunk = stepped((chunk, width), 0)
    own_tokens = pl.BlockSpec((feats, chunk), lambda step, places: (0, 2 * places[0] + step))
    normed_a, low_a, normed1, scale1 = kernel_call(
        norm1_kernel,
        "norm1",
        [(row_block, F32), (row_block, BF), (row_block, F32), ((own_rows, 1), F32)],
        places,
        near_own,
        near_got,
        got,
        *x_blocks,
        vec,
        grid=2,
        specs=[row_chunk] * 3 + [own_tokens] * 4 + [fixed((8, width))],
        out_specs=[row_chunk] * 3 + [stepped((chunk, 1), 0)],
    )

    def up(rows_in):
        pre = against(rows_in, up_full) + bias_up
        cdf = 0.5 * (1.0 + lax.erf(pre * (0.5**0.5)))
        slope = cdf + pre * (jnp.exp(-0.5 * pre * pre) * 0.3989422804014327)
        return (pre * cdf).astype(BF), slope

    a0, a1, a2 = low_a, flip(low_a, "dp"), flip(low_a, "t")
    hidden_near, slope_near = up(jnp.concatenate([a0, a1]))
    a2 = after(a2, hidden_near)
    a3 = flip(a2, "dp")
    hidden_far, slope_far = up(jnp.concatenate([a2, a3]))
    far_send = matmul(hidden_far[own_rows:], down_full).astype(BF)
    sent = to_far_chip(matmul(hidden_far[:own_rows], down_full), far_send)
    near_hidden = after(hidden_near, sent)
    got = flip(sent, "t")
    near_got = flip(matmul(near_hidden[own_rows:], down_full).astype(BF), "dp")
    near_own = matmul(near_hidden[:own_rows], down_full)
    got = after(got, near_got)
    turned_chunk = stepped((feats, chunk), 1)
    pair_chunk = stepped((2, feats, chunk), 2)
    result_here, result_send, grad_r2, low_g, sums2 = kernel_call(
        norm2_kernel,
        "norm2",
        [((2, feats, own_rows), BF)] * 2 + [(row_block, F32), (row_block, BF), ((8, width), F32)],
        places,
        near_own,
        near_got,
        got,
        normed_a,
        cot_parts[0],
        cot_far[0],
        cot_near[0],
        cot_near[1],
        vec,
        grid=2,
        specs=[row_chunk] * 4 + [turned_chunk] * 4 + [fixed((8, width))],
        out_specs=[pair_chunk] * 2 + [row_chunk] * 2 + [fixed((8, width))],
    )

    two_blocks = 2 * own_rows

    def weight_grad(near, far, blocks, extra):
        shape = (rows, ff_rows + extra, half)
        return kernel_call(
            weight_grad_kernel,
            "weight_grad",
            [(shape, BF)] * 2,
            places,
            near,
            far,
            *blocks,
            grid=rows,
            specs=[stepped((two_blocks, ff_rows), 1)] * 2 + [fixed(row_block)] * 4,
            out_specs=[stepped((1, *shape[1:]), 0)] * 2,
            scratch=[pltpu.VMEM((2, SEQ, half), BF)],
        )

    g0, g1, g2 = low_g, flip(low_g, "dp"), flip(low_g, "t")
    grad_pre_near = (against(jnp.concatenate([g0, g1]), down_full) * slope_near).astype(BF)
    g2 = after(g2, grad_pre_near)
    g3 = flip(g2, "dp")
    grad_pre_far = (against(jnp.concatenate([g2, g3]), down_full) * slope_far).astype(BF)
    far_send = matmul(grad_pre_far[own_rows:], up_full).astype(BF)
    sent = to_far_chip(matmul(grad_pre_far[:own_rows], up_full), far_send)
    near_pre = after(grad_pre_near, sent)
    got = flip(sent, "t")
    near_got = flip(matmul(near_pre[own_rows:], up_full).astype(BF), "dp")
    near_own = matmul(near_pre[:own_rows], up_full)
    hiddens, pres = after(((hidden_near, hidden_far), (near_pre, grad_pre_far)), near_own)
    down_mine, down_sent = weight_grad(*hiddens, (g0, g1, g2, g3), 0)
    down_got = flip(down_sent, "u")
    up_mine, up_sent = weight_grad(*pres, (a0, a1, a2, a3), 8)
    got = after(got, near_got, up_sent)
    low_r1, sums = kernel_call(
        norm1_back_kernel,
        "norm1_back",
        [(row_block, BF), ((8, width), F32)],
        places,
        near_own,
        near_got,
        got,
        grad_r2,
        normed1,
        scale1,
        vec,
        sums2,
        grid=2,
        specs=[row_chunk] * 5 + [stepped((chunk, 1), 0)] + [fixed((8, width))] * 2,
        out_specs=[row_chunk, fixed((8, width))],
    )

    d0, d1, d2 = low_r1, flip(low_r1, "dp"), flip(low_r1, "t")
    down_got = after(down_got, low_r1)
    up_sent, down_got = lax.optimization_barrier((up_sent, down_got))
    up_got = flip(up_sent, "u")
    d2 = after(d2, down_got)
    down_total = reduce_blocks(down_mine.astype(F32) + down_got.astype(F32))
    d3 = flip(d2, "dp")
    d_blocks = (d0, d1, d2, d3)
    out_shape = (rows, 2, out_rows, feats)
    grad_att, out_mine, out_sent = kernel_call(
        out_back_kernel,
        "out_back",
        [((rows, head_rows, SEQ), BF)] + [(out_shape, BF)] * 2,
        places,
        *d_blocks,
        out_full,
        low_attended,
    )
    out_got = flip(out_sent, "u")
    extra_rows = qkv_rows + 16
    pair_of_heads = rows // 2

    def attend_back(first, grad):
        def of(shape):
            return pl.BlockSpec(
                shape, lambda step, places: (first + step,) + (0,) * (len(shape) - 1)
            )

        return kernel_call(
            attend_back_kernel,
            "attend_back",
            [((pair_of_heads, qkv_rows, SEQ), BF)]
            + [((pair_of_heads, 2, extra_rows, feats), BF)] * 2,
            places,
            qkv,
            grad,
            log_norm,
            attended,
            *token_rows,
            sums,
            grid=pair_of_heads,
            specs=[
                of((1, 3, head_rows, SEQ)),
                of((1, head_rows, SEQ)),
                of((1, 1, SEQ)),
                of((1, head_rows, SEQ)),
            ]
            + [fixed((SEQ, feats))] * 4
            + [fixed((8, width))],
            out_specs=[stepped((1, qkv_rows, SEQ), 0)]
            + [stepped((1, 2, extra_rows, feats), 0)] * 2,
            scratch=[pltpu.VMEM((SEQ, SEQ), BF)] * 2,
            vmem=30,
        )

    grads_late, late_mine, late_sent = attend_back(pair_of_heads, grad_att)
    late_got = flip(late_sent, "u")
    up_got = after(up_got, late_sent)
    up_both = (up_mine.astype(F32) + up_got.astype(F32)).astype(BF)
    grad_att, up_both = lax.optimization_barrier((grad_att, up_both))
    up_total = reduce_blocks(up_both)
    grads_early, early_mine, early_sent = attend_back(0, grad_att)
    early_got = flip(early_sent, "u")
    late_got = after(late_got, early_sent)
    sum_shape = (2, extra_rows + out_rows, feats)
    late_sums = kernel_call(
        late_sum_kernel,
        "late_sum",
        [(sum_shape, BF)] * (rows - pair_of_heads),
        places,
        late_mine,
        late_got,
        out_mine,
        out_got,
    )
    late_sums, grads_late = lax.optimization_barrier((late_sums, grads_late))
    moved = [
        shift(late_sums[i], "row", -(pair_of_heads + i)) for i in range(rows - pair_of_heads)
    ]

    grad_proj = jnp.concatenate([grads_early, grads_late])

    def back_to(index):
        return inner_rows(
            weight[index].reshape(rows * qkv_rows, feats), grad_proj.reshape(rows * qkv_rows, SEQ)
        )

    sent = to_far_chip(back_to(1), back_to(3).astype(BF))
    got = flip(sent, "t")
    early_got = after(early_got, sent)
    early_own, *early_sums = kernel_call(
        early_sum_kernel,
        "early_sum",
        [(sum_shape, F32)] + [(sum_shape, BF)] * (pair_of_heads - 1),
        places,
        early_mine,
        early_got,
        out_mine,
        out_got,
    )
    moved += [shift(early_sums[i - 1], "row", -i) for i in range(1, pair_of_heads)]
    near_own, near_send = kernel_call(
        input_near_kernel,
        "input_near",
        [((feats, SEQ), F32), ((feats, SEQ), BF)],
        places,
        *after((weight[0], weight[2]), sent),
        grad_proj,
        *d_blocks,
        vmem=24,
    )
    grad_in = (near_own + flip(near_send, "dp").astype(F32) + got.astype(F32)).astype(BF)
    grad_tokens = lax.ppermute(grad_in, ("dp", "u"), swap_cores)

    def by_chip(total):
        return cut(total, chip, feats, 1), cut(total, 1 - chip, feats, 1)

    down_parts = spread_weights(*by_chip(after(down_total, sent)))
    (down_out,) = kernel_call(
        last_down_kernel, "last_down", [((4 * ff_rows, feats), F32)], places, *down_parts
    )
    up_parts = spread_weights(*by_chip(after(up_total, near_own)))
    up_out, up_bias_out = kernel_call(
        last_up_kernel,
        "last_up",
        [((feats, 4 * ff_rows), F32), ((1, 4 * ff_rows), F32)],
        places,
        *up_parts,
    )
    moved[-1] = after(moved[-1], down_out, up_out, grad_in)
    qkv_sums = kernel_call(
        last_sum_kernel,
        "last_sum",
        [((extra_rows + out_rows, feats), BF)] * 2,
        places,
        early_own,
        *moved,
    )
    qkv_parts = spread_weights(*qkv_sums)
    grad_tokens = after(grad_tokens, qkv_parts[2]).astype(F32)
    qkv_out, qv_out, norm_out, out_out = kernel_call(
        last_attn_kernel,
        "last_attn",
        [
            ((3, feats, 4 * head_rows), F32),
            ((2, 4 * head_rows), F32),
            ((8, feats), F32),
            ((4 * out_rows, feats), F32),
        ],
        places,
        *qkv_parts,
        scratch=[pltpu.VMEM((4 * head_rows, feats), F32)],
    )

    result_far = after(flip(after(result_send, grad_att), "t"), late_sent)
    result_near = flip(jnp.stack([result_here[1], result_far[1]]), "dp")
    result_parts = [result_here[0], result_near[0], result_far[0], result_near[1]]
    result_seq = after(four_in_order(core, chip, result_parts, 1), early_sent)
    result_out = lax.ppermute(result_seq, ("dp", "u"), swap_cores)
    return (
        result_out,
        grad_tokens,
        qkv_out.transpose(1, 0, 2),
        qv_out,
        out_out,
        norm_out[0],
        norm_out[1],
        norm_out[2],
        up_out,
        up_bias_out[0],
        down_out,
        norm_out[3],
        norm_out[4],
        norm_out[5],
    )


def solution(mesh):
    sizes = dict(mesh.shape)
    grouped = sizes["dp"] == 2 and sizes["col"] == 4 and D % (4 * sizes["row"] * HEAD_DIM) == 0
    if grouped:
        devices = mesh.devices.reshape(sizes["dp"], sizes["row"], 2, 2)
        inner_mesh, col, body = Mesh(devices, ("dp", "row", "u", "t")), ("u", "t"), fast_shards
    else:
        inner_mesh, col, body = mesh, "col", shards
    tokens_spec = P(col, ("dp", "row"))
    return jax.shard_map(
        body,
        mesh=inner_mesh,
        in_specs=(
            tokens_spec,
            P(col, None, "row"),
            P(None, "row"),
            P("row", col),
            P(col),
            P(col),
            P(col),
            P(col, "row"),
            P("row"),
            P("row", col),
            P(col),
            P(col),
            P(col),
            tokens_spec,
        ),
        out_specs=(
            tokens_spec,
            tokens_spec,
            P(col, None, "row"),
            P(None, "row"),
            P("row", col),
            P(col),
            P(col),
            P(col),
            P(col, "row"),
            P("row"),
            P("row", col),
            P(col),
            P(col),
            P(col),
        ),
        check_vma=False,
    )
```

```python
import jax
import jax.numpy as jnp
from jax import lax
from jax.experimental import pallas as pl
from jax.experimental.pallas import tpu as pltpu
from jax.sharding import Mesh
from jax.sharding import PartitionSpec as P

D = 1024
HEAD_DIM = 64
SEQ = 1024


norm_eps = 1e-05


def matmul(first_mat, second_mat):
    return jnp.dot(first_mat, second_mat, preferred_element_type=jnp.float32)


def against(first_mat, second_mat):
    return lax.dot_general(
        first_mat, second_mat, (((1,), (1,)), ((), ())), preferred_element_type=jnp.float32
    )


def inner_rows(first_mat, second_mat):
    return lax.dot_general(
        first_mat, second_mat, (((0,), (0,)), ((), ())), preferred_element_type=jnp.float32
    )


def by_row(values):
    return lax.all_gather(values, "row", axis=0, tiled=True)


def by_col(values):
    return lax.all_gather(values, "col", axis=0, tiled=True)


def reduce_col(source, weight, transposed):
    row_count = source.shape[0] // lax.axis_size("col")

    def partial_value(row_start, row_num):
        return against(source, weight) if transposed else matmul(source, weight)

    return lax.psum_scatter(
        partial_value(jnp.int32(0), row_count * lax.axis_size("col")),
        "col",
        scatter_dimension=0,
        tiled=True,
    )


def reduce_row(source, weight, transposed):
    row_count = source.shape[0] // lax.axis_size("row")

    def partial_value(row_start, row_num):
        return against(source, weight) if transposed else matmul(source, weight)

    return lax.psum_scatter(
        partial_value(jnp.int32(0), row_count * lax.axis_size("row")),
        "row",
        scatter_dimension=0,
        tiled=True,
    )


def feature_totals(first_terms, second_terms):
    return lax.psum((jnp.sum(first_terms, axis=1), jnp.sum(second_terms, axis=1)), "col")


def norm_forward(residual, gain_vec, shift_vec):
    totals = feature_totals(residual, residual * residual)
    mean_rows = totals[0][:, None] / D
    spread = totals[1][:, None] / D - mean_rows * mean_rows
    scale_rows = lax.rsqrt(spread + norm_eps)
    normed = (residual - mean_rows) * scale_rows
    return (normed * gain_vec + shift_vec, normed, scale_rows)


def norm_backward(grad_in, normed, scale_rows, gain_vec):
    scaled = grad_in * gain_vec
    totals = feature_totals(scaled, scaled * normed)
    grad_resid = scale_rows * (scaled - totals[0][:, None] / D - normed * (totals[1][:, None] / D))
    return (grad_resid, jnp.sum(grad_in * normed, axis=0), jnp.sum(grad_in, axis=0))


def gelu_exact(values):
    return jax.nn.gelu(values, approximate=False)


def by_heads(values, head_count):
    seq_count = values.shape[0] // SEQ
    return values.reshape(seq_count, SEQ, head_count, HEAD_DIM)


def attention_forward(queries, key_seq, value_seq):
    block_len = min(512, SEQ)
    outputs = []
    log_parts = []
    for offset in range(0, SEQ, block_len):
        query_block = queries[:, offset : offset + block_len]
        scores = jnp.einsum(
            "nqhd,nkhd->nhqk", query_block, key_seq, preferred_element_type=jnp.float32
        )
        row_max = jnp.max(scores, axis=-1, keepdims=True)
        exp_scores = jnp.exp(scores - row_max)
        denom = jnp.sum(exp_scores, axis=-1, keepdims=True)
        probs_low = (exp_scores / denom).astype(jnp.bfloat16)
        outputs.append(
            jnp.einsum("nhqk,nkhd->nqhd", probs_low, value_seq, preferred_element_type=jnp.float32)
        )
        log_parts.append(row_max + jnp.log(denom))
    attended = jnp.concatenate(outputs, axis=1)
    rows_here = attended.shape[0] * SEQ
    return (
        attended.reshape(rows_here, -1).astype(jnp.bfloat16),
        jnp.concatenate(log_parts, axis=2),
    )


def attention_backward(queries, key_seq, value_seq, grad_seq, log_norm):
    block_len = min(512, SEQ)
    grad_query_parts = []
    grad_key = jnp.zeros(key_seq.shape, jnp.float32)
    grad_value = jnp.zeros(value_seq.shape, jnp.float32)
    for offset in range(0, SEQ, block_len):
        query_block = queries[:, offset : offset + block_len]
        grad_block = grad_seq[:, offset : offset + block_len]
        scores = jnp.einsum(
            "nqhd,nkhd->nhqk", query_block, key_seq, preferred_element_type=jnp.float32
        )
        probs = jnp.exp(scores - log_norm[:, :, offset : offset + block_len])
        grad_probs = jnp.einsum(
            "nqhd,nkhd->nhqk", grad_block, value_seq, preferred_element_type=jnp.float32
        )
        row_delta = jnp.sum(grad_probs * probs, axis=-1, keepdims=True)
        grad_scores = (probs * (grad_probs - row_delta)).astype(jnp.bfloat16)
        grad_query_parts.append(
            jnp.einsum("nhqk,nkhd->nqhd", grad_scores, key_seq, preferred_element_type=jnp.float32)
        )
        grad_key = grad_key + jnp.einsum(
            "nhqk,nqhd->nkhd", grad_scores, query_block, preferred_element_type=jnp.float32
        )
        grad_value = grad_value + jnp.einsum(
            "nhqk,nqhd->nkhd",
            probs.astype(jnp.bfloat16),
            grad_block,
            preferred_element_type=jnp.float32,
        )
    grad_query = jnp.concatenate(grad_query_parts, axis=1)
    rows_here = grad_query.shape[0] * SEQ
    return (
        grad_query.reshape(rows_here, -1).astype(jnp.bfloat16),
        grad_key.reshape(rows_here, -1).astype(jnp.bfloat16),
        grad_value.reshape(rows_here, -1).astype(jnp.bfloat16),
    )


def shards(
    tokens,
    w_qkv,
    b_qv,
    w_out,
    b_out,
    norm1_gain,
    norm1_shift,
    w_up,
    b_up,
    w_down,
    b_down,
    norm2_gain,
    norm2_shift,
    cotangent,
):
    token_major = tokens.T
    width_col = token_major.shape[1]
    width_row = w_out.shape[0]
    qkv_weight = w_qkv.reshape(width_col, 3 * width_row)
    query_scale = HEAD_DIM ** (-0.5)
    head_count = width_row // HEAD_DIM
    gathered_in = by_row(token_major)
    projected = reduce_col(gathered_in, qkv_weight, False).reshape(-1, 3, width_row)
    queries = ((projected[:, 0] + b_qv[0]) * query_scale).astype(jnp.bfloat16)
    key_rows = projected[:, 1].astype(jnp.bfloat16)
    value_rows = (projected[:, 2] + b_qv[1]).astype(jnp.bfloat16)
    query_seq = by_heads(queries, head_count)
    key_seq = by_heads(key_rows, head_count)
    value_seq = by_heads(value_rows, head_count)
    attended, log_norm = attention_forward(query_seq, key_seq, value_seq)
    gathered_att = by_col(attended)
    attn_out = reduce_row(gathered_att, w_out, False) + b_out
    residual1 = token_major.astype(jnp.float32) + attn_out
    normed_a, normed1, scale1 = norm_forward(residual1, norm1_gain, norm1_shift)
    low_a = normed_a.astype(jnp.bfloat16)
    gathered_a = by_row(low_a)
    pre_act = reduce_col(gathered_a, w_up, False) + b_up
    hidden, gelu_pull = jax.vjp(gelu_exact, pre_act)
    hidden_low = hidden.astype(jnp.bfloat16)
    gathered_h = by_col(hidden_low)
    branch_out = reduce_row(gathered_h, w_down, False)
    residual2 = normed_a + branch_out + b_down
    result, normed2, scale2 = norm_forward(residual2, norm2_gain, norm2_shift)
    grad_out = cotangent.T.astype(jnp.float32)
    grad_r2, gain2_part, shift2_part = norm_backward(grad_out, normed2, scale2, norm2_gain)
    down_bias_part = jnp.sum(grad_r2, axis=0)
    grad_branch = grad_r2.astype(jnp.bfloat16)
    gathered_df = by_row(grad_branch)
    down_grad = inner_rows(gathered_h, gathered_df)
    grad_hidden = reduce_col(gathered_df, w_down, True)
    grad_pre = gelu_pull(grad_hidden)[0].astype(jnp.bfloat16)
    gathered_dz = by_col(grad_pre)
    up_grad = inner_rows(gathered_a, gathered_dz)
    up_bias_grad = jnp.sum(gathered_dz, axis=0, dtype=jnp.float32)
    grad_a_ff = reduce_row(gathered_dz, w_up, True)
    grad_a = grad_r2 + grad_a_ff
    grad_r1, gain1_part, shift1_part = norm_backward(grad_a, normed1, scale1, norm1_gain)
    out_bias_part = jnp.sum(grad_r1, axis=0)
    gathered_datt = by_row(grad_r1.astype(jnp.bfloat16))
    out_grad = inner_rows(gathered_att, gathered_datt)
    grad_attended = reduce_col(gathered_datt, w_out, True).astype(jnp.bfloat16)
    grad_seq = by_heads(grad_attended, head_count)
    grad_query, grad_key, grad_value = attention_backward(
        query_seq, key_seq, value_seq, grad_seq, log_norm
    )
    grad_proj = jnp.stack([grad_query * query_scale, grad_key, grad_value], axis=1).reshape(
        -1, 3 * width_row
    )
    gathered_dqkv = by_col(grad_proj)
    qkv_grad = inner_rows(gathered_in, gathered_dqkv).reshape(width_col, 3, width_row)
    bias_rows = jnp.sum(gathered_dqkv, axis=0, dtype=jnp.float32).reshape(3, width_row)
    qv_bias_grad = jnp.stack([bias_rows[0], bias_rows[2]])
    grad_input = reduce_row(gathered_dqkv, qkv_weight, True) + grad_r1
    norm_sums = lax.psum(
        (gain1_part, shift1_part, gain2_part, shift2_part, out_bias_part, down_bias_part),
        ("dp", "row"),
    )
    weight_sums = lax.psum(
        (qkv_grad, qv_bias_grad, out_grad, up_grad, up_bias_grad, down_grad), "dp"
    )
    return (
        result.astype(jnp.bfloat16).T,
        grad_input.T,
        weight_sums[0],
        weight_sums[1],
        weight_sums[2],
        norm_sums[4],
        norm_sums[0],
        norm_sums[1],
        weight_sums[3],
        weight_sums[4],
        weight_sums[5],
        norm_sums[5],
        norm_sums[2],
        norm_sums[3],
    )


BF = jnp.bfloat16
F32 = jnp.float32
PAIR = ((0, 1), (1, 0))
MEBIBYTE = 1024 * 1024
BLOCK = 256


def flip(values, axis_name):
    return lax.ppermute(values, axis_name, PAIR)


def shift(values, axis_name, step):
    size = lax.axis_size(axis_name)
    return lax.ppermute(values, axis_name, [(i, (i + step) % size) for i in range(size)])


def in_order(index, mine, other, axis):
    first = jnp.where(index == 0, mine, other)
    second = jnp.where(index == 0, other, mine)
    return jnp.concatenate([first, second], axis)


def four_in_order(low_bit, high_bit, parts, axis):
    low = [jnp.where(low_bit == 0, parts[i], parts[i ^ 1]) for i in range(4)]
    full = [jnp.where(high_bit == 0, low[i], low[i ^ 2]) for i in range(4)]
    return jnp.concatenate(full, axis)


def cut(values, index, size, axis):
    return lax.dynamic_slice_in_dim(values, index * size, size, axis)


def after(values, *earlier):
    return lax.optimization_barrier((values, earlier))[0]


def part(index, size):
    return pl.ds(pl.multiple_of(index * size, size), size)


def kernel_call(kernel, name, outs, places, *inputs, grid=1, specs=None, out_specs=None, scratch=(), vmem=16, long=False):
    return pl.pallas_call(
        kernel,
        grid_spec=pltpu.PrefetchScalarGridSpec(
            num_scalar_prefetch=1,
            grid=(grid,),
            in_specs=[fixed(x.shape) for x in inputs] if specs is None else specs,
            out_specs=[fixed(shape) for shape, _ in outs] if out_specs is None else out_specs,
            scratch_shapes=list(scratch),
        ),
        out_shape=[jax.ShapeDtypeStruct(shape, dtype) for shape, dtype in outs],
        compiler_params=pltpu.CompilerParams(vmem_limit_bytes=vmem * MEBIBYTE),
        cost_estimate=pl.CostEstimate(
            flops=10**10 if long else 1, bytes_accessed=10**8 if long else 1, transcendentals=0
        ),
        name=name,
    )(places, *inputs)


def fixed(shape):
    return pl.BlockSpec(shape, lambda step, places: (0,) * len(shape))


def stepped(shape, axis):
    return pl.BlockSpec(
        shape, lambda step, places: tuple(step if i == axis else 0 for i in range(len(shape)))
    )


def prepare_attn_kernel(places, w_qkv, b_qv, w_out, *refs):
    vectors, (keep, send, turned) = refs[:-3], refs[-3:]
    head = turned.shape[1] // 4
    for piece in range(3):
        turned[piece] = w_qkv[piece].T
    for ref, quarter in ((keep, places[0]), (send, places[1])):
        for piece in range(3):
            ref[piece * head : (piece + 1) * head] = turned[piece, part(quarter, head), :]
        bias = b_qv[...].astype(F32)
        own = sum(
            jnp.where(quarter == q, bias[:, q * head : (q + 1) * head], 0.0) for q in range(4)
        )
        line = jnp.concatenate([own[0:1], own[1:2]], 1)
        line = jnp.concatenate([line, jnp.zeros((1, keep.shape[1] - 2 * head), F32)], 1)
        rows = [jnp.broadcast_to(line, (8, keep.shape[1]))]
        rows += [vector[...].astype(F32).reshape(1, -1) for vector in vectors]
        rows += [jnp.zeros((2, keep.shape[1]), F32)]
        ref[3 * head : 3 * head + 16] = jnp.concatenate(rows, 0).astype(BF)
        ref[3 * head + 16 :] = w_out[part(quarter, head), :]


def prepare_ff_kernel(places, w_up, w_down, keep, send):
    for ref, quarter in ((keep, places[0]), (send, places[1])):
        ref[:BLOCK] = w_up[:, part(quarter, BLOCK)].T
        ref[BLOCK:] = w_down[part(quarter, BLOCK), :]


def attend_kernel(places, x00, x01, x10, x11, own, far, qkv_ref, out_ref, norm_ref, *weight_refs):
    head_rows = qkv_ref.shape[2]
    total = None
    for side, pair in ((0, (x00, x01)), (1, (x10, x11))):
        mine = (places[3] ^ side) == places[2]
        for end, x in enumerate(pair):
            weight = jnp.where(mine, own[0, end, : 3 * head_rows], far[0, end, : 3 * head_rows])
            weight_refs[2 * side + end][0] = weight
            piece = matmul(weight, x[...])
            total = piece if total is None else total + piece
    bias = own[0, 0, 3 * head_rows : 3 * head_rows + 8].astype(F32)[0:1, : 2 * head_rows]
    bias = jnp.broadcast_to(bias, (2 * head_rows, 2 * head_rows)).T
    query = (total[:head_rows] + bias[:head_rows, 0:1]) * HEAD_DIM**-0.5
    qkv_ref[0, 0] = query.astype(BF)
    key = total[head_rows : 2 * head_rows].astype(BF)
    qkv_ref[0, 1] = key
    value = (total[2 * head_rows :] + bias[head_rows:, 0:1]).astype(BF)
    qkv_ref[0, 2] = value
    key_t = key.T
    for start in range(0, SEQ, BLOCK):
        here = slice(start, start + BLOCK)
        scores = matmul(key_t, qkv_ref[0, 0, :, here])
        top = jnp.max(scores, axis=0, keepdims=True)
        weights = jnp.exp(scores - top)
        denom = jnp.sum(weights, axis=0, keepdims=True)
        out_ref[0, :, here] = matmul(value, weights.astype(BF)) * (1.0 / denom)
        norm_ref[0, :, here] = top + jnp.log(denom)


def turn_kernel(places, *refs):
    for ref, out_ref in zip(refs[:4], refs[4:]):
        out_ref[...] = ref[...].T


def out_far_kernel(places, early, late, own, far, own_ref, send_ref, full_ref, low_ref):
    heads, head_rows, _ = low_ref.shape
    half = far.shape[2]
    low_ref[: early.shape[0]] = early[...].astype(BF)
    low_ref[early.shape[0] :] = late[...].astype(BF)
    for head in range(heads):
        rows = slice(head * head_rows, (head + 1) * head_rows)
        full_ref[rows, part(places[2], half)] = own[head, 8:, :]
        full_ref[rows, part(1 - places[2], half)] = far[head, 8:, :]
    out_block(places, 3, low_ref, full_ref, send_ref)
    out_block(places, 2, low_ref, full_ref, own_ref)


def out_near_kernel(places, attended, full_ref, own_ref, send_ref):
    out_block(places, 1, attended, full_ref, send_ref)
    out_block(places, 0, attended, full_ref, own_ref)


def out_block(places, step, attended, full_ref, out_ref):
    rows = attended[:, :, part(places[0] ^ step, BLOCK)].reshape(-1, BLOCK)
    out_ref[...] = inner_rows(rows, full_ref[...]).astype(out_ref.dtype)


def norm1_kernel(places, near, core, got, x00, x01, x10, x11, vec, a_ref, low_ref, normed_ref, scale_ref):
    for side, pair in ((0, (x00, x01)), (1, (x10, x11))):
        for end, x in enumerate(pair):
            block = 2 * (places[3] ^ side) + (places[4] ^ end)
            a_ref[:, part(block, BLOCK)] = x[...].T.astype(F32)
    residual = a_ref[...] + (near[...] + core[...].astype(F32) + got[...].astype(F32) + vec[0:1])
    mean_rows = jnp.mean(residual, axis=1, keepdims=True)
    spread = jnp.mean(residual * residual, axis=1, keepdims=True) - mean_rows * mean_rows
    scale_rows = lax.rsqrt(spread + norm_eps)
    normed = (residual - mean_rows) * scale_rows
    values = normed * vec[1:2] + vec[2:3]
    a_ref[...] = values
    low_ref[...] = values.astype(BF)
    normed_ref[...] = normed
    scale_ref[...] = scale_rows


def back_of_norm(grad_in, normed, scale_rows, gain_vec):
    scaled = grad_in * gain_vec
    first = jnp.mean(scaled, axis=1, keepdims=True)
    second = jnp.mean(scaled * normed, axis=1, keepdims=True)
    return scale_rows * (scaled - first - normed * second)


def add_sums(sums_ref, *arrays):
    @pl.when(pl.program_id(0) == 0)
    def _():
        sums_ref[...] = jnp.zeros_like(sums_ref)

    for index, values in enumerate(arrays):
        sums_ref[index : index + 1] += jnp.sum(values, axis=0, keepdims=True)


def norm2_kernel(places, near, core, got, a_ref, c0, c1, c2, c3, vec, here_ref, send_ref, grad_ref, low_ref, sums_ref):
    for index, piece in enumerate((c0, c1, c2, c3)):
        block = 2 * (places[3] ^ (index >> 1)) + (places[4] ^ (index & 1))
        grad_ref[:, part(block, BLOCK)] = piece[...].T.astype(F32)
    branch = near[...] + core[...].astype(F32) + got[...].astype(F32) + vec[3:4]
    residual = a_ref[...] + branch
    mean_rows = jnp.mean(residual, axis=1, keepdims=True)
    spread = jnp.mean(residual * residual, axis=1, keepdims=True) - mean_rows * mean_rows
    scale_rows = lax.rsqrt(spread + norm_eps)
    normed = (residual - mean_rows) * scale_rows
    grad_out = grad_ref[...]
    grad = back_of_norm(grad_out, normed, scale_rows, vec[4:5])
    add_sums(sums_ref, grad, grad_out * normed, grad_out)
    grad_ref[...] = normed * vec[4:5] + vec[5:6]
    for side in range(2):
        for end, ref in ((0, here_ref), (1, send_ref)):
            block = 2 * (places[3] ^ side) + (places[4] ^ end)
            ref[side] = grad_ref[:, part(block, BLOCK)].T.astype(BF)
    grad_ref[...] = grad
    low_ref[...] = grad.astype(BF)


def norm1_back_kernel(places, near, core, got, grad2, normed_ref, scale_ref, vec, sums2, low_ref, sums_ref):
    grad_in = grad2[...] + (near[...] + core[...].astype(F32) + got[...].astype(F32))
    normed = normed_ref[...]
    grad = back_of_norm(grad_in, normed, scale_ref[...], vec[1:2])
    add_sums(sums_ref, grad, grad_in * normed, grad_in)
    sums_ref[3:6] = sums2[0:3]
    low_ref[...] = grad.astype(BF)


def weight_grad_kernel(places, left_near, left_far, r0, r1, r2, r3, mine_ref, sent_ref, right):
    half = mine_ref.shape[2]

    @pl.when(pl.program_id(0) == 0)
    def _():
        for index, rows in enumerate((r0, r1, r2, r3)):
            here = slice(index * BLOCK, (index + 1) * BLOCK)
            right[0, here] = rows[:, part(places[2], half)]
            right[1, here] = rows[:, part(1 - places[2], half)]

    left = jnp.concatenate([left_near[...], left_far[...]], 0)
    sent_ref[0, :BLOCK] = inner_rows(left, right[1]).astype(BF)
    mine_ref[0, :BLOCK] = inner_rows(left, right[0]).astype(BF)
    if mine_ref.shape[1] > BLOCK:
        sums = jnp.sum(left.astype(F32), axis=0, keepdims=True)
        sums = jnp.broadcast_to(jnp.concatenate([sums, sums], 1), (8, half)).astype(BF)
        sent_ref[0, BLOCK:] = sums
        mine_ref[0, BLOCK:] = sums


def out_back_kernel(places, d0, d1, d2, d3, full_ref, attended, grad_ref, mine_ref, sent_ref):
    heads, head_rows, _ = attended.shape
    blocks = (d0, d1, d2, d3)
    left = []
    for step, rows in enumerate(blocks):
        here = part(places[0] ^ step, BLOCK)
        grad = against(full_ref[...], rows[...]).astype(BF)
        grad_ref[:, :, here] = grad.reshape(heads, head_rows, BLOCK)
        left.append(attended[:, :, here].reshape(-1, BLOCK))
    width = mine_ref.shape[3]
    for ref, side in ((sent_ref, 1 - places[2]), (mine_ref, places[2])):
        for end in range(2):
            columns = part(2 * side + (places[4] ^ end), width)
            total = None
            for piece, rows in zip(left, blocks):
                product = matmul(piece, rows[:, columns])
                total = product if total is None else total + product
            ref[:, end] = total.astype(BF).reshape(heads, head_rows, width)


def attend_back_kernel(
    places, qkv_ref, grad_ref, norm_ref, attended, out_mine, out_sent, x00, x01, x10, x11, sums, out_ref, mine_ref, sent_ref, probs_low, scores_low
):
    head_rows = qkv_ref.shape[2]
    key = qkv_ref[0, 1]
    key_t = key.T
    value_t = qkv_ref[0, 2].T
    for start in range(0, SEQ, BLOCK):
        here = slice(start, start + BLOCK)
        grad = grad_ref[0, :, here]
        probs = jnp.exp(matmul(key_t, qkv_ref[0, 0, :, here]) - norm_ref[0, :, here])
        delta = jnp.sum(grad.astype(F32) * attended[0, :, here], axis=0, keepdims=True)
        grad_scores = (probs * (matmul(value_t, grad) - delta)).astype(BF)
        probs_low[:, here] = probs.astype(BF)
        scores_low[:, here] = grad_scores
        grad_query = matmul(key, grad_scores).astype(BF)
        out_ref[0, :head_rows, here] = (grad_query.astype(F32) * HEAD_DIM**-0.5).astype(BF)
    grad_key = matmul(scores_low[...], qkv_ref[0, 0].T)
    out_ref[0, head_rows : 2 * head_rows] = grad_key.T.astype(BF)
    grad_value = matmul(probs_low[...], grad_ref[0].T)
    out_ref[0, 2 * head_rows :] = grad_value.T.astype(BF)
    left = out_ref[0]
    bias = jnp.sum(left.astype(F32), axis=1, keepdims=True)
    bias = jnp.concatenate([bias[:head_rows], bias[2 * head_rows :]], 0)
    bias = jnp.broadcast_to(bias, (2 * head_rows, 2 * head_rows)).T[:8]
    bias = jnp.concatenate([bias, jnp.zeros((8, BLOCK - 2 * head_rows), F32)], 1)
    rows = 3 * head_rows
    for side, pair in ((0, (x00, x01)), (1, (x10, x11))):
        mine = (places[3] ^ side) == places[2]
        for end, x in enumerate(pair):
            weight = matmul(left, x[...]).astype(BF)
            block = sums[:, part(2 * (places[3] ^ side) + (places[4] ^ end), BLOCK)]
            extra = jnp.concatenate([block, bias], 0).astype(BF)

            @pl.when(mine)
            def _():
                mine_ref[0, end, :rows] = weight
                mine_ref[0, end, rows : rows + 16] = extra
                mine_ref[0, end, rows + 16 :] = out_mine[0, end]

            @pl.when(jnp.logical_not(mine))
            def _():
                sent_ref[0, end, :rows] = weight
                sent_ref[0, end, rows : rows + 16] = extra
                sent_ref[0, end, rows + 16 :] = out_sent[0, end]


def late_sum_kernel(places, mine, got, *sums):
    for head, ref in enumerate(sums):
        ref[...] = (mine[head].astype(F32) + got[head].astype(F32)).astype(BF)


def early_sum_kernel(places, mine, got, own_ref, *sums):
    own_ref[...] = mine[0].astype(F32) + got[0].astype(F32)
    for head, ref in enumerate(sums):
        ref[...] = (mine[head + 1].astype(F32) + got[head + 1].astype(F32)).astype(BF)


def sum_kernel(places, mine, got, own_ref, *sums):
    own_ref[...] = mine[0].astype(F32) + got[0].astype(F32)
    for block, ref in enumerate(sums):
        ref[...] = (mine[block + 1].astype(F32) + got[block + 1].astype(F32)).astype(BF)


def last_sum_kernel(places, *refs):
    here, there = refs[-2:]
    inputs = refs[:-2]
    third = len(inputs) // 3
    first = 0
    for group in range(3):
        pieces = inputs[group * third : (group + 1) * third]
        total = pieces[0][...]
        for ref in pieces[1:]:
            total = total + ref[...].astype(F32)
        if total.ndim == 3:
            mine, other = total[0], total[1]
        else:
            width = total.shape[1] // 2
            left, right = total[:, :width], total[:, width:]
            mine = jnp.where(places[4] == 0, left, right)
            other = jnp.where(places[4] == 0, right, left)
        rows = mine.shape[0]
        here[first : first + rows] = mine.astype(BF)
        there[first : first + rows] = other.astype(BF)
        first += rows


def input_near_kernel(places, own0, own1, send0, send1, grads0, grads1, d0, d1, d2, d3, own_ref, send_ref):
    def product(first, second):
        pairs = ((first, grads0), (second, grads1))
        flat = [[ref[...].reshape(-1, ref.shape[2]) for ref in pair] for pair in pairs]
        return inner_rows(*flat[0]) + inner_rows(*flat[1])

    send_ref[...] = product(send0, send1).astype(BF)
    own_ref[...] = product(own0, own1)
    block = 2 * places[3] + places[4]
    for step, d in enumerate((d0, d1, d2, d3)):
        here = part(places[0] ^ step, BLOCK)
        own_ref[:, here] += d[:, part(block, BLOCK)].T.astype(F32)


def last_kernel(
    places, p0, p1, p2, p3, qkv_out, qv_out, norm_out, out_out, down_out, up_out, bias_out, turned
):
    parts = (p0, p1, p2, p3)
    head = turned.shape[0] // 4
    for piece in range(3):
        for step, ref in enumerate(parts):
            turned[part(places[0] ^ step, head), :] = ref[piece * head : (piece + 1) * head].astype(F32)
        qkv_out[piece] = turned[...].T
    extra = [ref[3 * head : 3 * head + 16].astype(F32) for ref in parts]
    norm_out[...] = extra[0][:8] + extra[1][:8] + extra[2][:8] + extra[3][:8]
    lines = [[], []]
    for quarter in range(4):
        line = sum(
            jnp.where((places[0] ^ step) == quarter, extra[step][8:9], 0.0) for step in range(4)
        )
        lines[0].append(line[:, :head])
        lines[1].append(line[:, head : 2 * head])
    qv_out[...] = jnp.concatenate([jnp.concatenate(line, 1) for line in lines], 0)
    first = 4 * head + 16
    for step, ref in enumerate(parts):
        quarter = places[0] ^ step
        out_out[part(quarter, head), :] = ref[3 * head + 16 : first].astype(F32)
        down_out[part(quarter, BLOCK), :] = ref[first : first + BLOCK].astype(F32)
        up_out[:, part(quarter, BLOCK)] = ref[first + BLOCK : first + 2 * BLOCK].astype(F32).T
        bias_out[:, part(quarter, BLOCK)] = ref[first + 2 * BLOCK :].astype(F32)[0:1]


def to_far_chip(own, send):
    return (own + flip(send, "dp").astype(F32)).astype(BF)


def gather_rows(payload):
    size = lax.axis_size("row")
    return [payload] + [shift(payload, "row", step) for step in range(1, size)]


def move_rows(sums):
    return [shift(block, "row", -1 - i) for i, block in enumerate(sums)]


def spread_weights(mine, other):
    near = jnp.stack([mine, flip(other, "t")])
    far = flip(near, "dp")
    return near[0], far[0], near[1], far[1]


def fast_shards(
    tokens,
    w_qkv,
    b_qv,
    w_out,
    b_out,
    norm1_gain,
    norm1_shift,
    w_up,
    b_up,
    w_down,
    b_down,
    norm2_gain,
    norm2_shift,
    cotangent,
):
    core, chip = lax.axis_index("dp"), lax.axis_index("t")
    u_index, row = lax.axis_index("u"), lax.axis_index("row")
    rows = lax.axis_size("row")
    quarter = 2 * chip + core
    other_quarter = 2 * (1 - chip) + core
    places = jnp.stack([quarter, other_quarter, u_index, core, chip, row]).astype(jnp.int32)
    feats = tokens.shape[0]
    width = 4 * feats
    half = 2 * feats
    own_rows = SEQ // 4
    swap_cores = [(2 * d + u, 2 * u + d) for d in range(2) for u in range(2)]
    head_rows = w_out.shape[0] // 4
    qkv_rows, out_rows, ff_rows = 3 * head_rows, head_rows, w_down.shape[0] // 4

    x00 = lax.ppermute(tokens, ("dp", "u"), swap_cores)

    attn_rows = qkv_rows + 16 + out_rows
    attn_keep, attn_send = kernel_call(
        prepare_attn_kernel,
        "prepare_attn",
        [((attn_rows, feats), BF)] * 2,
        places,
        w_qkv.transpose(1, 0, 2),
        b_qv,
        w_out,
        b_out,
        norm1_gain,
        norm1_shift,
        b_down,
        norm2_gain,
        norm2_shift,
        scratch=[pltpu.VMEM((3, 4 * head_rows, feats), BF)],
        vmem=60,
    )
    attn_got = flip(attn_send, "t")
    ff_keep, ff_send = kernel_call(
        prepare_ff_kernel, "prepare_ff", [((2 * ff_rows, feats), BF)] * 2, places, after(w_up, attn_send), w_down, vmem=60
    )
    ff_got = flip(ff_send, "t")
    attn_got = after(attn_got, x00)
    cot = lax.ppermute(after(cotangent, x00), ("dp", "u"), swap_cores)
    x01 = flip(x00, "t")
    x10, x11 = flip(x00, "dp"), flip(x01, "dp")
    cot = after(cot, x01)
    cot_parts = [cut(cot, quarter ^ j, own_rows, 1) for j in range(4)]
    cot_far = flip(jnp.stack([cot_parts[2], cot_parts[3]]), "t")
    cot_near = flip(jnp.stack([cot_parts[1], cot_far[1]]), "dp")

    qkv_part = jnp.stack([attn_keep[: qkv_rows + 8], attn_got[: qkv_rows + 8]])
    ff_got = after(ff_got, qkv_part)
    qkv_own = jnp.stack(gather_rows(qkv_part))
    attn_both = in_order(chip, attn_keep[qkv_rows + 8 :], attn_got[qkv_rows + 8 :], 1)
    ff_both = in_order(chip, ff_keep, ff_got, 1)
    up_bias = lax.dynamic_index_in_dim(b_up.reshape(4, -1), quarter, 0, True)
    up_bias = jnp.pad(up_bias, ((0, 7), (0, half - ff_rows)))
    mixed_part = jnp.concatenate([attn_both, ff_both[:ff_rows], up_bias])
    mixed_pieces = gather_rows(after(mixed_part, qkv_own))
    qkv_far = flip(after(qkv_own, x01), "u")

    x_blocks = (x00, x01, x10, x11)
    pair_of_heads = rows // 2

    def attend(first, far_half):
        def of(shape):
            return pl.BlockSpec(
                shape, lambda step, places: (first + step,) + (0,) * (len(shape) - 1)
            )

        return kernel_call(
            attend_kernel,
            "attend",
            [
                ((pair_of_heads, 3, head_rows, SEQ), BF),
                ((pair_of_heads, head_rows, SEQ), F32),
                ((pair_of_heads, 1, SEQ), F32),
            ]
            + [((pair_of_heads, qkv_rows, feats), BF)] * 4,
            places,
            *x_blocks,
            qkv_own,
            far_half,
            grid=pair_of_heads,
            specs=[fixed((feats, SEQ))] * 4 + [of((1, 2, qkv_rows + 8, feats))] * 2,
            out_specs=[
                stepped((1, 3, head_rows, SEQ), 0),
                stepped((1, head_rows, SEQ), 0),
                stepped((1, 1, SEQ), 0),
            ]
            + [stepped((1, qkv_rows, feats), 0)] * 4,
            vmem=28,
            long=True,
        )

    qkv_early, attended_early, norm_early, *weight_early = attend(0, qkv_far)
    mixed_own = jnp.stack(after(mixed_pieces, norm_early, cot_near))
    down_pieces = gather_rows(after(ff_both[ff_rows:], mixed_own))
    vec_rows = 8 + out_rows
    out_own, up_own = mixed_own[:, :vec_rows], mixed_own[:, vec_rows:]
    out_far = flip(out_own, "u")
    up_far = flip(up_own, "u")
    far_late = after(qkv_far, mixed_own)
    qkv_late, attended_late, norm_late, *weight_late = attend(pair_of_heads, far_late)
    attended_late = after(attended_late, down_pieces[1])
    bias_up = up_own[:, ff_rows, :ff_rows].reshape(1, -1).astype(F32)
    vec = in_order(u_index, out_own[0, :8], out_far[0, :8], 1).astype(F32)
    up_pair = [x[:, :ff_rows].reshape(rows * ff_rows, half) for x in (up_own, up_far)]
    up_full = in_order(u_index, *up_pair, 1)

    row_block = (own_rows, width)
    pair_outs = [(row_block, F32), (row_block, BF)]
    far_own, far_send, out_full, low_attended = kernel_call(
        out_far_kernel,
        "out_far",
        pair_outs + [((rows * head_rows, width), BF), ((rows, head_rows, SEQ), BF)],
        places,
        attended_early,
        attended_late,
        out_own,
        out_far,
    )
    sent = to_far_chip(far_own, far_send)
    near_attended = after(low_attended, sent)
    got = flip(sent, "t")
    near_own, near_send = kernel_call(
        out_near_kernel, "out_near", pair_outs, places, near_attended, out_full
    )
    token_rows = kernel_call(
        turn_kernel, "turn", [((SEQ, feats), BF)] * 4, places, *after(x_blocks, near_own)
    )
    down_own = jnp.stack(after(down_pieces, token_rows))
    down_far = flip(down_own, "u").reshape(rows * ff_rows, half)
    down_full = in_order(u_index, down_own.reshape(rows * ff_rows, half), down_far, 1)
    near_got = flip(near_send, "dp")
    got = after(got, near_got, token_rows, up_far, down_own)
    chunk = own_rows // 2
    row_chunk = stepped((chunk, width), 0)
    own_tokens = pl.BlockSpec((feats, chunk), lambda step, places: (0, 2 * places[0] + step))
    normed_a, low_a, normed1, scale1 = kernel_call(
        norm1_kernel,
        "norm1",
        [(row_block, F32), (row_block, BF), (row_block, F32), ((own_rows, 1), F32)],
        places,
        near_own,
        near_got,
        got,
        *x_blocks,
        vec,
        grid=2,
        specs=[row_chunk] * 3 + [own_tokens] * 4 + [fixed((8, width))],
        out_specs=[row_chunk] * 3 + [stepped((chunk, 1), 0)],
    )

    def up(rows_in):
        pre = against(rows_in, up_full) + bias_up
        cdf = 0.5 * (1.0 + lax.erf(pre * (0.5**0.5)))
        slope = cdf + pre * (jnp.exp(-0.5 * pre * pre) * 0.3989422804014327)
        return (pre * cdf).astype(BF), slope

    a0, a1, a2 = low_a, flip(low_a, "dp"), flip(low_a, "t")
    hidden_near, slope_near = up(jnp.concatenate([a0, a1]))
    a2 = after(a2, hidden_near)
    a3 = flip(a2, "dp")
    hidden_far, slope_far = up(jnp.concatenate([a2, a3]))
    far_send = matmul(hidden_far[own_rows:], down_full).astype(BF)
    sent = to_far_chip(matmul(hidden_far[:own_rows], down_full), far_send)
    near_hidden = after(hidden_near, sent)
    got = flip(sent, "t")
    near_got = flip(matmul(near_hidden[own_rows:], down_full).astype(BF), "dp")
    near_own = matmul(near_hidden[:own_rows], down_full)
    got = after(got, near_got)
    turned_chunk = stepped((feats, chunk), 1)
    pair_chunk = stepped((2, feats, chunk), 2)
    result_here, result_send, grad_r2, low_g, sums2 = kernel_call(
        norm2_kernel,
        "norm2",
        [((2, feats, own_rows), BF)] * 2 + [(row_block, F32), (row_block, BF), ((8, width), F32)],
        places,
        near_own,
        near_got,
        got,
        normed_a,
        cot_parts[0],
        cot_far[0],
        cot_near[0],
        cot_near[1],
        vec,
        grid=2,
        specs=[row_chunk] * 4 + [turned_chunk] * 4 + [fixed((8, width))],
        out_specs=[pair_chunk] * 2 + [row_chunk] * 2 + [fixed((8, width))],
    )

    two_blocks = 2 * own_rows

    def weight_grad(near, far, blocks, extra):
        shape = (rows, ff_rows + extra, half)
        return kernel_call(
            weight_grad_kernel,
            "weight_grad",
            [(shape, BF)] * 2,
            places,
            near,
            far,
            *blocks,
            grid=rows,
            specs=[stepped((two_blocks, ff_rows), 1)] * 2 + [fixed(row_block)] * 4,
            out_specs=[stepped((1, *shape[1:]), 0)] * 2,
            scratch=[pltpu.VMEM((2, SEQ, half), BF)],
            long=True,
        )

    g0, g1, g2 = low_g, flip(low_g, "dp"), flip(low_g, "t")
    grad_pre_near = (against(jnp.concatenate([g0, g1]), down_full) * slope_near).astype(BF)
    g2 = after(g2, grad_pre_near)
    g3 = flip(g2, "dp")
    grad_pre_far = (against(jnp.concatenate([g2, g3]), down_full) * slope_far).astype(BF)
    far_send = matmul(grad_pre_far[own_rows:], up_full).astype(BF)
    sent = to_far_chip(matmul(grad_pre_far[:own_rows], up_full), far_send)
    near_pre = after(grad_pre_near, sent)
    got = flip(sent, "t")
    near_got = flip(matmul(near_pre[own_rows:], up_full).astype(BF), "dp")
    near_own = matmul(near_pre[:own_rows], up_full)
    hiddens, pres = after(((hidden_near, hidden_far), (near_pre, grad_pre_far)), near_own)
    down_mine, down_sent = weight_grad(*hiddens, (g0, g1, g2, g3), 0)
    down_got = flip(down_sent, "u")
    up_mine, up_sent = weight_grad(*pres, (a0, a1, a2, a3), 8)
    got = after(got, near_got, up_sent)
    low_r1, sums = kernel_call(
        norm1_back_kernel,
        "norm1_back",
        [(row_block, BF), ((8, width), F32)],
        places,
        near_own,
        near_got,
        got,
        grad_r2,
        normed1,
        scale1,
        vec,
        sums2,
        grid=2,
        specs=[row_chunk] * 5 + [stepped((chunk, 1), 0)] + [fixed((8, width))] * 2,
        out_specs=[row_chunk, fixed((8, width))],
    )

    d0, d1, d2 = low_r1, flip(low_r1, "dp"), flip(low_r1, "t")
    down_got = after(down_got, low_r1)
    up_sent, down_got = lax.optimization_barrier((up_sent, down_got))
    up_got = flip(up_sent, "u")
    d2 = after(d2, down_got)

    def sums_of(mine, got):
        shape = mine.shape[1:]
        return kernel_call(
            sum_kernel, "sum", [(shape, F32)] + [(shape, BF)] * (rows - 1), places, mine, got
        )

    d3 = flip(d2, "dp")
    d_blocks = (d0, d1, d2, d3)
    out_shape = (rows, 2, out_rows, feats)
    grad_att, out_mine, out_sent = kernel_call(
        out_back_kernel,
        "out_back",
        [((rows, head_rows, SEQ), BF)] + [(out_shape, BF)] * 2,
        places,
        *d_blocks,
        out_full,
        low_attended,
    )
    down_total, *down_sums = sums_of(down_mine, after(down_got, grad_att))
    grad_att = after(grad_att, down_sums)
    down_moved = move_rows(down_sums)
    extra_rows = qkv_rows + 16 + out_rows

    def attend_back(first, grad, qkv, log_norm, attended):
        def of(shape):
            return pl.BlockSpec(
                shape, lambda step, places: (first + step,) + (0,) * (len(shape) - 1)
            )

        return kernel_call(
            attend_back_kernel,
            "attend_back",
            [((pair_of_heads, qkv_rows, SEQ), BF)]
            + [((pair_of_heads, 2, extra_rows, feats), BF)] * 2,
            places,
            qkv,
            grad,
            log_norm,
            attended,
            out_mine,
            out_sent,
            *token_rows,
            sums,
            grid=pair_of_heads,
            specs=[
                stepped((1, 3, head_rows, SEQ), 0),
                of((1, head_rows, SEQ)),
                stepped((1, 1, SEQ), 0),
                stepped((1, head_rows, SEQ), 0),
                of((1, 2, out_rows, feats)),
                of((1, 2, out_rows, feats)),
            ]
            + [fixed((SEQ, feats))] * 4
            + [fixed((8, width))],
            out_specs=[stepped((1, qkv_rows, SEQ), 0)]
            + [stepped((1, 2, extra_rows, feats), 0)] * 2,
            scratch=[pltpu.VMEM((SEQ, SEQ), BF)] * 2,
            vmem=30,
            long=True,
        )

    result_far = flip(after(result_send, d3), "t")
    result_near = flip(jnp.stack([result_here[1], result_far[1]]), "dp")
    result_parts = [result_here[0], result_near[0], result_far[0], result_near[1]]

    grads_late, late_mine, late_sent = attend_back(
        pair_of_heads, grad_att, qkv_late, norm_late, attended_late
    )
    late_got = flip(late_sent, "u")
    up_total, *up_sums = sums_of(up_mine, after(up_got, late_sent))
    up_moved = move_rows(up_sums)
    early_att = after(grad_att, up_sums, down_moved, result_near)
    grads_early, early_mine, early_sent = attend_back(
        0, early_att, qkv_early, norm_early, attended_early
    )
    early_got = flip(early_sent, "u")
    sum_shape = (2, extra_rows, feats)
    def back_to(index, grads_early):
        pairs = ((weight_early[index], grads_early), (weight_late[index], grads_late))
        products = [
            inner_rows(w.reshape(-1, feats), grads.reshape(-1, SEQ)) for w, grads in pairs
        ]
        return products[0] + products[1]

    grads_now = after(grads_early, late_got, up_moved[0], up_moved[2:])
    far_send = back_to(3, grads_now).astype(BF)
    sent = to_far_chip(back_to(1, grads_now), far_send)
    got = flip(sent, "t")
    late_sums = kernel_call(
        late_sum_kernel,
        "late_sum",
        [(sum_shape, BF)] * (rows - pair_of_heads),
        places,
        late_mine,
        after(late_got, sent, up_moved),
    )
    moved = [
        shift(late_sums[i], "row", -(pair_of_heads + i)) for i in range(rows - pair_of_heads)
    ]


    early_own, *early_sums = kernel_call(
        early_sum_kernel,
        "early_sum",
        [(sum_shape, F32)] + [(sum_shape, BF)] * (pair_of_heads - 1),
        places,
        early_mine,
        after(early_got, late_sums),
    )
    moved += [shift(early_sums[i - 1], "row", -i) for i in range(1, pair_of_heads)]

    near_own, near_send = kernel_call(
        input_near_kernel,
        "input_near",
        [((feats, SEQ), F32), ((feats, SEQ), BF)],
        places,
        weight_early[0],
        weight_late[0],
        weight_early[2],
        weight_late[2],
        after(grads_early, early_sums),
        grads_late,
        *d_blocks,
        vmem=24,
    )
    near_got = flip(near_send, "dp")
    grad_in = (near_own + near_got.astype(F32) + got.astype(F32)).astype(BF)
    grad_tokens = lax.ppermute(grad_in, ("dp", "u"), swap_cores)
    result_seq = after(four_in_order(core, chip, result_parts, 1), early_sums)
    result_out = lax.ppermute(result_seq, ("dp", "u"), swap_cores)
    last_shape = (extra_rows + 2 * ff_rows + 8, feats)
    last_sums = kernel_call(
        last_sum_kernel,
        "last_sum",
        [(last_shape, BF)] * 2,
        places,
        after(early_own, grad_in, result_out),
        *moved,
        down_total,
        *down_moved,
        up_total,
        *up_moved,
    )
    last_parts = spread_weights(after(last_sums[0], grad_tokens), last_sums[1])
    grad_tokens = after(grad_tokens, last_parts[2]).astype(F32)
    qkv_out, qv_out, norm_out, out_out, down_out, up_out, up_bias_out = kernel_call(
        last_kernel,
        "last",
        [
            ((3, feats, 4 * head_rows), F32),
            ((2, 4 * head_rows), F32),
            ((8, feats), F32),
            ((4 * out_rows, feats), F32),
            ((4 * ff_rows, feats), F32),
            ((feats, 4 * ff_rows), F32),
            ((1, 4 * ff_rows), F32),
        ],
        places,
        *last_parts,
        scratch=[pltpu.VMEM((4 * head_rows, feats), F32)],
    )

    return (
        result_out,
        grad_tokens,
        qkv_out.transpose(1, 0, 2),
        qv_out,
        out_out,
        norm_out[0],
        norm_out[1],
        norm_out[2],
        up_out,
        up_bias_out[0],
        down_out,
        norm_out[3],
        norm_out[4],
        norm_out[5],
    )


def solution(mesh):
    sizes = dict(mesh.shape)
    grouped = sizes["dp"] == 2 and sizes["col"] == 4 and D % (4 * sizes["row"] * HEAD_DIM) == 0
    if grouped:
        devices = mesh.devices.reshape(sizes["dp"], sizes["row"], 2, 2)
        inner_mesh, col, body = Mesh(devices, ("dp", "row", "u", "t")), ("u", "t"), fast_shards
    else:
        inner_mesh, col, body = mesh, "col", shards
    tokens_spec = P(col, ("dp", "row"))
    return jax.shard_map(
        body,
        mesh=inner_mesh,
        in_specs=(
            tokens_spec,
            P(col, None, "row"),
            P(None, "row"),
            P("row", col),
            P(col),
            P(col),
            P(col),
            P(col, "row"),
            P("row"),
            P("row", col),
            P(col),
            P(col),
            P(col),
            tokens_spec,
        ),
        out_specs=(
            tokens_spec,
            tokens_spec,
            P(col, None, "row"),
            P(None, "row"),
            P("row", col),
            P(col),
            P(col),
            P(col),
            P(col, "row"),
            P("row"),
            P("row", col),
            P(col),
            P(col),
            P(col),
        ),
        check_vma=False,
    )
```

```python
import jax
import jax.numpy as jnp
from jax import lax
from jax.experimental import pallas as pl
from jax.experimental.pallas import tpu as pltpu
from jax.sharding import Mesh
from jax.sharding import PartitionSpec as P

D = 1024
HEAD_DIM = 64
SEQ = 1024


norm_eps = 1e-05


def matmul(first_mat, second_mat):
    return jnp.dot(first_mat, second_mat, preferred_element_type=jnp.float32)


def against(first_mat, second_mat):
    return lax.dot_general(
        first_mat, second_mat, (((1,), (1,)), ((), ())), preferred_element_type=jnp.float32
    )


def inner_rows(first_mat, second_mat):
    return lax.dot_general(
        first_mat, second_mat, (((0,), (0,)), ((), ())), preferred_element_type=jnp.float32
    )


def by_row(values):
    return lax.all_gather(values, "row", axis=0, tiled=True)


def by_col(values):
    return lax.all_gather(values, "col", axis=0, tiled=True)


def reduce_col(source, weight, transposed):
    row_count = source.shape[0] // lax.axis_size("col")

    def partial_value(row_start, row_num):
        return against(source, weight) if transposed else matmul(source, weight)

    return lax.psum_scatter(
        partial_value(jnp.int32(0), row_count * lax.axis_size("col")),
        "col",
        scatter_dimension=0,
        tiled=True,
    )


def reduce_row(source, weight, transposed):
    row_count = source.shape[0] // lax.axis_size("row")

    def partial_value(row_start, row_num):
        return against(source, weight) if transposed else matmul(source, weight)

    return lax.psum_scatter(
        partial_value(jnp.int32(0), row_count * lax.axis_size("row")),
        "row",
        scatter_dimension=0,
        tiled=True,
    )


def feature_totals(first_terms, second_terms):
    return lax.psum((jnp.sum(first_terms, axis=1), jnp.sum(second_terms, axis=1)), "col")


def norm_forward(residual, gain_vec, shift_vec):
    totals = feature_totals(residual, residual * residual)
    mean_rows = totals[0][:, None] / D
    spread = totals[1][:, None] / D - mean_rows * mean_rows
    scale_rows = lax.rsqrt(spread + norm_eps)
    normed = (residual - mean_rows) * scale_rows
    return (normed * gain_vec + shift_vec, normed, scale_rows)


def norm_backward(grad_in, normed, scale_rows, gain_vec):
    scaled = grad_in * gain_vec
    totals = feature_totals(scaled, scaled * normed)
    grad_resid = scale_rows * (scaled - totals[0][:, None] / D - normed * (totals[1][:, None] / D))
    return (grad_resid, jnp.sum(grad_in * normed, axis=0), jnp.sum(grad_in, axis=0))


def gelu_exact(values):
    return jax.nn.gelu(values, approximate=False)


def by_heads(values, head_count):
    seq_count = values.shape[0] // SEQ
    return values.reshape(seq_count, SEQ, head_count, HEAD_DIM)


def attention_forward(queries, key_seq, value_seq):
    block_len = min(512, SEQ)
    outputs = []
    log_parts = []
    for offset in range(0, SEQ, block_len):
        query_block = queries[:, offset : offset + block_len]
        scores = jnp.einsum(
            "nqhd,nkhd->nhqk", query_block, key_seq, preferred_element_type=jnp.float32
        )
        row_max = jnp.max(scores, axis=-1, keepdims=True)
        exp_scores = jnp.exp(scores - row_max)
        denom = jnp.sum(exp_scores, axis=-1, keepdims=True)
        probs_low = (exp_scores / denom).astype(jnp.bfloat16)
        outputs.append(
            jnp.einsum("nhqk,nkhd->nqhd", probs_low, value_seq, preferred_element_type=jnp.float32)
        )
        log_parts.append(row_max + jnp.log(denom))
    attended = jnp.concatenate(outputs, axis=1)
    rows_here = attended.shape[0] * SEQ
    return (
        attended.reshape(rows_here, -1).astype(jnp.bfloat16),
        jnp.concatenate(log_parts, axis=2),
    )


def attention_backward(queries, key_seq, value_seq, grad_seq, log_norm):
    block_len = min(512, SEQ)
    grad_query_parts = []
    grad_key = jnp.zeros(key_seq.shape, jnp.float32)
    grad_value = jnp.zeros(value_seq.shape, jnp.float32)
    for offset in range(0, SEQ, block_len):
        query_block = queries[:, offset : offset + block_len]
        grad_block = grad_seq[:, offset : offset + block_len]
        scores = jnp.einsum(
            "nqhd,nkhd->nhqk", query_block, key_seq, preferred_element_type=jnp.float32
        )
        probs = jnp.exp(scores - log_norm[:, :, offset : offset + block_len])
        grad_probs = jnp.einsum(
            "nqhd,nkhd->nhqk", grad_block, value_seq, preferred_element_type=jnp.float32
        )
        row_delta = jnp.sum(grad_probs * probs, axis=-1, keepdims=True)
        grad_scores = (probs * (grad_probs - row_delta)).astype(jnp.bfloat16)
        grad_query_parts.append(
            jnp.einsum("nhqk,nkhd->nqhd", grad_scores, key_seq, preferred_element_type=jnp.float32)
        )
        grad_key = grad_key + jnp.einsum(
            "nhqk,nqhd->nkhd", grad_scores, query_block, preferred_element_type=jnp.float32
        )
        grad_value = grad_value + jnp.einsum(
            "nhqk,nqhd->nkhd",
            probs.astype(jnp.bfloat16),
            grad_block,
            preferred_element_type=jnp.float32,
        )
    grad_query = jnp.concatenate(grad_query_parts, axis=1)
    rows_here = grad_query.shape[0] * SEQ
    return (
        grad_query.reshape(rows_here, -1).astype(jnp.bfloat16),
        grad_key.reshape(rows_here, -1).astype(jnp.bfloat16),
        grad_value.reshape(rows_here, -1).astype(jnp.bfloat16),
    )


def shards(
    tokens,
    w_qkv,
    b_qv,
    w_out,
    b_out,
    norm1_gain,
    norm1_shift,
    w_up,
    b_up,
    w_down,
    b_down,
    norm2_gain,
    norm2_shift,
    cotangent,
):
    token_major = tokens.T
    width_col = token_major.shape[1]
    width_row = w_out.shape[0]
    qkv_weight = w_qkv.reshape(width_col, 3 * width_row)
    query_scale = HEAD_DIM ** (-0.5)
    head_count = width_row // HEAD_DIM
    gathered_in = by_row(token_major)
    projected = reduce_col(gathered_in, qkv_weight, False).reshape(-1, 3, width_row)
    queries = ((projected[:, 0] + b_qv[0]) * query_scale).astype(jnp.bfloat16)
    key_rows = projected[:, 1].astype(jnp.bfloat16)
    value_rows = (projected[:, 2] + b_qv[1]).astype(jnp.bfloat16)
    query_seq = by_heads(queries, head_count)
    key_seq = by_heads(key_rows, head_count)
    value_seq = by_heads(value_rows, head_count)
    attended, log_norm = attention_forward(query_seq, key_seq, value_seq)
    gathered_att = by_col(attended)
    attn_out = reduce_row(gathered_att, w_out, False) + b_out
    residual1 = token_major.astype(jnp.float32) + attn_out
    normed_a, normed1, scale1 = norm_forward(residual1, norm1_gain, norm1_shift)
    low_a = normed_a.astype(jnp.bfloat16)
    gathered_a = by_row(low_a)
    pre_act = reduce_col(gathered_a, w_up, False) + b_up
    hidden, gelu_pull = jax.vjp(gelu_exact, pre_act)
    hidden_low = hidden.astype(jnp.bfloat16)
    gathered_h = by_col(hidden_low)
    branch_out = reduce_row(gathered_h, w_down, False)
    residual2 = normed_a + branch_out + b_down
    result, normed2, scale2 = norm_forward(residual2, norm2_gain, norm2_shift)
    grad_out = cotangent.T.astype(jnp.float32)
    grad_r2, gain2_part, shift2_part = norm_backward(grad_out, normed2, scale2, norm2_gain)
    down_bias_part = jnp.sum(grad_r2, axis=0)
    grad_branch = grad_r2.astype(jnp.bfloat16)
    gathered_df = by_row(grad_branch)
    down_grad = inner_rows(gathered_h, gathered_df)
    grad_hidden = reduce_col(gathered_df, w_down, True)
    grad_pre = gelu_pull(grad_hidden)[0].astype(jnp.bfloat16)
    gathered_dz = by_col(grad_pre)
    up_grad = inner_rows(gathered_a, gathered_dz)
    up_bias_grad = jnp.sum(gathered_dz, axis=0, dtype=jnp.float32)
    grad_a_ff = reduce_row(gathered_dz, w_up, True)
    grad_a = grad_r2 + grad_a_ff
    grad_r1, gain1_part, shift1_part = norm_backward(grad_a, normed1, scale1, norm1_gain)
    out_bias_part = jnp.sum(grad_r1, axis=0)
    gathered_datt = by_row(grad_r1.astype(jnp.bfloat16))
    out_grad = inner_rows(gathered_att, gathered_datt)
    grad_attended = reduce_col(gathered_datt, w_out, True).astype(jnp.bfloat16)
    grad_seq = by_heads(grad_attended, head_count)
    grad_query, grad_key, grad_value = attention_backward(
        query_seq, key_seq, value_seq, grad_seq, log_norm
    )
    grad_proj = jnp.stack([grad_query * query_scale, grad_key, grad_value], axis=1).reshape(
        -1, 3 * width_row
    )
    gathered_dqkv = by_col(grad_proj)
    qkv_grad = inner_rows(gathered_in, gathered_dqkv).reshape(width_col, 3, width_row)
    bias_rows = jnp.sum(gathered_dqkv, axis=0, dtype=jnp.float32).reshape(3, width_row)
    qv_bias_grad = jnp.stack([bias_rows[0], bias_rows[2]])
    grad_input = reduce_row(gathered_dqkv, qkv_weight, True) + grad_r1
    norm_sums = lax.psum(
        (gain1_part, shift1_part, gain2_part, shift2_part, out_bias_part, down_bias_part),
        ("dp", "row"),
    )
    weight_sums = lax.psum(
        (qkv_grad, qv_bias_grad, out_grad, up_grad, up_bias_grad, down_grad), "dp"
    )
    return (
        result.astype(jnp.bfloat16).T,
        grad_input.T,
        weight_sums[0],
        weight_sums[1],
        weight_sums[2],
        norm_sums[4],
        norm_sums[0],
        norm_sums[1],
        weight_sums[3],
        weight_sums[4],
        weight_sums[5],
        norm_sums[5],
        norm_sums[2],
        norm_sums[3],
    )


BF = jnp.bfloat16
F32 = jnp.float32
PAIR = ((0, 1), (1, 0))
MEBIBYTE = 1024 * 1024
BLOCK = 256


def flip(values, axis_name):
    return lax.ppermute(values, axis_name, PAIR)


def shift(values, axis_name, step):
    size = lax.axis_size(axis_name)
    return lax.ppermute(values, axis_name, [(i, (i + step) % size) for i in range(size)])


def in_order(index, mine, other, axis):
    first = jnp.where(index == 0, mine, other)
    second = jnp.where(index == 0, other, mine)
    return jnp.concatenate([first, second], axis)


def four_in_order(low_bit, high_bit, parts, axis):
    low = [jnp.where(low_bit == 0, parts[i], parts[i ^ 1]) for i in range(4)]
    full = [jnp.where(high_bit == 0, low[i], low[i ^ 2]) for i in range(4)]
    return jnp.concatenate(full, axis)


def cut(values, index, size, axis):
    return lax.dynamic_slice_in_dim(values, index * size, size, axis)


def after(values, *earlier):
    return lax.optimization_barrier((values, earlier))[0]


def part(index, size):
    return pl.ds(pl.multiple_of(index * size, size), size)


def kernel_call(kernel, name, outs, places, *inputs, grid=1, specs=None, out_specs=None, scratch=(), vmem=16, long=False):
    return pl.pallas_call(
        kernel,
        grid_spec=pltpu.PrefetchScalarGridSpec(
            num_scalar_prefetch=1,
            grid=(grid,),
            in_specs=[fixed(x.shape) for x in inputs] if specs is None else specs,
            out_specs=[fixed(shape) for shape, _ in outs] if out_specs is None else out_specs,
            scratch_shapes=list(scratch),
        ),
        out_shape=[jax.ShapeDtypeStruct(shape, dtype) for shape, dtype in outs],
        compiler_params=pltpu.CompilerParams(vmem_limit_bytes=vmem * MEBIBYTE),
        cost_estimate=pl.CostEstimate(
            flops=10**10 if long else 1, bytes_accessed=10**8 if long else 1, transcendentals=0
        ),
        name=name,
    )(places, *inputs)


def fixed(shape):
    return pl.BlockSpec(shape, lambda step, places: (0,) * len(shape))


def stepped(shape, axis):
    return pl.BlockSpec(
        shape, lambda step, places: tuple(step if i == axis else 0 for i in range(len(shape)))
    )


def prepare_attn_kernel(places, w_qkv, b_qv, w_out, *refs):
    vectors, (keep, send, turned) = refs[:-3], refs[-3:]
    head = turned.shape[1] // 4
    for piece in range(3):
        turned[piece] = w_qkv[piece].T
    for ref, quarter in ((keep, places[0]), (send, places[1])):
        for piece in range(3):
            ref[piece * head : (piece + 1) * head] = turned[piece, part(quarter, head), :]
        bias = b_qv[...].astype(F32)
        own = sum(
            jnp.where(quarter == q, bias[:, q * head : (q + 1) * head], 0.0) for q in range(4)
        )
        line = jnp.concatenate([own[0:1], own[1:2]], 1)
        line = jnp.concatenate([line, jnp.zeros((1, keep.shape[1] - 2 * head), F32)], 1)
        rows = [jnp.broadcast_to(line, (8, keep.shape[1]))]
        rows += [vector[...].astype(F32).reshape(1, -1) for vector in vectors]
        rows += [jnp.zeros((2, keep.shape[1]), F32)]
        ref[3 * head : 3 * head + 16] = jnp.concatenate(rows, 0).astype(BF)
        ref[3 * head + 16 :] = w_out[part(quarter, head), :]


def prepare_ff_kernel(places, w_up, w_down, keep, send):
    for ref, quarter in ((keep, places[0]), (send, places[1])):
        ref[:BLOCK] = w_up[:, part(quarter, BLOCK)].T
        ref[BLOCK:] = w_down[part(quarter, BLOCK), :]


def attend_kernel(places, x00, x01, x10, x11, own, far, qkv_ref, out_ref, norm_ref, *weight_refs):
    head_rows = qkv_ref.shape[2]
    total = None
    for side, pair in ((0, (x00, x01)), (1, (x10, x11))):
        mine = (places[3] ^ side) == places[2]
        for end, x in enumerate(pair):
            weight = jnp.where(mine, own[0, end, : 3 * head_rows], far[0, end, : 3 * head_rows])
            weight_refs[2 * side + end][0] = weight
            piece = matmul(weight, x[...])
            total = piece if total is None else total + piece
    bias = own[0, 0, 3 * head_rows : 3 * head_rows + 8].astype(F32)[0:1, : 2 * head_rows]
    bias = jnp.broadcast_to(bias, (2 * head_rows, 2 * head_rows)).T
    query = (total[:head_rows] + bias[:head_rows, 0:1]) * HEAD_DIM**-0.5
    qkv_ref[0, 0] = query.astype(BF)
    key = total[head_rows : 2 * head_rows].astype(BF)
    qkv_ref[0, 1] = key
    value = (total[2 * head_rows :] + bias[head_rows:, 0:1]).astype(BF)
    qkv_ref[0, 2] = value
    key_t = key.T
    for start in range(0, SEQ, BLOCK):
        here = slice(start, start + BLOCK)
        scores = matmul(key_t, qkv_ref[0, 0, :, here])
        top = jnp.max(scores, axis=0, keepdims=True)
        weights = jnp.exp(scores - top)
        denom = jnp.sum(weights, axis=0, keepdims=True)
        out_ref[0, :, here] = matmul(value, weights.astype(BF)) * (1.0 / denom)
        norm_ref[0, :, here] = top + jnp.log(denom)


def turn_kernel(places, *refs):
    for ref, out_ref in zip(refs[:4], refs[4:]):
        out_ref[...] = ref[...].T


def out_far_kernel(places, early, late, own, far, own_ref, send_ref, full_ref, low_ref):
    heads, head_rows, _ = low_ref.shape
    half = far.shape[2]
    low_ref[: early.shape[0]] = early[...].astype(BF)
    low_ref[early.shape[0] :] = late[...].astype(BF)
    for head in range(heads):
        rows = slice(head * head_rows, (head + 1) * head_rows)
        full_ref[rows, part(places[2], half)] = own[head, 8:, :]
        full_ref[rows, part(1 - places[2], half)] = far[head, 8:, :]
    out_block(places, 3, low_ref, full_ref, send_ref)
    out_block(places, 2, low_ref, full_ref, own_ref)


def out_near_kernel(places, attended, full_ref, own_ref, send_ref):
    out_block(places, 1, attended, full_ref, send_ref)
    out_block(places, 0, attended, full_ref, own_ref)


def out_block(places, step, attended, full_ref, out_ref):
    rows = attended[:, :, part(places[0] ^ step, BLOCK)].reshape(-1, BLOCK)
    out_ref[...] = inner_rows(rows, full_ref[...]).astype(out_ref.dtype)


def norm1_kernel(places, near, core, got, x00, x01, x10, x11, vec, a_ref, low_ref, normed_ref, scale_ref):
    for side, pair in ((0, (x00, x01)), (1, (x10, x11))):
        for end, x in enumerate(pair):
            block = 2 * (places[3] ^ side) + (places[4] ^ end)
            a_ref[:, part(block, BLOCK)] = x[...].T.astype(F32)
    residual = a_ref[...] + (near[...] + core[...].astype(F32) + got[...].astype(F32) + vec[0:1])
    mean_rows = jnp.mean(residual, axis=1, keepdims=True)
    spread = jnp.mean(residual * residual, axis=1, keepdims=True) - mean_rows * mean_rows
    scale_rows = lax.rsqrt(spread + norm_eps)
    normed = (residual - mean_rows) * scale_rows
    values = normed * vec[1:2] + vec[2:3]
    a_ref[...] = values
    low_ref[...] = values.astype(BF)
    normed_ref[...] = normed
    scale_ref[...] = scale_rows


def back_of_norm(grad_in, normed, scale_rows, gain_vec):
    scaled = grad_in * gain_vec
    first = jnp.mean(scaled, axis=1, keepdims=True)
    second = jnp.mean(scaled * normed, axis=1, keepdims=True)
    return scale_rows * (scaled - first - normed * second)


def add_sums(sums_ref, *arrays):
    @pl.when(pl.program_id(0) == 0)
    def _():
        sums_ref[...] = jnp.zeros_like(sums_ref)

    for index, values in enumerate(arrays):
        sums_ref[index : index + 1] += jnp.sum(values, axis=0, keepdims=True)


def norm2_kernel(places, near, core, got, a_ref, c0, c1, c2, c3, vec, here_ref, send_ref, grad_ref, low_ref, sums_ref):
    for index, piece in enumerate((c0, c1, c2, c3)):
        block = 2 * (places[3] ^ (index >> 1)) + (places[4] ^ (index & 1))
        grad_ref[:, part(block, BLOCK)] = piece[...].T.astype(F32)
    branch = near[...] + core[...].astype(F32) + got[...].astype(F32) + vec[3:4]
    residual = a_ref[...] + branch
    mean_rows = jnp.mean(residual, axis=1, keepdims=True)
    spread = jnp.mean(residual * residual, axis=1, keepdims=True) - mean_rows * mean_rows
    scale_rows = lax.rsqrt(spread + norm_eps)
    normed = (residual - mean_rows) * scale_rows
    grad_out = grad_ref[...]
    grad = back_of_norm(grad_out, normed, scale_rows, vec[4:5])
    add_sums(sums_ref, grad, grad_out * normed, grad_out)
    grad_ref[...] = normed * vec[4:5] + vec[5:6]
    for side in range(2):
        for end, ref in ((0, here_ref), (1, send_ref)):
            block = 2 * (places[3] ^ side) + (places[4] ^ end)
            ref[side] = grad_ref[:, part(block, BLOCK)].T.astype(BF)
    grad_ref[...] = grad
    low_ref[...] = grad.astype(BF)


def norm1_back_kernel(places, near, core, got, grad2, normed_ref, scale_ref, vec, sums2, low_ref, sums_ref):
    grad_in = grad2[...] + (near[...] + core[...].astype(F32) + got[...].astype(F32))
    normed = normed_ref[...]
    grad = back_of_norm(grad_in, normed, scale_ref[...], vec[1:2])
    add_sums(sums_ref, grad, grad_in * normed, grad_in)
    sums_ref[3:6] = sums2[0:3]
    low_ref[...] = grad.astype(BF)


def weight_grad_kernel(places, left_near, left_far, r0, r1, r2, r3, mine_ref, sent_ref, right):
    half = mine_ref.shape[2]

    @pl.when(pl.program_id(0) == 0)
    def _():
        for index, rows in enumerate((r0, r1, r2, r3)):
            here = slice(index * BLOCK, (index + 1) * BLOCK)
            right[0, here] = rows[:, part(places[2], half)]
            right[1, here] = rows[:, part(1 - places[2], half)]

    left = jnp.concatenate([left_near[...], left_far[...]], 0)
    sent_ref[0, :BLOCK] = inner_rows(left, right[1]).astype(BF)
    mine_ref[0, :BLOCK] = inner_rows(left, right[0]).astype(BF)
    if mine_ref.shape[1] > BLOCK:
        sums = jnp.sum(left.astype(F32), axis=0, keepdims=True)
        sums = jnp.broadcast_to(jnp.concatenate([sums, sums], 1), (8, half)).astype(BF)
        sent_ref[0, BLOCK:] = sums
        mine_ref[0, BLOCK:] = sums


def out_back_kernel(places, d0, d1, d2, d3, full_ref, attended, grad_ref, mine_ref, sent_ref):
    heads, head_rows, _ = attended.shape
    blocks = (d0, d1, d2, d3)
    left = []
    for step, rows in enumerate(blocks):
        here = part(places[0] ^ step, BLOCK)
        grad = against(full_ref[...], rows[...]).astype(BF)
        grad_ref[:, :, here] = grad.reshape(heads, head_rows, BLOCK)
        left.append(attended[:, :, here].reshape(-1, BLOCK))
    width = mine_ref.shape[3]
    for ref, side in ((sent_ref, 1 - places[2]), (mine_ref, places[2])):
        for end in range(2):
            columns = part(2 * side + (places[4] ^ end), width)
            total = None
            for piece, rows in zip(left, blocks):
                product = matmul(piece, rows[:, columns])
                total = product if total is None else total + product
            ref[:, end] = total.astype(BF).reshape(heads, head_rows, width)


def attend_back_kernel(
    places, qkv_ref, grad_ref, norm_ref, attended, out_mine, out_sent, x00, x01, x10, x11, sums, out_ref, mine_ref, sent_ref, probs_low, scores_low
):
    head_rows = qkv_ref.shape[2]
    key = qkv_ref[0, 1]
    key_t = key.T
    value_t = qkv_ref[0, 2].T
    for start in range(0, SEQ, BLOCK):
        here = slice(start, start + BLOCK)
        grad = grad_ref[0, :, here]
        probs = jnp.exp(matmul(key_t, qkv_ref[0, 0, :, here]) - norm_ref[0, :, here])
        delta = jnp.sum(grad.astype(F32) * attended[0, :, here], axis=0, keepdims=True)
        grad_scores = (probs * (matmul(value_t, grad) - delta)).astype(BF)
        probs_low[:, here] = probs.astype(BF)
        scores_low[:, here] = grad_scores
        grad_query = matmul(key, grad_scores).astype(BF)
        out_ref[0, :head_rows, here] = (grad_query.astype(F32) * HEAD_DIM**-0.5).astype(BF)
    grad_key = matmul(scores_low[...], qkv_ref[0, 0].T)
    out_ref[0, head_rows : 2 * head_rows] = grad_key.T.astype(BF)
    grad_value = matmul(probs_low[...], grad_ref[0].T)
    out_ref[0, 2 * head_rows :] = grad_value.T.astype(BF)
    left = out_ref[0]
    bias = jnp.sum(left.astype(F32), axis=1, keepdims=True)
    bias = jnp.concatenate([bias[:head_rows], bias[2 * head_rows :]], 0)
    bias = jnp.broadcast_to(bias, (2 * head_rows, 2 * head_rows)).T[:8]
    bias = jnp.concatenate([bias, jnp.zeros((8, BLOCK - 2 * head_rows), F32)], 1)
    rows = 3 * head_rows
    for side, pair in ((0, (x00, x01)), (1, (x10, x11))):
        mine = (places[3] ^ side) == places[2]
        for end, x in enumerate(pair):
            weight = matmul(left, x[...]).astype(BF)
            block = sums[:, part(2 * (places[3] ^ side) + (places[4] ^ end), BLOCK)]
            extra = jnp.concatenate([block, bias], 0).astype(BF)

            @pl.when(mine)
            def _():
                mine_ref[0, end, :rows] = weight
                mine_ref[0, end, rows : rows + 16] = extra
                mine_ref[0, end, rows + 16 :] = out_mine[0, end]

            @pl.when(jnp.logical_not(mine))
            def _():
                sent_ref[0, end, :rows] = weight
                sent_ref[0, end, rows : rows + 16] = extra
                sent_ref[0, end, rows + 16 :] = out_sent[0, end]


def tail_sum_kernel(places, early_mine, early_got, late_mine, late_got, own_ref, *sums):
    own_ref[...] = early_mine[0].astype(F32) + early_got[0].astype(F32)
    blocks = [(early_mine, early_got, i) for i in range(1, early_mine.shape[0])]
    blocks += [(late_mine, late_got, i) for i in range(late_mine.shape[0])]
    for ref, (mine, got, head) in zip(sums, blocks):
        ref[...] = (mine[head].astype(F32) + got[head].astype(F32)).astype(BF)


def sum_kernel(places, mine, got, own_ref, *sums):
    own_ref[...] = mine[0].astype(F32) + got[0].astype(F32)
    for block, ref in enumerate(sums):
        ref[...] = (mine[block + 1].astype(F32) + got[block + 1].astype(F32)).astype(BF)


def last_ff_kernel(places, *refs):
    here, there = refs[-2:]
    inputs = refs[:-2]
    half = len(inputs) // 2
    first = 0
    for pieces in (inputs[:half], inputs[half:]):
        total = pieces[0][...]
        for ref in pieces[1:]:
            total = total + ref[...].astype(F32)
        rows, width = total.shape[0], total.shape[1] // 2
        left, right = total[:, :width], total[:, width:]
        is_left = places[4] == 0
        here[first : first + rows] = jnp.where(is_left, left, right).astype(BF)
        there[first : first + rows] = jnp.where(is_left, right, left).astype(BF)
        first += rows


def last_sum_kernel(places, own_ref, *refs):
    total = own_ref[...]
    for ref in refs[:-2]:
        total = total + ref[...].astype(F32)
    refs[-2][...] = total[0].astype(BF)
    refs[-1][...] = total[1].astype(BF)


def input_near_kernel(places, own0, own1, send0, send1, grads0, grads1, d0, d1, d2, d3, own_ref, send_ref):
    def product(first, second):
        pairs = ((first, grads0), (second, grads1))
        flat = [[ref[...].reshape(-1, ref.shape[2]) for ref in pair] for pair in pairs]
        return inner_rows(*flat[0]) + inner_rows(*flat[1])

    send_ref[...] = product(send0, send1).astype(BF)
    own_ref[...] = product(own0, own1)
    block = 2 * places[3] + places[4]
    for step, d in enumerate((d0, d1, d2, d3)):
        here = part(places[0] ^ step, BLOCK)
        own_ref[:, here] += d[:, part(block, BLOCK)].T.astype(F32)


def last_ff_out_kernel(places, p0, p1, p2, p3, down_out, up_out, bias_out):
    for step, ref in enumerate((p0, p1, p2, p3)):
        quarter = places[0] ^ step
        down_out[part(quarter, BLOCK), :] = ref[:BLOCK].astype(F32)
        up_out[:, part(quarter, BLOCK)] = ref[BLOCK : 2 * BLOCK].astype(F32).T
        bias_out[:, part(quarter, BLOCK)] = ref[2 * BLOCK :].astype(F32)[0:1]


def last_kernel(places, p0, p1, p2, p3, qkv_out, qv_out, norm_out, out_out, turned):
    parts = (p0, p1, p2, p3)
    head = turned.shape[0] // 4
    for piece in range(3):
        for step, ref in enumerate(parts):
            turned[part(places[0] ^ step, head), :] = ref[piece * head : (piece + 1) * head].astype(F32)
        qkv_out[piece] = turned[...].T
    extra = [ref[3 * head : 3 * head + 16].astype(F32) for ref in parts]
    norm_out[...] = extra[0][:8] + extra[1][:8] + extra[2][:8] + extra[3][:8]
    lines = [[], []]
    for quarter in range(4):
        line = sum(
            jnp.where((places[0] ^ step) == quarter, extra[step][8:9], 0.0) for step in range(4)
        )
        lines[0].append(line[:, :head])
        lines[1].append(line[:, head : 2 * head])
    qv_out[...] = jnp.concatenate([jnp.concatenate(line, 1) for line in lines], 0)
    for step, ref in enumerate(parts):
        out_out[part(places[0] ^ step, head), :] = ref[3 * head + 16 :].astype(F32)


def to_far_chip(own, send):
    return (own + flip(send, "dp").astype(F32)).astype(BF)


def gather_rows(payload):
    size = lax.axis_size("row")
    return [payload] + [shift(payload, "row", step) for step in range(1, size)]


def move_rows(sums):
    return [shift(block, "row", -1 - i) for i, block in enumerate(sums)]


def spread_weights(mine, other):
    return spread_cores(mine, flip(other, "t"))


def spread_cores(mine, got):
    near = jnp.stack([mine, got])
    far = flip(near, "dp")
    return near[0], far[0], near[1], far[1]


def fast_shards(
    tokens,
    w_qkv,
    b_qv,
    w_out,
    b_out,
    norm1_gain,
    norm1_shift,
    w_up,
    b_up,
    w_down,
    b_down,
    norm2_gain,
    norm2_shift,
    cotangent,
):
    core, chip = lax.axis_index("dp"), lax.axis_index("t")
    u_index, row = lax.axis_index("u"), lax.axis_index("row")
    rows = lax.axis_size("row")
    quarter = 2 * chip + core
    other_quarter = 2 * (1 - chip) + core
    places = jnp.stack([quarter, other_quarter, u_index, core, chip, row]).astype(jnp.int32)
    feats = tokens.shape[0]
    width = 4 * feats
    half = 2 * feats
    own_rows = SEQ // 4
    swap_cores = [(2 * d + u, 2 * u + d) for d in range(2) for u in range(2)]
    head_rows = w_out.shape[0] // 4
    qkv_rows, out_rows, ff_rows = 3 * head_rows, head_rows, w_down.shape[0] // 4

    x00 = lax.ppermute(tokens, ("dp", "u"), swap_cores)

    attn_rows = qkv_rows + 16 + out_rows
    attn_keep, attn_send = kernel_call(
        prepare_attn_kernel,
        "prepare_attn",
        [((attn_rows, feats), BF)] * 2,
        places,
        w_qkv.transpose(1, 0, 2),
        b_qv,
        w_out,
        b_out,
        norm1_gain,
        norm1_shift,
        b_down,
        norm2_gain,
        norm2_shift,
        scratch=[pltpu.VMEM((3, 4 * head_rows, feats), BF)],
        vmem=60,
    )
    attn_got = flip(attn_send, "t")
    ff_keep, ff_send = kernel_call(
        prepare_ff_kernel, "prepare_ff", [((2 * ff_rows, feats), BF)] * 2, places, after(w_up, attn_send), w_down, vmem=60
    )
    ff_got = flip(ff_send, "t")
    attn_got = after(attn_got, x00)
    cot = lax.ppermute(after(cotangent, x00), ("dp", "u"), swap_cores)
    x01 = flip(x00, "t")
    x10, x11 = flip(x00, "dp"), flip(x01, "dp")
    cot = after(cot, x01)
    cot_parts = [cut(cot, quarter ^ j, own_rows, 1) for j in range(4)]
    cot_far = flip(jnp.stack([cot_parts[2], cot_parts[3]]), "t")
    cot_near = flip(jnp.stack([cot_parts[1], cot_far[1]]), "dp")

    qkv_part = jnp.stack([attn_keep[: qkv_rows + 8], attn_got[: qkv_rows + 8]])
    ff_got = after(ff_got, qkv_part)
    qkv_own = jnp.stack(gather_rows(qkv_part))
    attn_both = in_order(chip, attn_keep[qkv_rows + 8 :], attn_got[qkv_rows + 8 :], 1)
    ff_both = in_order(chip, ff_keep, ff_got, 1)
    up_bias = lax.dynamic_index_in_dim(b_up.reshape(4, -1), quarter, 0, True)
    up_bias = jnp.pad(up_bias, ((0, 7), (0, half - ff_rows)))
    mixed_part = jnp.concatenate([attn_both, ff_both[:ff_rows], up_bias])
    mixed_pieces = gather_rows(after(mixed_part, qkv_own))
    qkv_far = flip(after(qkv_own, x01), "u")

    x_blocks = (x00, x01, x10, x11)
    pair_of_heads = rows // 2

    def attend(first, far_half):
        def of(shape):
            return pl.BlockSpec(
                shape, lambda step, places: (first + step,) + (0,) * (len(shape) - 1)
            )

        return kernel_call(
            attend_kernel,
            "attend",
            [
                ((pair_of_heads, 3, head_rows, SEQ), BF),
                ((pair_of_heads, head_rows, SEQ), F32),
                ((pair_of_heads, 1, SEQ), F32),
            ]
            + [((pair_of_heads, qkv_rows, feats), BF)] * 4,
            places,
            *x_blocks,
            qkv_own,
            far_half,
            grid=pair_of_heads,
            specs=[fixed((feats, SEQ))] * 4 + [of((1, 2, qkv_rows + 8, feats))] * 2,
            out_specs=[
                stepped((1, 3, head_rows, SEQ), 0),
                stepped((1, head_rows, SEQ), 0),
                stepped((1, 1, SEQ), 0),
            ]
            + [stepped((1, qkv_rows, feats), 0)] * 4,
            vmem=28,
            long=True,
        )

    qkv_early, attended_early, norm_early, *weight_early = attend(0, qkv_far)
    mixed_own = jnp.stack(after(mixed_pieces, norm_early, cot_near))
    down_pieces = gather_rows(after(ff_both[ff_rows:], mixed_own))
    vec_rows = 8 + out_rows
    out_own, up_own = mixed_own[:, :vec_rows], mixed_own[:, vec_rows:]
    out_far = flip(out_own, "u")
    up_far = flip(up_own, "u")
    far_late = after(qkv_far, mixed_own)
    qkv_late, attended_late, norm_late, *weight_late = attend(pair_of_heads, far_late)
    attended_late = after(attended_late, down_pieces[1], down_pieces[3:])
    bias_up = up_own[:, ff_rows, :ff_rows].reshape(1, -1).astype(F32)
    vec = in_order(u_index, out_own[0, :8], out_far[0, :8], 1).astype(F32)
    up_pair = [x[:, :ff_rows].reshape(rows * ff_rows, half) for x in (up_own, up_far)]
    up_full = in_order(u_index, *up_pair, 1)

    row_block = (own_rows, width)
    pair_outs = [(row_block, F32), (row_block, BF)]
    far_own, far_send, out_full, low_attended = kernel_call(
        out_far_kernel,
        "out_far",
        pair_outs + [((rows * head_rows, width), BF), ((rows, head_rows, SEQ), BF)],
        places,
        attended_early,
        attended_late,
        out_own,
        out_far,
    )
    sent = to_far_chip(far_own, far_send)
    near_attended = after(low_attended, sent, up_far, down_pieces)
    got = flip(sent, "t")
    near_own, near_send = kernel_call(
        out_near_kernel, "out_near", pair_outs, places, near_attended, out_full
    )
    down_own = jnp.stack(after(down_pieces, near_own))
    down_far = flip(down_own, "u").reshape(rows * ff_rows, half)
    down_full = in_order(u_index, down_own.reshape(rows * ff_rows, half), down_far, 1)
    near_got = flip(near_send, "dp")
    got = after(got, near_got, up_far, down_own)
    chunk = own_rows // 2
    row_chunk = stepped((chunk, width), 0)
    own_tokens = pl.BlockSpec((feats, chunk), lambda step, places: (0, 2 * places[0] + step))
    normed_a, low_a, normed1, scale1 = kernel_call(
        norm1_kernel,
        "norm1",
        [(row_block, F32), (row_block, BF), (row_block, F32), ((own_rows, 1), F32)],
        places,
        near_own,
        near_got,
        got,
        *x_blocks,
        vec,
        grid=2,
        specs=[row_chunk] * 3 + [own_tokens] * 4 + [fixed((8, width))],
        out_specs=[row_chunk] * 3 + [stepped((chunk, 1), 0)],
    )

    def up(rows_in):
        pre = against(rows_in, up_full) + bias_up
        cdf = 0.5 * (1.0 + lax.erf(pre * (0.5**0.5)))
        slope = cdf + pre * (jnp.exp(-0.5 * pre * pre) * 0.3989422804014327)
        return (pre * cdf).astype(BF), slope

    a0, a1, a2 = low_a, flip(low_a, "dp"), flip(low_a, "t")
    hidden_near, slope_near = up(jnp.concatenate([a0, a1]))
    a2 = after(a2, hidden_near)
    a3 = flip(a2, "dp")
    hidden_far, slope_far = up(jnp.concatenate([a2, a3]))
    far_send = matmul(hidden_far[own_rows:], down_full).astype(BF)
    sent = to_far_chip(matmul(hidden_far[:own_rows], down_full), far_send)
    near_hidden = after(hidden_near, sent)
    token_rows = kernel_call(
        turn_kernel, "turn", [((SEQ, feats), BF)] * 4, places, *after(x_blocks, near_hidden)
    )
    got = flip(sent, "t")
    near_got = flip(matmul(near_hidden[own_rows:], down_full).astype(BF), "dp")
    near_own = matmul(near_hidden[:own_rows], down_full)
    got = after(got, near_got, token_rows)
    turned_chunk = stepped((feats, chunk), 1)
    pair_chunk = stepped((2, feats, chunk), 2)
    result_here, result_send, grad_r2, low_g, sums2 = kernel_call(
        norm2_kernel,
        "norm2",
        [((2, feats, own_rows), BF)] * 2 + [(row_block, F32), (row_block, BF), ((8, width), F32)],
        places,
        near_own,
        near_got,
        got,
        normed_a,
        cot_parts[0],
        cot_far[0],
        cot_near[0],
        cot_near[1],
        vec,
        grid=2,
        specs=[row_chunk] * 4 + [turned_chunk] * 4 + [fixed((8, width))],
        out_specs=[pair_chunk] * 2 + [row_chunk] * 2 + [fixed((8, width))],
    )

    two_blocks = 2 * own_rows

    def weight_grad(near, far, blocks, extra):
        shape = (rows, ff_rows + extra, half)
        return kernel_call(
            weight_grad_kernel,
            "weight_grad",
            [(shape, BF)] * 2,
            places,
            near,
            far,
            *blocks,
            grid=rows,
            specs=[stepped((two_blocks, ff_rows), 1)] * 2 + [fixed(row_block)] * 4,
            out_specs=[stepped((1, *shape[1:]), 0)] * 2,
            scratch=[pltpu.VMEM((2, SEQ, half), BF)],
            long=True,
        )

    g0, g1, g2 = low_g, flip(low_g, "dp"), flip(low_g, "t")
    grad_pre_near = (against(jnp.concatenate([g0, g1]), down_full) * slope_near).astype(BF)
    g2 = after(g2, grad_pre_near)
    g3 = flip(g2, "dp")
    grad_pre_far = (against(jnp.concatenate([g2, g3]), down_full) * slope_far).astype(BF)
    far_send = matmul(grad_pre_far[own_rows:], up_full).astype(BF)
    sent = to_far_chip(matmul(grad_pre_far[:own_rows], up_full), far_send)
    near_pre = after(grad_pre_near, sent)
    got = flip(sent, "t")
    near_got = flip(matmul(near_pre[own_rows:], up_full).astype(BF), "dp")
    near_own = matmul(near_pre[:own_rows], up_full)
    hiddens, pres = after(((hidden_near, hidden_far), (near_pre, grad_pre_far)), near_own)
    down_mine, down_sent = weight_grad(*hiddens, (g0, g1, g2, g3), 0)
    down_got = flip(down_sent, "u")
    up_mine, up_sent = weight_grad(*pres, (a0, a1, a2, a3), 8)
    got = after(got, near_got, up_sent)
    low_r1, sums = kernel_call(
        norm1_back_kernel,
        "norm1_back",
        [(row_block, BF), ((8, width), F32)],
        places,
        near_own,
        near_got,
        got,
        grad_r2,
        normed1,
        scale1,
        vec,
        sums2,
        grid=2,
        specs=[row_chunk] * 5 + [stepped((chunk, 1), 0)] + [fixed((8, width))] * 2,
        out_specs=[row_chunk, fixed((8, width))],
    )

    d0, d1, d2 = low_r1, flip(low_r1, "dp"), flip(low_r1, "t")
    down_got = after(down_got, low_r1)
    up_sent, down_got = lax.optimization_barrier((up_sent, down_got))
    up_got = flip(up_sent, "u")
    d2 = after(d2, down_got)

    def sums_of(mine, got):
        shape = mine.shape[1:]
        return kernel_call(
            sum_kernel, "sum", [(shape, F32)] + [(shape, BF)] * (rows - 1), places, mine, got
        )

    d3 = flip(d2, "dp")
    d_blocks = (d0, d1, d2, d3)
    out_shape = (rows, 2, out_rows, feats)
    grad_att, out_mine, out_sent = kernel_call(
        out_back_kernel,
        "out_back",
        [((rows, head_rows, SEQ), BF)] + [(out_shape, BF)] * 2,
        places,
        *d_blocks,
        out_full,
        low_attended,
    )
    down_total, *down_sums = sums_of(down_mine, after(down_got, grad_att))
    grad_att = after(grad_att, down_sums)
    down_moved = move_rows(down_sums)
    extra_rows = qkv_rows + 16 + out_rows

    def attend_back(first, grad, qkv, log_norm, attended):
        def of(shape):
            return pl.BlockSpec(
                shape, lambda step, places: (first + step,) + (0,) * (len(shape) - 1)
            )

        return kernel_call(
            attend_back_kernel,
            "attend_back",
            [((pair_of_heads, qkv_rows, SEQ), BF)]
            + [((pair_of_heads, 2, extra_rows, feats), BF)] * 2,
            places,
            qkv,
            grad,
            log_norm,
            attended,
            out_mine,
            out_sent,
            *token_rows,
            sums,
            grid=pair_of_heads,
            specs=[
                stepped((1, 3, head_rows, SEQ), 0),
                of((1, head_rows, SEQ)),
                stepped((1, 1, SEQ), 0),
                stepped((1, head_rows, SEQ), 0),
                of((1, 2, out_rows, feats)),
                of((1, 2, out_rows, feats)),
            ]
            + [fixed((SEQ, feats))] * 4
            + [fixed((8, width))],
            out_specs=[stepped((1, qkv_rows, SEQ), 0)]
            + [stepped((1, 2, extra_rows, feats), 0)] * 2,
            scratch=[pltpu.VMEM((SEQ, SEQ), BF)] * 2,
            vmem=30,
            long=True,
        )

    result_far = flip(after(result_send, d3), "t")
    result_near = flip(jnp.stack([result_here[1], result_far[1]]), "dp")
    result_parts = [result_here[0], result_near[0], result_far[0], result_near[1]]

    grads_late, late_mine, late_sent = attend_back(
        pair_of_heads, grad_att, qkv_late, norm_late, attended_late
    )
    late_got = flip(late_sent, "u")
    up_total, *up_sums = sums_of(up_mine, after(up_got, late_sent))
    up_moved = move_rows(up_sums)
    early_att = after(grad_att, up_sums, down_moved, result_near)
    grads_early, early_mine, early_sent = attend_back(
        0, early_att, qkv_early, norm_early, attended_early
    )
    early_got = flip(after(early_sent, up_moved[0], up_moved[2:]), "u")
    sum_shape = (2, extra_rows, feats)
    early_own, *tail_sums = kernel_call(
        tail_sum_kernel,
        "tail_sum",
        [(sum_shape, F32)] + [(sum_shape, BF)] * (rows - 1),
        places,
        early_mine,
        early_got,
        late_mine,
        after(late_got, early_sent, up_moved),
    )
    moved = move_rows(tail_sums)

    def back_to(index, grads_early):
        pairs = ((weight_early[index], grads_early), (weight_late[index], grads_late))
        products = [
            inner_rows(w.reshape(-1, feats), grads.reshape(-1, SEQ)) for w, grads in pairs
        ]
        return products[0] + products[1]

    grads_now = after(grads_early, tail_sums)
    far_send = back_to(3, grads_now).astype(BF)
    sent = to_far_chip(back_to(1, grads_now), far_send)
    got = flip(sent, "t")
    near_own, near_send = kernel_call(
        input_near_kernel,
        "input_near",
        [((feats, SEQ), F32), ((feats, SEQ), BF)],
        places,
        weight_early[0],
        weight_late[0],
        weight_early[2],
        weight_late[2],
        after(grads_early, sent),
        grads_late,
        *d_blocks,
        vmem=24,
    )
    near_got = flip(near_send, "dp")
    result_seq = after(four_in_order(core, chip, result_parts, 1), tail_sums)
    result_out = lax.ppermute(result_seq, ("dp", "u"), swap_cores)
    ff_sums = kernel_call(
        last_ff_kernel,
        "last_ff",
        [((2 * ff_rows + 8, feats), BF)] * 2,
        places,
        after(down_total, near_own, result_out),
        *down_moved,
        up_total,
        *up_moved,
    )
    ff_got = flip(ff_sums[1], "t")
    got = after(got, moved, ff_got)
    grad_in = (near_own + near_got.astype(F32) + got.astype(F32)).astype(BF)
    grad_tokens = lax.ppermute(grad_in, ("dp", "u"), swap_cores)
    last_sums = kernel_call(
        last_sum_kernel,
        "last_sum",
        [(sum_shape[1:], BF)] * 2,
        places,
        after(early_own, grad_in),
        *moved,
    )
    last_got = flip(last_sums[1], "t")
    down_out, up_out, up_bias_out = kernel_call(
        last_ff_out_kernel,
        "last_ff_out",
        [((4 * ff_rows, feats), F32), ((feats, 4 * ff_rows), F32), ((1, 4 * ff_rows), F32)],
        places,
        *spread_cores(after(ff_sums[0], last_got), ff_got),
    )
    last_parts = spread_cores(after(last_sums[0], grad_tokens), last_got)
    grad_tokens = after(grad_tokens, last_parts[2]).astype(F32)
    qkv_out, qv_out, norm_out, out_out = kernel_call(
        last_kernel,
        "last",
        [
            ((3, feats, 4 * head_rows), F32),
            ((2, 4 * head_rows), F32),
            ((8, feats), F32),
            ((4 * out_rows, feats), F32),
        ],
        places,
        *last_parts,
        scratch=[pltpu.VMEM((4 * head_rows, feats), F32)],
    )
    return (
        result_out,
        grad_tokens,
        qkv_out.transpose(1, 0, 2),
        qv_out,
        out_out,
        norm_out[0],
        norm_out[1],
        norm_out[2],
        up_out,
        up_bias_out[0],
        down_out,
        norm_out[3],
        norm_out[4],
        norm_out[5],
    )


def solution(mesh):
    sizes = dict(mesh.shape)
    grouped = sizes["dp"] == 2 and sizes["col"] == 4 and D % (4 * sizes["row"] * HEAD_DIM) == 0
    if grouped:
        devices = mesh.devices.reshape(sizes["dp"], sizes["row"], 2, 2)
        inner_mesh, col, body = Mesh(devices, ("dp", "row", "u", "t")), ("u", "t"), fast_shards
    else:
        inner_mesh, col, body = mesh, "col", shards
    tokens_spec = P(col, ("dp", "row"))
    return jax.shard_map(
        body,
        mesh=inner_mesh,
        in_specs=(
            tokens_spec,
            P(col, None, "row"),
            P(None, "row"),
            P("row", col),
            P(col),
            P(col),
            P(col),
            P(col, "row"),
            P("row"),
            P("row", col),
            P(col),
            P(col),
            P(col),
            tokens_spec,
        ),
        out_specs=(
            tokens_spec,
            tokens_spec,
            P(col, None, "row"),
            P(None, "row"),
            P("row", col),
            P(col),
            P(col),
            P(col),
            P(col, "row"),
            P("row"),
            P("row", col),
            P(col),
            P(col),
            P(col),
        ),
        check_vma=False,
    )
```

```python
import jax
import jax.numpy as jnp
from jax import lax
from jax.experimental import pallas as pl
from jax.experimental.pallas import tpu as pltpu
from jax.sharding import Mesh
from jax.sharding import PartitionSpec as P

D = 1024
HEAD_DIM = 64
SEQ = 1024


norm_eps = 1e-05


def matmul(first_mat, second_mat):
    return jnp.dot(first_mat, second_mat, preferred_element_type=jnp.float32)


def against(first_mat, second_mat):
    return lax.dot_general(
        first_mat, second_mat, (((1,), (1,)), ((), ())), preferred_element_type=jnp.float32
    )


def inner_rows(first_mat, second_mat):
    return lax.dot_general(
        first_mat, second_mat, (((0,), (0,)), ((), ())), preferred_element_type=jnp.float32
    )


def by_row(values):
    return lax.all_gather(values, "row", axis=0, tiled=True)


def by_col(values):
    return lax.all_gather(values, "col", axis=0, tiled=True)


def reduce_col(source, weight, transposed):
    row_count = source.shape[0] // lax.axis_size("col")

    def partial_value(row_start, row_num):
        return against(source, weight) if transposed else matmul(source, weight)

    return lax.psum_scatter(
        partial_value(jnp.int32(0), row_count * lax.axis_size("col")),
        "col",
        scatter_dimension=0,
        tiled=True,
    )


def reduce_row(source, weight, transposed):
    row_count = source.shape[0] // lax.axis_size("row")

    def partial_value(row_start, row_num):
        return against(source, weight) if transposed else matmul(source, weight)

    return lax.psum_scatter(
        partial_value(jnp.int32(0), row_count * lax.axis_size("row")),
        "row",
        scatter_dimension=0,
        tiled=True,
    )


def feature_totals(first_terms, second_terms):
    return lax.psum((jnp.sum(first_terms, axis=1), jnp.sum(second_terms, axis=1)), "col")


def norm_forward(residual, gain_vec, shift_vec):
    totals = feature_totals(residual, residual * residual)
    mean_rows = totals[0][:, None] / D
    spread = totals[1][:, None] / D - mean_rows * mean_rows
    scale_rows = lax.rsqrt(spread + norm_eps)
    normed = (residual - mean_rows) * scale_rows
    return (normed * gain_vec + shift_vec, normed, scale_rows)


def norm_backward(grad_in, normed, scale_rows, gain_vec):
    scaled = grad_in * gain_vec
    totals = feature_totals(scaled, scaled * normed)
    grad_resid = scale_rows * (scaled - totals[0][:, None] / D - normed * (totals[1][:, None] / D))
    return (grad_resid, jnp.sum(grad_in * normed, axis=0), jnp.sum(grad_in, axis=0))


def gelu_exact(values):
    return jax.nn.gelu(values, approximate=False)


def by_heads(values, head_count):
    seq_count = values.shape[0] // SEQ
    return values.reshape(seq_count, SEQ, head_count, HEAD_DIM)


def attention_forward(queries, key_seq, value_seq):
    block_len = min(512, SEQ)
    outputs = []
    log_parts = []
    for offset in range(0, SEQ, block_len):
        query_block = queries[:, offset : offset + block_len]
        scores = jnp.einsum(
            "nqhd,nkhd->nhqk", query_block, key_seq, preferred_element_type=jnp.float32
        )
        row_max = jnp.max(scores, axis=-1, keepdims=True)
        exp_scores = jnp.exp(scores - row_max)
        denom = jnp.sum(exp_scores, axis=-1, keepdims=True)
        probs_low = (exp_scores / denom).astype(jnp.bfloat16)
        outputs.append(
            jnp.einsum("nhqk,nkhd->nqhd", probs_low, value_seq, preferred_element_type=jnp.float32)
        )
        log_parts.append(row_max + jnp.log(denom))
    attended = jnp.concatenate(outputs, axis=1)
    rows_here = attended.shape[0] * SEQ
    return (
        attended.reshape(rows_here, -1).astype(jnp.bfloat16),
        jnp.concatenate(log_parts, axis=2),
    )


def attention_backward(queries, key_seq, value_seq, grad_seq, log_norm):
    block_len = min(512, SEQ)
    grad_query_parts = []
    grad_key = jnp.zeros(key_seq.shape, jnp.float32)
    grad_value = jnp.zeros(value_seq.shape, jnp.float32)
    for offset in range(0, SEQ, block_len):
        query_block = queries[:, offset : offset + block_len]
        grad_block = grad_seq[:, offset : offset + block_len]
        scores = jnp.einsum(
            "nqhd,nkhd->nhqk", query_block, key_seq, preferred_element_type=jnp.float32
        )
        probs = jnp.exp(scores - log_norm[:, :, offset : offset + block_len])
        grad_probs = jnp.einsum(
            "nqhd,nkhd->nhqk", grad_block, value_seq, preferred_element_type=jnp.float32
        )
        row_delta = jnp.sum(grad_probs * probs, axis=-1, keepdims=True)
        grad_scores = (probs * (grad_probs - row_delta)).astype(jnp.bfloat16)
        grad_query_parts.append(
            jnp.einsum("nhqk,nkhd->nqhd", grad_scores, key_seq, preferred_element_type=jnp.float32)
        )
        grad_key = grad_key + jnp.einsum(
            "nhqk,nqhd->nkhd", grad_scores, query_block, preferred_element_type=jnp.float32
        )
        grad_value = grad_value + jnp.einsum(
            "nhqk,nqhd->nkhd",
            probs.astype(jnp.bfloat16),
            grad_block,
            preferred_element_type=jnp.float32,
        )
    grad_query = jnp.concatenate(grad_query_parts, axis=1)
    rows_here = grad_query.shape[0] * SEQ
    return (
        grad_query.reshape(rows_here, -1).astype(jnp.bfloat16),
        grad_key.reshape(rows_here, -1).astype(jnp.bfloat16),
        grad_value.reshape(rows_here, -1).astype(jnp.bfloat16),
    )


def shards(
    tokens,
    w_qkv,
    b_qv,
    w_out,
    b_out,
    norm1_gain,
    norm1_shift,
    w_up,
    b_up,
    w_down,
    b_down,
    norm2_gain,
    norm2_shift,
    cotangent,
):
    token_major = tokens.T
    width_col = token_major.shape[1]
    width_row = w_out.shape[0]
    qkv_weight = w_qkv.reshape(width_col, 3 * width_row)
    query_scale = HEAD_DIM ** (-0.5)
    head_count = width_row // HEAD_DIM
    gathered_in = by_row(token_major)
    projected = reduce_col(gathered_in, qkv_weight, False).reshape(-1, 3, width_row)
    queries = ((projected[:, 0] + b_qv[0]) * query_scale).astype(jnp.bfloat16)
    key_rows = projected[:, 1].astype(jnp.bfloat16)
    value_rows = (projected[:, 2] + b_qv[1]).astype(jnp.bfloat16)
    query_seq = by_heads(queries, head_count)
    key_seq = by_heads(key_rows, head_count)
    value_seq = by_heads(value_rows, head_count)
    attended, log_norm = attention_forward(query_seq, key_seq, value_seq)
    gathered_att = by_col(attended)
    attn_out = reduce_row(gathered_att, w_out, False) + b_out
    residual1 = token_major.astype(jnp.float32) + attn_out
    normed_a, normed1, scale1 = norm_forward(residual1, norm1_gain, norm1_shift)
    low_a = normed_a.astype(jnp.bfloat16)
    gathered_a = by_row(low_a)
    pre_act = reduce_col(gathered_a, w_up, False) + b_up
    hidden, gelu_pull = jax.vjp(gelu_exact, pre_act)
    hidden_low = hidden.astype(jnp.bfloat16)
    gathered_h = by_col(hidden_low)
    branch_out = reduce_row(gathered_h, w_down, False)
    residual2 = normed_a + branch_out + b_down
    result, normed2, scale2 = norm_forward(residual2, norm2_gain, norm2_shift)
    grad_out = cotangent.T.astype(jnp.float32)
    grad_r2, gain2_part, shift2_part = norm_backward(grad_out, normed2, scale2, norm2_gain)
    down_bias_part = jnp.sum(grad_r2, axis=0)
    grad_branch = grad_r2.astype(jnp.bfloat16)
    gathered_df = by_row(grad_branch)
    down_grad = inner_rows(gathered_h, gathered_df)
    grad_hidden = reduce_col(gathered_df, w_down, True)
    grad_pre = gelu_pull(grad_hidden)[0].astype(jnp.bfloat16)
    gathered_dz = by_col(grad_pre)
    up_grad = inner_rows(gathered_a, gathered_dz)
    up_bias_grad = jnp.sum(gathered_dz, axis=0, dtype=jnp.float32)
    grad_a_ff = reduce_row(gathered_dz, w_up, True)
    grad_a = grad_r2 + grad_a_ff
    grad_r1, gain1_part, shift1_part = norm_backward(grad_a, normed1, scale1, norm1_gain)
    out_bias_part = jnp.sum(grad_r1, axis=0)
    gathered_datt = by_row(grad_r1.astype(jnp.bfloat16))
    out_grad = inner_rows(gathered_att, gathered_datt)
    grad_attended = reduce_col(gathered_datt, w_out, True).astype(jnp.bfloat16)
    grad_seq = by_heads(grad_attended, head_count)
    grad_query, grad_key, grad_value = attention_backward(
        query_seq, key_seq, value_seq, grad_seq, log_norm
    )
    grad_proj = jnp.stack([grad_query * query_scale, grad_key, grad_value], axis=1).reshape(
        -1, 3 * width_row
    )
    gathered_dqkv = by_col(grad_proj)
    qkv_grad = inner_rows(gathered_in, gathered_dqkv).reshape(width_col, 3, width_row)
    bias_rows = jnp.sum(gathered_dqkv, axis=0, dtype=jnp.float32).reshape(3, width_row)
    qv_bias_grad = jnp.stack([bias_rows[0], bias_rows[2]])
    grad_input = reduce_row(gathered_dqkv, qkv_weight, True) + grad_r1
    norm_sums = lax.psum(
        (gain1_part, shift1_part, gain2_part, shift2_part, out_bias_part, down_bias_part),
        ("dp", "row"),
    )
    weight_sums = lax.psum(
        (qkv_grad, qv_bias_grad, out_grad, up_grad, up_bias_grad, down_grad), "dp"
    )
    return (
        result.astype(jnp.bfloat16).T,
        grad_input.T,
        weight_sums[0],
        weight_sums[1],
        weight_sums[2],
        norm_sums[4],
        norm_sums[0],
        norm_sums[1],
        weight_sums[3],
        weight_sums[4],
        weight_sums[5],
        norm_sums[5],
        norm_sums[2],
        norm_sums[3],
    )


BF = jnp.bfloat16
F32 = jnp.float32
PAIR = ((0, 1), (1, 0))
MEBIBYTE = 1024 * 1024
BLOCK = 256
QUERIES = 512


def flip(values, axis_name):
    return lax.ppermute(values, axis_name, PAIR)


def shift(values, axis_name, step):
    size = lax.axis_size(axis_name)
    return lax.ppermute(values, axis_name, [(i, (i + step) % size) for i in range(size)])


def in_order(index, mine, other, axis):
    first = jnp.where(index == 0, mine, other)
    second = jnp.where(index == 0, other, mine)
    return jnp.concatenate([first, second], axis)


def four_in_order(low_bit, high_bit, parts, axis):
    low = [jnp.where(low_bit == 0, parts[i], parts[i ^ 1]) for i in range(4)]
    full = [jnp.where(high_bit == 0, low[i], low[i ^ 2]) for i in range(4)]
    return jnp.concatenate(full, axis)


def cut(values, index, size, axis):
    return lax.dynamic_slice_in_dim(values, index * size, size, axis)


def after(values, *earlier):
    return lax.optimization_barrier((values, earlier))[0]


def part(index, size):
    return pl.ds(pl.multiple_of(index * size, size), size)


def kernel_call(kernel, name, outs, places, *inputs, grid=1, specs=None, out_specs=None, scratch=(), vmem=16, long=False):
    return pl.pallas_call(
        kernel,
        grid_spec=pltpu.PrefetchScalarGridSpec(
            num_scalar_prefetch=1,
            grid=(grid,),
            in_specs=[fixed(x.shape) for x in inputs] if specs is None else specs,
            out_specs=[fixed(shape) for shape, _ in outs] if out_specs is None else out_specs,
            scratch_shapes=list(scratch),
        ),
        out_shape=[jax.ShapeDtypeStruct(shape, dtype) for shape, dtype in outs],
        compiler_params=pltpu.CompilerParams(vmem_limit_bytes=vmem * MEBIBYTE),
        cost_estimate=pl.CostEstimate(
            flops=10**10 if long else 1, bytes_accessed=10**8 if long else 1, transcendentals=0
        ),
        name=name,
    )(places, *inputs)


def fixed(shape):
    return pl.BlockSpec(shape, lambda step, places: (0,) * len(shape))


def stepped(shape, axis):
    return pl.BlockSpec(
        shape, lambda step, places: tuple(step if i == axis else 0 for i in range(len(shape)))
    )


def prepare_attn_kernel(places, w_qkv, b_qv, w_out, *refs):
    vectors, (keep, send, turned) = refs[:-3], refs[-3:]
    head = turned.shape[1] // 4
    for piece in range(3):
        turned[piece] = w_qkv[piece].T
    for ref, quarter in ((keep, places[0]), (send, places[1])):
        for piece in range(3):
            ref[piece * head : (piece + 1) * head] = turned[piece, part(quarter, head), :]
        bias = b_qv[...].astype(F32)
        own = sum(
            jnp.where(quarter == q, bias[:, q * head : (q + 1) * head], 0.0) for q in range(4)
        )
        line = jnp.concatenate([own[0:1], own[1:2]], 1)
        line = jnp.concatenate([line, jnp.zeros((1, keep.shape[1] - 2 * head), F32)], 1)
        rows = [jnp.broadcast_to(line, (8, keep.shape[1]))]
        rows += [vector[...].astype(F32).reshape(1, -1) for vector in vectors]
        rows += [jnp.zeros((2, keep.shape[1]), F32)]
        ref[3 * head : 3 * head + 16] = jnp.concatenate(rows, 0).astype(BF)
        ref[3 * head + 16 :] = w_out[part(quarter, head), :]


def prepare_ff_kernel(places, w_up, w_down, keep, send):
    for ref, quarter in ((keep, places[0]), (send, places[1])):
        ref[:BLOCK] = w_up[:, part(quarter, BLOCK)].T
        ref[BLOCK:] = w_down[part(quarter, BLOCK), :]


def attend_kernel(places, x00, x01, x10, x11, own, far, qkv_ref, out_ref, norm_ref, *weight_refs):
    head_rows = qkv_ref.shape[2]
    total = None
    for side, pair in ((0, (x00, x01)), (1, (x10, x11))):
        mine = (places[3] ^ side) == places[2]
        for end, x in enumerate(pair):
            weight = jnp.where(mine, own[0, end, : 3 * head_rows], far[0, end, : 3 * head_rows])
            weight_refs[2 * side + end][0] = weight
            piece = matmul(weight, x[...])
            total = piece if total is None else total + piece
    bias = own[0, 0, 3 * head_rows : 3 * head_rows + 8].astype(F32)[0:1, : 2 * head_rows]
    bias = jnp.broadcast_to(bias, (2 * head_rows, 2 * head_rows)).T
    query = (total[:head_rows] + bias[:head_rows, 0:1]) * HEAD_DIM**-0.5
    qkv_ref[0, 0] = query.astype(BF)
    key = total[head_rows : 2 * head_rows].astype(BF)
    qkv_ref[0, 1] = key
    value = (total[2 * head_rows :] + bias[head_rows:, 0:1]).astype(BF)
    qkv_ref[0, 2] = value
    key_t = key.T
    for start in range(0, SEQ, QUERIES):
        here = slice(start, start + QUERIES)
        scores = matmul(key_t, qkv_ref[0, 0, :, here])
        top = jnp.max(scores, axis=0, keepdims=True)
        weights = jnp.exp(scores - top)
        denom = jnp.sum(weights, axis=0, keepdims=True)
        out_ref[0, :, here] = matmul(value, weights.astype(BF)) * (1.0 / denom)
        norm_ref[0, :, here] = top + jnp.log(denom)


def turn_kernel(places, *refs):
    for ref, out_ref in zip(refs[:4], refs[4:]):
        out_ref[...] = ref[...].T


def out_far_kernel(places, early, late, own, far, own_ref, send_ref, full_ref, low_ref):
    heads, head_rows, _ = low_ref.shape
    half = far.shape[2]
    low_ref[: early.shape[0]] = early[...].astype(BF)
    low_ref[early.shape[0] :] = late[...].astype(BF)
    for head in range(heads):
        rows = slice(head * head_rows, (head + 1) * head_rows)
        full_ref[rows, part(places[2], half)] = own[head, 8:, :]
        full_ref[rows, part(1 - places[2], half)] = far[head, 8:, :]
    out_block(places, 3, low_ref, full_ref, send_ref)
    out_block(places, 2, low_ref, full_ref, own_ref)


def out_near_kernel(places, attended, full_ref, own_ref, send_ref):
    out_block(places, 1, attended, full_ref, send_ref)
    out_block(places, 0, attended, full_ref, own_ref)


def out_block(places, step, attended, full_ref, out_ref):
    rows = attended[:, :, part(places[0] ^ step, BLOCK)].reshape(-1, BLOCK)
    out_ref[...] = inner_rows(rows, full_ref[...]).astype(out_ref.dtype)


def norm1_kernel(places, near, core, got, x00, x01, x10, x11, vec, a_ref, low_ref, normed_ref, scale_ref):
    for side, pair in ((0, (x00, x01)), (1, (x10, x11))):
        for end, x in enumerate(pair):
            block = 2 * (places[3] ^ side) + (places[4] ^ end)
            a_ref[:, part(block, BLOCK)] = x[...].T.astype(F32)
    residual = a_ref[...] + (near[...] + core[...].astype(F32) + got[...].astype(F32) + vec[0:1])
    mean_rows = jnp.mean(residual, axis=1, keepdims=True)
    spread = jnp.mean(residual * residual, axis=1, keepdims=True) - mean_rows * mean_rows
    scale_rows = lax.rsqrt(spread + norm_eps)
    normed = (residual - mean_rows) * scale_rows
    values = normed * vec[1:2] + vec[2:3]
    a_ref[...] = values
    low_ref[...] = values.astype(BF)
    normed_ref[...] = normed
    scale_ref[...] = scale_rows


def back_of_norm(grad_in, normed, scale_rows, gain_vec):
    scaled = grad_in * gain_vec
    first = jnp.mean(scaled, axis=1, keepdims=True)
    second = jnp.mean(scaled * normed, axis=1, keepdims=True)
    return scale_rows * (scaled - first - normed * second)


def add_sums(sums_ref, *arrays):
    @pl.when(pl.program_id(0) == 0)
    def _():
        sums_ref[...] = jnp.zeros_like(sums_ref)

    for index, values in enumerate(arrays):
        sums_ref[index : index + 1] += jnp.sum(values, axis=0, keepdims=True)


def norm2_kernel(places, near, core, got, a_ref, c0, c1, c2, c3, vec, here_ref, send_ref, grad_ref, low_ref, sums_ref):
    for index, piece in enumerate((c0, c1, c2, c3)):
        block = 2 * (places[3] ^ (index >> 1)) + (places[4] ^ (index & 1))
        grad_ref[:, part(block, BLOCK)] = piece[...].T.astype(F32)
    branch = near[...] + core[...].astype(F32) + got[...].astype(F32) + vec[3:4]
    residual = a_ref[...] + branch
    mean_rows = jnp.mean(residual, axis=1, keepdims=True)
    spread = jnp.mean(residual * residual, axis=1, keepdims=True) - mean_rows * mean_rows
    scale_rows = lax.rsqrt(spread + norm_eps)
    normed = (residual - mean_rows) * scale_rows
    grad_out = grad_ref[...]
    grad = back_of_norm(grad_out, normed, scale_rows, vec[4:5])
    add_sums(sums_ref, grad, grad_out * normed, grad_out)
    grad_ref[...] = normed * vec[4:5] + vec[5:6]
    for side in range(2):
        for end, ref in ((0, here_ref), (1, send_ref)):
            block = 2 * (places[3] ^ side) + (places[4] ^ end)
            ref[side] = grad_ref[:, part(block, BLOCK)].T.astype(BF)
    grad_ref[...] = grad
    low_ref[...] = grad.astype(BF)


def norm1_back_kernel(places, near, core, got, grad2, normed_ref, scale_ref, vec, sums2, low_ref, sums_ref):
    grad_in = grad2[...] + (near[...] + core[...].astype(F32) + got[...].astype(F32))
    normed = normed_ref[...]
    grad = back_of_norm(grad_in, normed, scale_ref[...], vec[1:2])
    add_sums(sums_ref, grad, grad_in * normed, grad_in)
    sums_ref[3:6] = sums2[0:3]
    low_ref[...] = grad.astype(BF)


def weight_grad_kernel(places, left_near, left_far, r0, r1, r2, r3, mine_ref, sent_ref, right):
    half = mine_ref.shape[2]

    @pl.when(pl.program_id(0) == 0)
    def _():
        for index, rows in enumerate((r0, r1, r2, r3)):
            here = slice(index * BLOCK, (index + 1) * BLOCK)
            right[0, here] = rows[:, part(places[2], half)]
            right[1, here] = rows[:, part(1 - places[2], half)]

    left = jnp.concatenate([left_near[...], left_far[...]], 0)
    sent_ref[0, :BLOCK] = inner_rows(left, right[1]).astype(BF)
    mine_ref[0, :BLOCK] = inner_rows(left, right[0]).astype(BF)
    if mine_ref.shape[1] > BLOCK:
        sums = jnp.sum(left.astype(F32), axis=0, keepdims=True)
        sums = jnp.broadcast_to(jnp.concatenate([sums, sums], 1), (8, half)).astype(BF)
        sent_ref[0, BLOCK:] = sums
        mine_ref[0, BLOCK:] = sums


def out_back_kernel(places, d0, d1, d2, d3, full_ref, attended, grad_ref, mine_ref, sent_ref):
    heads, head_rows, _ = attended.shape
    blocks = (d0, d1, d2, d3)
    left = []
    for step, rows in enumerate(blocks):
        here = part(places[0] ^ step, BLOCK)
        grad = against(full_ref[...], rows[...]).astype(BF)
        grad_ref[:, :, here] = grad.reshape(heads, head_rows, BLOCK)
        left.append(attended[:, :, here].reshape(-1, BLOCK))
    width = mine_ref.shape[3]
    for ref, side in ((sent_ref, 1 - places[2]), (mine_ref, places[2])):
        for end in range(2):
            columns = part(2 * side + (places[4] ^ end), width)
            total = None
            for piece, rows in zip(left, blocks):
                product = matmul(piece, rows[:, columns])
                total = product if total is None else total + product
            ref[:, end] = total.astype(BF).reshape(heads, head_rows, width)


def attend_back_kernel(
    places, qkv_ref, grad_ref, norm_ref, attended, out_mine, out_sent, x00, x01, x10, x11, sums, out_ref, mine_ref, sent_ref, probs_low, scores_low
):
    head_rows = qkv_ref.shape[2]
    key = qkv_ref[0, 1]
    key_t = key.T
    value_t = qkv_ref[0, 2].T
    for start in range(0, SEQ, BLOCK):
        here = slice(start, start + BLOCK)
        grad = grad_ref[0, :, here]
        probs = jnp.exp(matmul(key_t, qkv_ref[0, 0, :, here]) - norm_ref[0, :, here])
        delta = jnp.sum(grad.astype(F32) * attended[0, :, here], axis=0, keepdims=True)
        grad_scores = (probs * (matmul(value_t, grad) - delta)).astype(BF)
        probs_low[:, here] = probs.astype(BF)
        scores_low[:, here] = grad_scores
        grad_query = matmul(key, grad_scores).astype(BF)
        out_ref[0, :head_rows, here] = (grad_query.astype(F32) * HEAD_DIM**-0.5).astype(BF)
    grad_key = matmul(scores_low[...], qkv_ref[0, 0].T)
    out_ref[0, head_rows : 2 * head_rows] = grad_key.T.astype(BF)
    grad_value = matmul(probs_low[...], grad_ref[0].T)
    out_ref[0, 2 * head_rows :] = grad_value.T.astype(BF)
    left = out_ref[0]
    bias = jnp.sum(left.astype(F32), axis=1, keepdims=True)
    bias = jnp.concatenate([bias[:head_rows], bias[2 * head_rows :]], 0)
    bias = jnp.broadcast_to(bias, (2 * head_rows, 2 * head_rows)).T[:8]
    bias = jnp.concatenate([bias, jnp.zeros((8, BLOCK - 2 * head_rows), F32)], 1)
    rows = 3 * head_rows
    for side, pair in ((0, (x00, x01)), (1, (x10, x11))):
        mine = (places[3] ^ side) == places[2]
        for end, x in enumerate(pair):
            weight = matmul(left, x[...]).astype(BF)
            block = sums[:, part(2 * (places[3] ^ side) + (places[4] ^ end), BLOCK)]
            extra = jnp.concatenate([block, bias], 0).astype(BF)

            @pl.when(mine)
            def _():
                mine_ref[0, end, :rows] = weight
                mine_ref[0, end, rows : rows + 16] = extra
                mine_ref[0, end, rows + 16 :] = out_mine[0, end]

            @pl.when(jnp.logical_not(mine))
            def _():
                sent_ref[0, end, :rows] = weight
                sent_ref[0, end, rows : rows + 16] = extra
                sent_ref[0, end, rows + 16 :] = out_sent[0, end]


def tail_sum_kernel(places, early_mine, early_got, late_mine, late_got, own_ref, *sums):
    own_ref[...] = early_mine[0].astype(F32) + early_got[0].astype(F32)
    blocks = [(early_mine, early_got, i) for i in range(1, early_mine.shape[0])]
    blocks += [(late_mine, late_got, i) for i in range(late_mine.shape[0])]
    for ref, (mine, got, head) in zip(sums, blocks):
        ref[...] = (mine[head].astype(F32) + got[head].astype(F32)).astype(BF)


def sum_kernel(places, mine, got, own_ref, *sums):
    own_ref[...] = mine[0].astype(F32) + got[0].astype(F32)
    for block, ref in enumerate(sums):
        ref[...] = (mine[block + 1].astype(F32) + got[block + 1].astype(F32)).astype(BF)


def last_ff_kernel(places, *refs):
    here, there = refs[-2:]
    inputs = refs[:-2]
    half = len(inputs) // 2
    first = 0
    for pieces in (inputs[:half], inputs[half:]):
        total = pieces[0][...]
        for ref in pieces[1:]:
            total = total + ref[...].astype(F32)
        rows, width = total.shape[0], total.shape[1] // 2
        left, right = total[:, :width], total[:, width:]
        is_left = places[4] == 0
        here[first : first + rows] = jnp.where(is_left, left, right).astype(BF)
        there[first : first + rows] = jnp.where(is_left, right, left).astype(BF)
        first += rows


def last_sum_kernel(places, own_ref, *refs):
    total = own_ref[...]
    for ref in refs[:-2]:
        total = total + ref[...].astype(F32)
    refs[-2][...] = total[0].astype(BF)
    refs[-1][...] = total[1].astype(BF)


def input_near_kernel(places, own0, own1, send0, send1, grads0, grads1, d0, d1, d2, d3, own_ref, send_ref):
    def product(first, second):
        pairs = ((first, grads0), (second, grads1))
        flat = [[ref[...].reshape(-1, ref.shape[2]) for ref in pair] for pair in pairs]
        return inner_rows(*flat[0]) + inner_rows(*flat[1])

    send_ref[...] = product(send0, send1).astype(BF)
    own_ref[...] = product(own0, own1)
    block = 2 * places[3] + places[4]
    for step, d in enumerate((d0, d1, d2, d3)):
        here = part(places[0] ^ step, BLOCK)
        own_ref[:, here] += d[:, part(block, BLOCK)].T.astype(F32)


def last_ff_out_kernel(places, p0, p1, p2, p3, down_out, up_out, bias_out):
    for step, ref in enumerate((p0, p1, p2, p3)):
        quarter = places[0] ^ step
        down_out[part(quarter, BLOCK), :] = ref[:BLOCK].astype(F32)
        up_out[:, part(quarter, BLOCK)] = ref[BLOCK : 2 * BLOCK].astype(F32).T
        bias_out[:, part(quarter, BLOCK)] = ref[2 * BLOCK :].astype(F32)[0:1]


def last_kernel(places, p0, p1, p2, p3, qkv_out, qv_out, norm_out, out_out, turned):
    parts = (p0, p1, p2, p3)
    head = turned.shape[0] // 4
    for piece in range(3):
        for step, ref in enumerate(parts):
            turned[part(places[0] ^ step, head), :] = ref[piece * head : (piece + 1) * head].astype(F32)
        qkv_out[piece] = turned[...].T
    extra = [ref[3 * head : 3 * head + 16].astype(F32) for ref in parts]
    norm_out[...] = extra[0][:8] + extra[1][:8] + extra[2][:8] + extra[3][:8]
    lines = [[], []]
    for quarter in range(4):
        line = sum(
            jnp.where((places[0] ^ step) == quarter, extra[step][8:9], 0.0) for step in range(4)
        )
        lines[0].append(line[:, :head])
        lines[1].append(line[:, head : 2 * head])
    qv_out[...] = jnp.concatenate([jnp.concatenate(line, 1) for line in lines], 0)
    for step, ref in enumerate(parts):
        out_out[part(places[0] ^ step, head), :] = ref[3 * head + 16 :].astype(F32)


def to_far_chip(own, send):
    return (own + flip(send, "dp").astype(F32)).astype(BF)


def gather_rows(payload):
    size = lax.axis_size("row")
    return [payload] + [shift(payload, "row", step) for step in range(1, size)]


def move_rows(sums):
    return [shift(block, "row", -1 - i) for i, block in enumerate(sums)]


def spread_weights(mine, other):
    return spread_cores(mine, flip(other, "t"))


def spread_cores(mine, got):
    near = jnp.stack([mine, got])
    far = flip(near, "dp")
    return near[0], far[0], near[1], far[1]


def fast_shards(
    tokens,
    w_qkv,
    b_qv,
    w_out,
    b_out,
    norm1_gain,
    norm1_shift,
    w_up,
    b_up,
    w_down,
    b_down,
    norm2_gain,
    norm2_shift,
    cotangent,
):
    core, chip = lax.axis_index("dp"), lax.axis_index("t")
    u_index, row = lax.axis_index("u"), lax.axis_index("row")
    rows = lax.axis_size("row")
    quarter = 2 * chip + core
    other_quarter = 2 * (1 - chip) + core
    places = jnp.stack([quarter, other_quarter, u_index, core, chip, row]).astype(jnp.int32)
    feats = tokens.shape[0]
    width = 4 * feats
    half = 2 * feats
    own_rows = SEQ // 4
    swap_cores = [(2 * d + u, 2 * u + d) for d in range(2) for u in range(2)]
    head_rows = w_out.shape[0] // 4
    qkv_rows, out_rows, ff_rows = 3 * head_rows, head_rows, w_down.shape[0] // 4

    x00 = lax.ppermute(tokens, ("dp", "u"), swap_cores)

    attn_rows = qkv_rows + 16 + out_rows
    attn_keep, attn_send = kernel_call(
        prepare_attn_kernel,
        "prepare_attn",
        [((attn_rows, feats), BF)] * 2,
        places,
        w_qkv.transpose(1, 0, 2),
        b_qv,
        w_out,
        b_out,
        norm1_gain,
        norm1_shift,
        b_down,
        norm2_gain,
        norm2_shift,
        scratch=[pltpu.VMEM((3, 4 * head_rows, feats), BF)],
        vmem=60,
    )
    attn_got = flip(attn_send, "t")
    ff_keep, ff_send = kernel_call(
        prepare_ff_kernel, "prepare_ff", [((2 * ff_rows, feats), BF)] * 2, places, after(w_up, attn_send), w_down, vmem=60
    )
    ff_got = flip(ff_send, "t")
    attn_got = after(attn_got, x00)
    x10 = flip(x00, "dp")
    qkv_part = jnp.stack([attn_keep[: qkv_rows + 8], attn_got[: qkv_rows + 8]])
    cot = lax.ppermute(after(cotangent, qkv_part), ("dp", "u"), swap_cores)
    x01 = flip(after(x00, qkv_part), "t")
    x11 = flip(x01, "dp")
    cot = after(cot, x01)
    cot_parts = [cut(cot, quarter ^ j, own_rows, 1) for j in range(4)]
    cot_far = flip(jnp.stack([cot_parts[2], cot_parts[3]]), "t")
    cot_near = flip(jnp.stack([cot_parts[1], cot_far[1]]), "dp")

    ff_got = after(ff_got, qkv_part)
    qkv_own = jnp.stack(gather_rows(qkv_part))
    attn_both = in_order(chip, attn_keep[qkv_rows + 8 :], attn_got[qkv_rows + 8 :], 1)
    ff_both = in_order(chip, ff_keep, ff_got, 1)
    up_bias = lax.dynamic_index_in_dim(b_up.reshape(4, -1), quarter, 0, True)
    up_bias = jnp.pad(up_bias, ((0, 7), (0, half - ff_rows)))
    mixed_part = jnp.concatenate([attn_both, ff_both[:ff_rows], up_bias])
    mixed_pieces = gather_rows(after(mixed_part, qkv_own))
    qkv_far = flip(after(qkv_own, x01), "u")

    x_blocks = (x00, x01, x10, x11)
    pair_of_heads = rows // 2

    def attend(first, far_half):
        def of(shape):
            return pl.BlockSpec(
                shape, lambda step, places: (first + step,) + (0,) * (len(shape) - 1)
            )

        return kernel_call(
            attend_kernel,
            "attend",
            [
                ((pair_of_heads, 3, head_rows, SEQ), BF),
                ((pair_of_heads, head_rows, SEQ), F32),
                ((pair_of_heads, 1, SEQ), F32),
            ]
            + [((pair_of_heads, qkv_rows, feats), BF)] * 4,
            places,
            *x_blocks,
            qkv_own,
            far_half,
            grid=pair_of_heads,
            specs=[fixed((feats, SEQ))] * 4 + [of((1, 2, qkv_rows + 8, feats))] * 2,
            out_specs=[
                stepped((1, 3, head_rows, SEQ), 0),
                stepped((1, head_rows, SEQ), 0),
                stepped((1, 1, SEQ), 0),
            ]
            + [stepped((1, qkv_rows, feats), 0)] * 4,
            vmem=28,
            long=True,
        )

    qkv_early, attended_early, norm_early, *weight_early = attend(0, qkv_far)
    mixed_own = jnp.stack(after(mixed_pieces, norm_early, cot_near))
    down_pieces = gather_rows(after(ff_both[ff_rows:], mixed_own))
    vec_rows = 8 + out_rows
    out_own, up_own = mixed_own[:, :vec_rows], mixed_own[:, vec_rows:]
    out_far = flip(out_own, "u")
    up_far = flip(up_own, "u")
    far_late = after(qkv_far, mixed_own)
    qkv_late, attended_late, norm_late, *weight_late = attend(pair_of_heads, far_late)
    attended_late = after(attended_late, down_pieces[1], down_pieces[3:])
    bias_up = up_own[:, ff_rows, :ff_rows].reshape(1, -1).astype(F32)
    vec = in_order(u_index, out_own[0, :8], out_far[0, :8], 1).astype(F32)
    up_pair = [x[:, :ff_rows].reshape(rows * ff_rows, half) for x in (up_own, up_far)]
    up_full = in_order(u_index, *up_pair, 1)

    row_block = (own_rows, width)
    pair_outs = [(row_block, F32), (row_block, BF)]
    far_own, far_send, out_full, low_attended = kernel_call(
        out_far_kernel,
        "out_far",
        pair_outs + [((rows * head_rows, width), BF), ((rows, head_rows, SEQ), BF)],
        places,
        attended_early,
        attended_late,
        out_own,
        out_far,
    )
    sent = to_far_chip(far_own, far_send)
    near_attended = after(low_attended, sent, up_far, down_pieces)
    got = flip(sent, "t")
    near_own, near_send = kernel_call(
        out_near_kernel, "out_near", pair_outs, places, near_attended, out_full
    )
    down_own = jnp.stack(after(down_pieces, near_own))
    down_far = flip(down_own, "u").reshape(rows * ff_rows, half)
    down_full = in_order(u_index, down_own.reshape(rows * ff_rows, half), down_far, 1)
    near_got = flip(near_send, "dp")
    got = after(got, near_got, up_far, down_own)
    chunk = own_rows // 2
    row_chunk = stepped((chunk, width), 0)
    own_tokens = pl.BlockSpec((feats, chunk), lambda step, places: (0, 2 * places[0] + step))
    normed_a, low_a, normed1, scale1 = kernel_call(
        norm1_kernel,
        "norm1",
        [(row_block, F32), (row_block, BF), (row_block, F32), ((own_rows, 1), F32)],
        places,
        near_own,
        near_got,
        got,
        *x_blocks,
        vec,
        grid=2,
        specs=[row_chunk] * 3 + [own_tokens] * 4 + [fixed((8, width))],
        out_specs=[row_chunk] * 3 + [stepped((chunk, 1), 0)],
    )

    def up(rows_in):
        pre = against(rows_in, up_full) + bias_up
        cdf = 0.5 * (1.0 + lax.erf(pre * (0.5**0.5)))
        slope = cdf + pre * (jnp.exp(-0.5 * pre * pre) * 0.3989422804014327)
        return (pre * cdf).astype(BF), slope

    a0, a1, a2 = low_a, flip(low_a, "dp"), flip(low_a, "t")
    hidden_near, slope_near = up(jnp.concatenate([a0, a1]))
    a2 = after(a2, hidden_near)
    a3 = flip(a2, "dp")
    hidden_far, slope_far = up(jnp.concatenate([a2, a3]))
    far_send = matmul(hidden_far[own_rows:], down_full).astype(BF)
    sent = to_far_chip(matmul(hidden_far[:own_rows], down_full), far_send)
    near_hidden = after(hidden_near, sent)
    token_rows = kernel_call(
        turn_kernel, "turn", [((SEQ, feats), BF)] * 4, places, *after(x_blocks, near_hidden)
    )
    got = flip(sent, "t")
    near_got = flip(matmul(near_hidden[own_rows:], down_full).astype(BF), "dp")
    near_own = matmul(near_hidden[:own_rows], down_full)
    got = after(got, near_got, token_rows)
    turned_chunk = stepped((feats, chunk), 1)
    pair_chunk = stepped((2, feats, chunk), 2)
    result_here, result_send, grad_r2, low_g, sums2 = kernel_call(
        norm2_kernel,
        "norm2",
        [((2, feats, own_rows), BF)] * 2 + [(row_block, F32), (row_block, BF), ((8, width), F32)],
        places,
        near_own,
        near_got,
        got,
        normed_a,
        cot_parts[0],
        cot_far[0],
        cot_near[0],
        cot_near[1],
        vec,
        grid=2,
        specs=[row_chunk] * 4 + [turned_chunk] * 4 + [fixed((8, width))],
        out_specs=[pair_chunk] * 2 + [row_chunk] * 2 + [fixed((8, width))],
    )

    two_blocks = 2 * own_rows

    def weight_grad(near, far, blocks, extra):
        shape = (rows, ff_rows + extra, half)
        return kernel_call(
            weight_grad_kernel,
            "weight_grad",
            [(shape, BF)] * 2,
            places,
            near,
            far,
            *blocks,
            grid=rows,
            specs=[stepped((two_blocks, ff_rows), 1)] * 2 + [fixed(row_block)] * 4,
            out_specs=[stepped((1, *shape[1:]), 0)] * 2,
            scratch=[pltpu.VMEM((2, SEQ, half), BF)],
            long=True,
        )

    g0, g1, g2 = low_g, flip(low_g, "dp"), flip(low_g, "t")
    grad_pre_near = (against(jnp.concatenate([g0, g1]), down_full) * slope_near).astype(BF)
    g2 = after(g2, grad_pre_near)
    g3 = flip(g2, "dp")
    grad_pre_far = (against(jnp.concatenate([g2, g3]), down_full) * slope_far).astype(BF)
    far_send = matmul(grad_pre_far[own_rows:], up_full).astype(BF)
    sent = to_far_chip(matmul(grad_pre_far[:own_rows], up_full), far_send)
    near_pre = after(grad_pre_near, sent)
    got = flip(sent, "t")
    near_got = flip(matmul(near_pre[own_rows:], up_full).astype(BF), "dp")
    near_own = matmul(near_pre[:own_rows], up_full)
    hiddens, pres = after(((hidden_near, hidden_far), (near_pre, grad_pre_far)), near_own)
    down_mine, down_sent = weight_grad(*hiddens, (g0, g1, g2, g3), 0)
    down_got = flip(down_sent, "u")
    up_mine, up_sent = weight_grad(*pres, (a0, a1, a2, a3), 8)
    got = after(got, near_got, up_sent)
    low_r1, sums = kernel_call(
        norm1_back_kernel,
        "norm1_back",
        [(row_block, BF), ((8, width), F32)],
        places,
        near_own,
        near_got,
        got,
        grad_r2,
        normed1,
        scale1,
        vec,
        sums2,
        grid=2,
        specs=[row_chunk] * 5 + [stepped((chunk, 1), 0)] + [fixed((8, width))] * 2,
        out_specs=[row_chunk, fixed((8, width))],
    )

    d0, d1, d2 = low_r1, flip(low_r1, "dp"), flip(low_r1, "t")
    down_got = after(down_got, low_r1)
    up_sent, down_got = lax.optimization_barrier((up_sent, down_got))
    up_got = flip(up_sent, "u")
    d2 = after(d2, down_got)

    def sums_of(mine, got):
        shape = mine.shape[1:]
        return kernel_call(
            sum_kernel, "sum", [(shape, F32)] + [(shape, BF)] * (rows - 1), places, mine, got
        )

    d3 = flip(d2, "dp")
    d_blocks = (d0, d1, d2, d3)
    out_shape = (rows, 2, out_rows, feats)
    grad_att, out_mine, out_sent = kernel_call(
        out_back_kernel,
        "out_back",
        [((rows, head_rows, SEQ), BF)] + [(out_shape, BF)] * 2,
        places,
        *d_blocks,
        out_full,
        low_attended,
    )
    down_total, *down_sums = sums_of(down_mine, after(down_got, grad_att))
    grad_att = after(grad_att, down_sums)
    down_moved = move_rows(down_sums)
    extra_rows = qkv_rows + 16 + out_rows

    def attend_back(first, grad, qkv, log_norm, attended):
        def of(shape):
            return pl.BlockSpec(
                shape, lambda step, places: (first + step,) + (0,) * (len(shape) - 1)
            )

        return kernel_call(
            attend_back_kernel,
            "attend_back",
            [((pair_of_heads, qkv_rows, SEQ), BF)]
            + [((pair_of_heads, 2, extra_rows, feats), BF)] * 2,
            places,
            qkv,
            grad,
            log_norm,
            attended,
            out_mine,
            out_sent,
            *token_rows,
            sums,
            grid=pair_of_heads,
            specs=[
                stepped((1, 3, head_rows, SEQ), 0),
                of((1, head_rows, SEQ)),
                stepped((1, 1, SEQ), 0),
                stepped((1, head_rows, SEQ), 0),
                of((1, 2, out_rows, feats)),
                of((1, 2, out_rows, feats)),
            ]
            + [fixed((SEQ, feats))] * 4
            + [fixed((8, width))],
            out_specs=[stepped((1, qkv_rows, SEQ), 0)]
            + [stepped((1, 2, extra_rows, feats), 0)] * 2,
            scratch=[pltpu.VMEM((SEQ, SEQ), BF)] * 2,
            vmem=30,
            long=True,
        )

    result_far = flip(after(result_send, d3), "t")
    result_near = flip(jnp.stack([result_here[1], result_far[1]]), "dp")
    result_parts = [result_here[0], result_near[0], result_far[0], result_near[1]]

    grads_late, late_mine, late_sent = attend_back(
        pair_of_heads, grad_att, qkv_late, norm_late, attended_late
    )
    late_got = flip(late_sent, "u")
    up_total, *up_sums = sums_of(up_mine, after(up_got, late_sent))
    up_moved = move_rows(up_sums)
    early_att = after(grad_att, up_sums, down_moved, result_near)
    grads_early, early_mine, early_sent = attend_back(
        0, early_att, qkv_early, norm_early, attended_early
    )
    early_got = flip(after(early_sent, up_moved[0], up_moved[2:]), "u")
    sum_shape = (2, extra_rows, feats)
    early_own, *tail_sums = kernel_call(
        tail_sum_kernel,
        "tail_sum",
        [(sum_shape, F32)] + [(sum_shape, BF)] * (rows - 1),
        places,
        early_mine,
        early_got,
        late_mine,
        after(late_got, early_sent, up_moved),
    )
    moved = move_rows(tail_sums)

    def back_to(index, grads_early):
        pairs = ((weight_early[index], grads_early), (weight_late[index], grads_late))
        products = [
            inner_rows(w.reshape(-1, feats), grads.reshape(-1, SEQ)) for w, grads in pairs
        ]
        return products[0] + products[1]

    grads_now = after(grads_early, tail_sums)
    far_send = back_to(3, grads_now).astype(BF)
    sent = to_far_chip(back_to(1, grads_now), far_send)
    got = flip(sent, "t")
    near_own, near_send = kernel_call(
        input_near_kernel,
        "input_near",
        [((feats, SEQ), F32), ((feats, SEQ), BF)],
        places,
        weight_early[0],
        weight_late[0],
        weight_early[2],
        weight_late[2],
        after(grads_early, sent),
        grads_late,
        *d_blocks,
        vmem=24,
    )
    near_got = flip(near_send, "dp")
    result_seq = after(four_in_order(core, chip, result_parts, 1), tail_sums)
    result_out = lax.ppermute(result_seq, ("dp", "u"), swap_cores)
    ff_sums = kernel_call(
        last_ff_kernel,
        "last_ff",
        [((2 * ff_rows + 8, feats), BF)] * 2,
        places,
        after(down_total, near_own, result_out),
        *down_moved,
        up_total,
        *up_moved,
    )
    ff_got = flip(ff_sums[1], "t")
    got = after(got, moved, ff_got)
    grad_in = (near_own + near_got.astype(F32) + got.astype(F32)).astype(BF)
    grad_tokens = lax.ppermute(grad_in, ("dp", "u"), swap_cores)
    last_sums = kernel_call(
        last_sum_kernel,
        "last_sum",
        [(sum_shape[1:], BF)] * 2,
        places,
        after(early_own, grad_in),
        *moved,
    )
    last_got = flip(last_sums[1], "t")
    down_out, up_out, up_bias_out = kernel_call(
        last_ff_out_kernel,
        "last_ff_out",
        [((4 * ff_rows, feats), F32), ((feats, 4 * ff_rows), F32), ((1, 4 * ff_rows), F32)],
        places,
        *spread_cores(after(ff_sums[0], last_got), ff_got),
    )
    last_parts = spread_cores(after(last_sums[0], grad_tokens), last_got)
    grad_tokens = after(grad_tokens, last_parts[2]).astype(F32)
    qkv_out, qv_out, norm_out, out_out = kernel_call(
        last_kernel,
        "last",
        [
            ((3, feats, 4 * head_rows), F32),
            ((2, 4 * head_rows), F32),
            ((8, feats), F32),
            ((4 * out_rows, feats), F32),
        ],
        places,
        *last_parts,
        scratch=[pltpu.VMEM((4 * head_rows, feats), F32)],
    )
    return (
        result_out,
        grad_tokens,
        qkv_out.transpose(1, 0, 2),
        qv_out,
        out_out,
        norm_out[0],
        norm_out[1],
        norm_out[2],
        up_out,
        up_bias_out[0],
        down_out,
        norm_out[3],
        norm_out[4],
        norm_out[5],
    )


def solution(mesh):
    sizes = dict(mesh.shape)
    grouped = sizes["dp"] == 2 and sizes["col"] == 4 and D % (4 * sizes["row"] * HEAD_DIM) == 0
    if grouped:
        devices = mesh.devices.reshape(sizes["dp"], sizes["row"], 2, 2)
        inner_mesh, col, body = Mesh(devices, ("dp", "row", "u", "t")), ("u", "t"), fast_shards
    else:
        inner_mesh, col, body = mesh, "col", shards
    tokens_spec = P(col, ("dp", "row"))
    return jax.shard_map(
        body,
        mesh=inner_mesh,
        in_specs=(
            tokens_spec,
            P(col, None, "row"),
            P(None, "row"),
            P("row", col),
            P(col),
            P(col),
            P(col),
            P(col, "row"),
            P("row"),
            P("row", col),
            P(col),
            P(col),
            P(col),
            tokens_spec,
        ),
        out_specs=(
            tokens_spec,
            tokens_spec,
            P(col, None, "row"),
            P(None, "row"),
            P("row", col),
            P(col),
            P(col),
            P(col),
            P(col, "row"),
            P("row"),
            P("row", col),
            P(col),
            P(col),
            P(col),
        ),
        check_vma=False,
    )
```

```python
import jax
import jax.numpy as jnp
from jax import lax
from jax.experimental import pallas as pl
from jax.experimental.pallas import tpu as pltpu
from jax.sharding import Mesh
from jax.sharding import PartitionSpec as P

D = 1024
HEAD_DIM = 64
SEQ = 1024


norm_eps = 1e-05


def matmul(first_mat, second_mat):
    return jnp.dot(first_mat, second_mat, preferred_element_type=jnp.float32)


def against(first_mat, second_mat):
    return lax.dot_general(
        first_mat, second_mat, (((1,), (1,)), ((), ())), preferred_element_type=jnp.float32
    )


def inner_rows(first_mat, second_mat):
    return lax.dot_general(
        first_mat, second_mat, (((0,), (0,)), ((), ())), preferred_element_type=jnp.float32
    )


def by_row(values):
    return lax.all_gather(values, "row", axis=0, tiled=True)


def by_col(values):
    return lax.all_gather(values, "col", axis=0, tiled=True)


def reduce_col(source, weight, transposed):
    row_count = source.shape[0] // lax.axis_size("col")

    def partial_value(row_start, row_num):
        return against(source, weight) if transposed else matmul(source, weight)

    return lax.psum_scatter(
        partial_value(jnp.int32(0), row_count * lax.axis_size("col")),
        "col",
        scatter_dimension=0,
        tiled=True,
    )


def reduce_row(source, weight, transposed):
    row_count = source.shape[0] // lax.axis_size("row")

    def partial_value(row_start, row_num):
        return against(source, weight) if transposed else matmul(source, weight)

    return lax.psum_scatter(
        partial_value(jnp.int32(0), row_count * lax.axis_size("row")),
        "row",
        scatter_dimension=0,
        tiled=True,
    )


def feature_totals(first_terms, second_terms):
    return lax.psum((jnp.sum(first_terms, axis=1), jnp.sum(second_terms, axis=1)), "col")


def norm_forward(residual, gain_vec, shift_vec):
    totals = feature_totals(residual, residual * residual)
    mean_rows = totals[0][:, None] / D
    spread = totals[1][:, None] / D - mean_rows * mean_rows
    scale_rows = lax.rsqrt(spread + norm_eps)
    normed = (residual - mean_rows) * scale_rows
    return (normed * gain_vec + shift_vec, normed, scale_rows)


def norm_backward(grad_in, normed, scale_rows, gain_vec):
    scaled = grad_in * gain_vec
    totals = feature_totals(scaled, scaled * normed)
    grad_resid = scale_rows * (scaled - totals[0][:, None] / D - normed * (totals[1][:, None] / D))
    return (grad_resid, jnp.sum(grad_in * normed, axis=0), jnp.sum(grad_in, axis=0))


def gelu_exact(values):
    return jax.nn.gelu(values, approximate=False)


def by_heads(values, head_count):
    seq_count = values.shape[0] // SEQ
    return values.reshape(seq_count, SEQ, head_count, HEAD_DIM)


def attention_forward(queries, key_seq, value_seq):
    block_len = min(512, SEQ)
    outputs = []
    log_parts = []
    for offset in range(0, SEQ, block_len):
        query_block = queries[:, offset : offset + block_len]
        scores = jnp.einsum(
            "nqhd,nkhd->nhqk", query_block, key_seq, preferred_element_type=jnp.float32
        )
        row_max = jnp.max(scores, axis=-1, keepdims=True)
        exp_scores = jnp.exp(scores - row_max)
        denom = jnp.sum(exp_scores, axis=-1, keepdims=True)
        probs_low = (exp_scores / denom).astype(jnp.bfloat16)
        outputs.append(
            jnp.einsum("nhqk,nkhd->nqhd", probs_low, value_seq, preferred_element_type=jnp.float32)
        )
        log_parts.append(row_max + jnp.log(denom))
    attended = jnp.concatenate(outputs, axis=1)
    rows_here = attended.shape[0] * SEQ
    return (
        attended.reshape(rows_here, -1).astype(jnp.bfloat16),
        jnp.concatenate(log_parts, axis=2),
    )


def attention_backward(queries, key_seq, value_seq, grad_seq, log_norm):
    block_len = min(512, SEQ)
    grad_query_parts = []
    grad_key = jnp.zeros(key_seq.shape, jnp.float32)
    grad_value = jnp.zeros(value_seq.shape, jnp.float32)
    for offset in range(0, SEQ, block_len):
        query_block = queries[:, offset : offset + block_len]
        grad_block = grad_seq[:, offset : offset + block_len]
        scores = jnp.einsum(
            "nqhd,nkhd->nhqk", query_block, key_seq, preferred_element_type=jnp.float32
        )
        probs = jnp.exp(scores - log_norm[:, :, offset : offset + block_len])
        grad_probs = jnp.einsum(
            "nqhd,nkhd->nhqk", grad_block, value_seq, preferred_element_type=jnp.float32
        )
        row_delta = jnp.sum(grad_probs * probs, axis=-1, keepdims=True)
        grad_scores = (probs * (grad_probs - row_delta)).astype(jnp.bfloat16)
        grad_query_parts.append(
            jnp.einsum("nhqk,nkhd->nqhd", grad_scores, key_seq, preferred_element_type=jnp.float32)
        )
        grad_key = grad_key + jnp.einsum(
            "nhqk,nqhd->nkhd", grad_scores, query_block, preferred_element_type=jnp.float32
        )
        grad_value = grad_value + jnp.einsum(
            "nhqk,nqhd->nkhd",
            probs.astype(jnp.bfloat16),
            grad_block,
            preferred_element_type=jnp.float32,
        )
    grad_query = jnp.concatenate(grad_query_parts, axis=1)
    rows_here = grad_query.shape[0] * SEQ
    return (
        grad_query.reshape(rows_here, -1).astype(jnp.bfloat16),
        grad_key.reshape(rows_here, -1).astype(jnp.bfloat16),
        grad_value.reshape(rows_here, -1).astype(jnp.bfloat16),
    )


def shards(
    tokens,
    w_qkv,
    b_qv,
    w_out,
    b_out,
    norm1_gain,
    norm1_shift,
    w_up,
    b_up,
    w_down,
    b_down,
    norm2_gain,
    norm2_shift,
    cotangent,
):
    token_major = tokens.T
    width_col = token_major.shape[1]
    width_row = w_out.shape[0]
    qkv_weight = w_qkv.reshape(width_col, 3 * width_row)
    query_scale = HEAD_DIM ** (-0.5)
    head_count = width_row // HEAD_DIM
    gathered_in = by_row(token_major)
    projected = reduce_col(gathered_in, qkv_weight, False).reshape(-1, 3, width_row)
    queries = ((projected[:, 0] + b_qv[0]) * query_scale).astype(jnp.bfloat16)
    key_rows = projected[:, 1].astype(jnp.bfloat16)
    value_rows = (projected[:, 2] + b_qv[1]).astype(jnp.bfloat16)
    query_seq = by_heads(queries, head_count)
    key_seq = by_heads(key_rows, head_count)
    value_seq = by_heads(value_rows, head_count)
    attended, log_norm = attention_forward(query_seq, key_seq, value_seq)
    gathered_att = by_col(attended)
    attn_out = reduce_row(gathered_att, w_out, False) + b_out
    residual1 = token_major.astype(jnp.float32) + attn_out
    normed_a, normed1, scale1 = norm_forward(residual1, norm1_gain, norm1_shift)
    low_a = normed_a.astype(jnp.bfloat16)
    gathered_a = by_row(low_a)
    pre_act = reduce_col(gathered_a, w_up, False) + b_up
    hidden, gelu_pull = jax.vjp(gelu_exact, pre_act)
    hidden_low = hidden.astype(jnp.bfloat16)
    gathered_h = by_col(hidden_low)
    branch_out = reduce_row(gathered_h, w_down, False)
    residual2 = normed_a + branch_out + b_down
    result, normed2, scale2 = norm_forward(residual2, norm2_gain, norm2_shift)
    grad_out = cotangent.T.astype(jnp.float32)
    grad_r2, gain2_part, shift2_part = norm_backward(grad_out, normed2, scale2, norm2_gain)
    down_bias_part = jnp.sum(grad_r2, axis=0)
    grad_branch = grad_r2.astype(jnp.bfloat16)
    gathered_df = by_row(grad_branch)
    down_grad = inner_rows(gathered_h, gathered_df)
    grad_hidden = reduce_col(gathered_df, w_down, True)
    grad_pre = gelu_pull(grad_hidden)[0].astype(jnp.bfloat16)
    gathered_dz = by_col(grad_pre)
    up_grad = inner_rows(gathered_a, gathered_dz)
    up_bias_grad = jnp.sum(gathered_dz, axis=0, dtype=jnp.float32)
    grad_a_ff = reduce_row(gathered_dz, w_up, True)
    grad_a = grad_r2 + grad_a_ff
    grad_r1, gain1_part, shift1_part = norm_backward(grad_a, normed1, scale1, norm1_gain)
    out_bias_part = jnp.sum(grad_r1, axis=0)
    gathered_datt = by_row(grad_r1.astype(jnp.bfloat16))
    out_grad = inner_rows(gathered_att, gathered_datt)
    grad_attended = reduce_col(gathered_datt, w_out, True).astype(jnp.bfloat16)
    grad_seq = by_heads(grad_attended, head_count)
    grad_query, grad_key, grad_value = attention_backward(
        query_seq, key_seq, value_seq, grad_seq, log_norm
    )
    grad_proj = jnp.stack([grad_query * query_scale, grad_key, grad_value], axis=1).reshape(
        -1, 3 * width_row
    )
    gathered_dqkv = by_col(grad_proj)
    qkv_grad = inner_rows(gathered_in, gathered_dqkv).reshape(width_col, 3, width_row)
    bias_rows = jnp.sum(gathered_dqkv, axis=0, dtype=jnp.float32).reshape(3, width_row)
    qv_bias_grad = jnp.stack([bias_rows[0], bias_rows[2]])
    grad_input = reduce_row(gathered_dqkv, qkv_weight, True) + grad_r1
    norm_sums = lax.psum(
        (gain1_part, shift1_part, gain2_part, shift2_part, out_bias_part, down_bias_part),
        ("dp", "row"),
    )
    weight_sums = lax.psum(
        (qkv_grad, qv_bias_grad, out_grad, up_grad, up_bias_grad, down_grad), "dp"
    )
    return (
        result.astype(jnp.bfloat16).T,
        grad_input.T,
        weight_sums[0],
        weight_sums[1],
        weight_sums[2],
        norm_sums[4],
        norm_sums[0],
        norm_sums[1],
        weight_sums[3],
        weight_sums[4],
        weight_sums[5],
        norm_sums[5],
        norm_sums[2],
        norm_sums[3],
    )


BF = jnp.bfloat16
F32 = jnp.float32
PAIR = ((0, 1), (1, 0))
MEBIBYTE = 1024 * 1024
BLOCK = 256
QUERIES = 1024


def flip(values, axis_name):
    return lax.ppermute(values, axis_name, PAIR)


def shift(values, axis_name, step):
    size = lax.axis_size(axis_name)
    return lax.ppermute(values, axis_name, [(i, (i + step) % size) for i in range(size)])


def in_order(index, mine, other, axis):
    first = jnp.where(index == 0, mine, other)
    second = jnp.where(index == 0, other, mine)
    return jnp.concatenate([first, second], axis)


def four_in_order(low_bit, high_bit, parts, axis):
    low = [jnp.where(low_bit == 0, parts[i], parts[i ^ 1]) for i in range(4)]
    full = [jnp.where(high_bit == 0, low[i], low[i ^ 2]) for i in range(4)]
    return jnp.concatenate(full, axis)


def cut(values, index, size, axis):
    return lax.dynamic_slice_in_dim(values, index * size, size, axis)


def after(values, *earlier):
    return lax.optimization_barrier((values, earlier))[0]


def part(index, size):
    return pl.ds(pl.multiple_of(index * size, size), size)


def kernel_call(kernel, name, outs, places, *inputs, grid=1, specs=None, out_specs=None, scratch=(), vmem=16, long=False):
    return pl.pallas_call(
        kernel,
        grid_spec=pltpu.PrefetchScalarGridSpec(
            num_scalar_prefetch=1,
            grid=(grid,),
            in_specs=[fixed(x.shape) for x in inputs] if specs is None else specs,
            out_specs=[fixed(shape) for shape, _ in outs] if out_specs is None else out_specs,
            scratch_shapes=list(scratch),
        ),
        out_shape=[jax.ShapeDtypeStruct(shape, dtype) for shape, dtype in outs],
        compiler_params=pltpu.CompilerParams(vmem_limit_bytes=vmem * MEBIBYTE),
        cost_estimate=pl.CostEstimate(
            flops=10**10 if long else 1, bytes_accessed=10**8 if long else 1, transcendentals=0
        ),
        name=name,
    )(places, *inputs)


def fixed(shape):
    return pl.BlockSpec(shape, lambda step, places: (0,) * len(shape))


def stepped(shape, axis):
    return pl.BlockSpec(
        shape, lambda step, places: tuple(step if i == axis else 0 for i in range(len(shape)))
    )


def prepare_attn_kernel(places, w_qkv, b_qv, w_out, *refs):
    vectors, (keep, send, turned) = refs[:-3], refs[-3:]
    head = turned.shape[1] // 4
    for piece in range(3):
        turned[piece] = w_qkv[piece].T
    for ref, quarter in ((keep, places[0]), (send, places[1])):
        for piece in range(3):
            ref[piece * head : (piece + 1) * head] = turned[piece, part(quarter, head), :]
        bias = b_qv[...].astype(F32)
        own = sum(
            jnp.where(quarter == q, bias[:, q * head : (q + 1) * head], 0.0) for q in range(4)
        )
        line = jnp.concatenate([own[0:1], own[1:2]], 1)
        line = jnp.concatenate([line, jnp.zeros((1, keep.shape[1] - 2 * head), F32)], 1)
        rows = [jnp.broadcast_to(line, (8, keep.shape[1]))]
        rows += [vector[...].astype(F32).reshape(1, -1) for vector in vectors]
        rows += [jnp.zeros((2, keep.shape[1]), F32)]
        ref[3 * head : 3 * head + 16] = jnp.concatenate(rows, 0).astype(BF)
        ref[3 * head + 16 :] = w_out[part(quarter, head), :]


def prepare_ff_kernel(places, w_up, w_down, keep, send):
    for ref, quarter in ((keep, places[0]), (send, places[1])):
        ref[:BLOCK] = w_up[:, part(quarter, BLOCK)].T
        ref[BLOCK:] = w_down[part(quarter, BLOCK), :]


def attend_kernel(places, x00, x01, x10, x11, own, far, qkv_ref, out_ref, norm_ref, *weight_refs):
    head_rows = qkv_ref.shape[2]
    total = None
    for side, pair in ((0, (x00, x01)), (1, (x10, x11))):
        mine = (places[3] ^ side) == places[2]
        for end, x in enumerate(pair):
            weight = jnp.where(mine, own[0, end, : 3 * head_rows], far[0, end, : 3 * head_rows])
            weight_refs[2 * side + end][0] = weight
            piece = matmul(weight, x[...])
            total = piece if total is None else total + piece
    bias = own[0, 0, 3 * head_rows : 3 * head_rows + 8].astype(F32)[0:1, : 2 * head_rows]
    bias = jnp.broadcast_to(bias, (2 * head_rows, 2 * head_rows)).T
    query = (total[:head_rows] + bias[:head_rows, 0:1]) * HEAD_DIM**-0.5
    qkv_ref[0, 0] = query.astype(BF)
    key = total[head_rows : 2 * head_rows].astype(BF)
    qkv_ref[0, 1] = key
    value = (total[2 * head_rows :] + bias[head_rows:, 0:1]).astype(BF)
    qkv_ref[0, 2] = value
    key_t = key.T
    for start in range(0, SEQ, QUERIES):
        here = slice(start, start + QUERIES)
        scores = matmul(key_t, qkv_ref[0, 0, :, here])
        top = jnp.max(scores, axis=0, keepdims=True)
        weights = jnp.exp(scores - top)
        denom = jnp.sum(weights, axis=0, keepdims=True)
        out_ref[0, :, here] = matmul(value, weights.astype(BF)) * (1.0 / denom)
        norm_ref[0, :, here] = top + jnp.log(denom)


def turn_kernel(places, *refs):
    for ref, out_ref in zip(refs[:4], refs[4:]):
        out_ref[...] = ref[...].T


def out_far_kernel(places, early, late, own, far, own_ref, send_ref, full_ref, low_ref):
    heads, head_rows, _ = low_ref.shape
    half = far.shape[2]
    low_ref[: early.shape[0]] = early[...].astype(BF)
    low_ref[early.shape[0] :] = late[...].astype(BF)
    for head in range(heads):
        rows = slice(head * head_rows, (head + 1) * head_rows)
        full_ref[rows, part(places[2], half)] = own[head, 8:, :]
        full_ref[rows, part(1 - places[2], half)] = far[head, 8:, :]
    out_block(places, 3, low_ref, full_ref, send_ref)
    out_block(places, 2, low_ref, full_ref, own_ref)


def out_near_kernel(places, attended, full_ref, own_ref, send_ref):
    out_block(places, 1, attended, full_ref, send_ref)
    out_block(places, 0, attended, full_ref, own_ref)


def out_block(places, step, attended, full_ref, out_ref):
    rows = attended[:, :, part(places[0] ^ step, BLOCK)].reshape(-1, BLOCK)
    out_ref[...] = inner_rows(rows, full_ref[...]).astype(out_ref.dtype)


def norm1_kernel(places, near, core, got, x00, x01, x10, x11, vec, a_ref, low_ref, normed_ref, scale_ref):
    for side, pair in ((0, (x00, x01)), (1, (x10, x11))):
        for end, x in enumerate(pair):
            block = 2 * (places[3] ^ side) + (places[4] ^ end)
            a_ref[:, part(block, BLOCK)] = x[...].T.astype(F32)
    residual = a_ref[...] + (near[...] + core[...].astype(F32) + got[...].astype(F32) + vec[0:1])
    mean_rows = jnp.mean(residual, axis=1, keepdims=True)
    spread = jnp.mean(residual * residual, axis=1, keepdims=True) - mean_rows * mean_rows
    scale_rows = lax.rsqrt(spread + norm_eps)
    normed = (residual - mean_rows) * scale_rows
    values = normed * vec[1:2] + vec[2:3]
    a_ref[...] = values
    low_ref[...] = values.astype(BF)
    normed_ref[...] = normed
    scale_ref[...] = scale_rows


def back_of_norm(grad_in, normed, scale_rows, gain_vec):
    scaled = grad_in * gain_vec
    first = jnp.mean(scaled, axis=1, keepdims=True)
    second = jnp.mean(scaled * normed, axis=1, keepdims=True)
    return scale_rows * (scaled - first - normed * second)


def add_sums(sums_ref, *arrays):
    @pl.when(pl.program_id(0) == 0)
    def _():
        sums_ref[...] = jnp.zeros_like(sums_ref)

    for index, values in enumerate(arrays):
        sums_ref[index : index + 1] += jnp.sum(values, axis=0, keepdims=True)


def norm2_kernel(places, near, core, got, a_ref, c0, c1, c2, c3, vec, here_ref, send_ref, grad_ref, low_ref, sums_ref):
    for index, piece in enumerate((c0, c1, c2, c3)):
        block = 2 * (places[3] ^ (index >> 1)) + (places[4] ^ (index & 1))
        grad_ref[:, part(block, BLOCK)] = piece[...].T.astype(F32)
    branch = near[...] + core[...].astype(F32) + got[...].astype(F32) + vec[3:4]
    residual = a_ref[...] + branch
    mean_rows = jnp.mean(residual, axis=1, keepdims=True)
    spread = jnp.mean(residual * residual, axis=1, keepdims=True) - mean_rows * mean_rows
    scale_rows = lax.rsqrt(spread + norm_eps)
    normed = (residual - mean_rows) * scale_rows
    grad_out = grad_ref[...]
    grad = back_of_norm(grad_out, normed, scale_rows, vec[4:5])
    add_sums(sums_ref, grad, grad_out * normed, grad_out)
    grad_ref[...] = normed * vec[4:5] + vec[5:6]
    for side in range(2):
        for end, ref in ((0, here_ref), (1, send_ref)):
            block = 2 * (places[3] ^ side) + (places[4] ^ end)
            ref[side] = grad_ref[:, part(block, BLOCK)].T.astype(BF)
    grad_ref[...] = grad
    low_ref[...] = grad.astype(BF)


def norm1_back_kernel(places, near, core, got, grad2, normed_ref, scale_ref, vec, sums2, low_ref, sums_ref):
    grad_in = grad2[...] + (near[...] + core[...].astype(F32) + got[...].astype(F32))
    normed = normed_ref[...]
    grad = back_of_norm(grad_in, normed, scale_ref[...], vec[1:2])
    add_sums(sums_ref, grad, grad_in * normed, grad_in)
    sums_ref[3:6] = sums2[0:3]
    low_ref[...] = grad.astype(BF)


def weight_grad_kernel(places, left_near, left_far, r0, r1, r2, r3, mine_ref, sent_ref, right):
    half = mine_ref.shape[2]

    @pl.when(pl.program_id(0) == 0)
    def _():
        for index, rows in enumerate((r0, r1, r2, r3)):
            here = slice(index * BLOCK, (index + 1) * BLOCK)
            right[0, here] = rows[:, part(places[2], half)]
            right[1, here] = rows[:, part(1 - places[2], half)]

    left = jnp.concatenate([left_near[...], left_far[...]], 0)
    sent_ref[0, :BLOCK] = inner_rows(left, right[1]).astype(BF)
    mine_ref[0, :BLOCK] = inner_rows(left, right[0]).astype(BF)
    if mine_ref.shape[1] > BLOCK:
        sums = jnp.sum(left.astype(F32), axis=0, keepdims=True)
        sums = jnp.broadcast_to(jnp.concatenate([sums, sums], 1), (8, half)).astype(BF)
        sent_ref[0, BLOCK:] = sums
        mine_ref[0, BLOCK:] = sums


def out_back_kernel(places, d0, d1, d2, d3, full_ref, attended, grad_ref, mine_ref, sent_ref):
    heads, head_rows, _ = attended.shape
    blocks = (d0, d1, d2, d3)
    left = []
    for step, rows in enumerate(blocks):
        here = part(places[0] ^ step, BLOCK)
        grad = against(full_ref[...], rows[...]).astype(BF)
        grad_ref[:, :, here] = grad.reshape(heads, head_rows, BLOCK)
        left.append(attended[:, :, here].reshape(-1, BLOCK))
    width = mine_ref.shape[3]
    for ref, side in ((sent_ref, 1 - places[2]), (mine_ref, places[2])):
        for end in range(2):
            columns = part(2 * side + (places[4] ^ end), width)
            total = None
            for piece, rows in zip(left, blocks):
                product = matmul(piece, rows[:, columns])
                total = product if total is None else total + product
            ref[:, end] = total.astype(BF).reshape(heads, head_rows, width)


def attend_back_kernel(
    places, qkv_ref, grad_ref, norm_ref, attended, out_mine, out_sent, x00, x01, x10, x11, sums, out_ref, mine_ref, sent_ref, probs_low, scores_low
):
    head_rows = qkv_ref.shape[2]
    key = qkv_ref[0, 1]
    key_t = key.T
    value_t = qkv_ref[0, 2].T
    for start in range(0, SEQ, BLOCK):
        here = slice(start, start + BLOCK)
        grad = grad_ref[0, :, here]
        probs = jnp.exp(matmul(key_t, qkv_ref[0, 0, :, here]) - norm_ref[0, :, here])
        delta = jnp.sum(grad.astype(F32) * attended[0, :, here], axis=0, keepdims=True)
        grad_scores = (probs * (matmul(value_t, grad) - delta)).astype(BF)
        probs_low[:, here] = probs.astype(BF)
        scores_low[:, here] = grad_scores
        grad_query = matmul(key, grad_scores).astype(BF)
        out_ref[0, :head_rows, here] = (grad_query.astype(F32) * HEAD_DIM**-0.5).astype(BF)
    grad_key = matmul(scores_low[...], qkv_ref[0, 0].T)
    out_ref[0, head_rows : 2 * head_rows] = grad_key.T.astype(BF)
    grad_value = matmul(probs_low[...], grad_ref[0].T)
    out_ref[0, 2 * head_rows :] = grad_value.T.astype(BF)
    left = out_ref[0]
    bias = jnp.sum(left.astype(F32), axis=1, keepdims=True)
    bias = jnp.concatenate([bias[:head_rows], bias[2 * head_rows :]], 0)
    bias = jnp.broadcast_to(bias, (2 * head_rows, 2 * head_rows)).T[:8]
    bias = jnp.concatenate([bias, jnp.zeros((8, BLOCK - 2 * head_rows), F32)], 1)
    rows = 3 * head_rows
    for side, pair in ((0, (x00, x01)), (1, (x10, x11))):
        mine = (places[3] ^ side) == places[2]
        for end, x in enumerate(pair):
            weight = matmul(left, x[...]).astype(BF)
            block = sums[:, part(2 * (places[3] ^ side) + (places[4] ^ end), BLOCK)]
            extra = jnp.concatenate([block, bias], 0).astype(BF)

            @pl.when(mine)
            def _():
                mine_ref[0, end, :rows] = weight
                mine_ref[0, end, rows : rows + 16] = extra
                mine_ref[0, end, rows + 16 :] = out_mine[0, end]

            @pl.when(jnp.logical_not(mine))
            def _():
                sent_ref[0, end, :rows] = weight
                sent_ref[0, end, rows : rows + 16] = extra
                sent_ref[0, end, rows + 16 :] = out_sent[0, end]


def tail_sum_kernel(places, early_mine, early_got, late_mine, late_got, own_ref, *sums):
    own_ref[...] = early_mine[0].astype(F32) + early_got[0].astype(F32)
    blocks = [(early_mine, early_got, i) for i in range(1, early_mine.shape[0])]
    blocks += [(late_mine, late_got, i) for i in range(late_mine.shape[0])]
    for ref, (mine, got, head) in zip(sums, blocks):
        ref[...] = (mine[head].astype(F32) + got[head].astype(F32)).astype(BF)


def sum_kernel(places, mine, got, own_ref, *sums):
    own_ref[...] = mine[0].astype(F32) + got[0].astype(F32)
    for block, ref in enumerate(sums):
        ref[...] = (mine[block + 1].astype(F32) + got[block + 1].astype(F32)).astype(BF)


def last_ff_kernel(places, *refs):
    here, there = refs[-2:]
    inputs = refs[:-2]
    half = len(inputs) // 2
    first = 0
    for pieces in (inputs[:half], inputs[half:]):
        total = pieces[0][...]
        for ref in pieces[1:]:
            total = total + ref[...].astype(F32)
        rows, width = total.shape[0], total.shape[1] // 2
        left, right = total[:, :width], total[:, width:]
        is_left = places[4] == 0
        here[first : first + rows] = jnp.where(is_left, left, right).astype(BF)
        there[first : first + rows] = jnp.where(is_left, right, left).astype(BF)
        first += rows


def last_sum_kernel(places, own_ref, *refs):
    total = own_ref[...]
    for ref in refs[:-2]:
        total = total + ref[...].astype(F32)
    refs[-2][...] = total[0].astype(BF)
    refs[-1][...] = total[1].astype(BF)


def input_near_kernel(places, own0, own1, send0, send1, grads0, grads1, d0, d1, d2, d3, own_ref, send_ref):
    def product(first, second):
        pairs = ((first, grads0), (second, grads1))
        flat = [[ref[...].reshape(-1, ref.shape[2]) for ref in pair] for pair in pairs]
        return inner_rows(*flat[0]) + inner_rows(*flat[1])

    send_ref[...] = product(send0, send1).astype(BF)
    own_ref[...] = product(own0, own1)
    block = 2 * places[3] + places[4]
    for step, d in enumerate((d0, d1, d2, d3)):
        here = part(places[0] ^ step, BLOCK)
        own_ref[:, here] += d[:, part(block, BLOCK)].T.astype(F32)


def last_ff_out_kernel(places, p0, p1, p2, p3, down_out, up_out, bias_out):
    for step, ref in enumerate((p0, p1, p2, p3)):
        quarter = places[0] ^ step
        down_out[part(quarter, BLOCK), :] = ref[:BLOCK].astype(F32)
        up_out[:, part(quarter, BLOCK)] = ref[BLOCK : 2 * BLOCK].astype(F32).T
        bias_out[:, part(quarter, BLOCK)] = ref[2 * BLOCK :].astype(F32)[0:1]


def last_kernel(places, p0, p1, p2, p3, qkv_out, qv_out, norm_out, out_out, turned):
    parts = (p0, p1, p2, p3)
    head = turned.shape[0] // 4
    for piece in range(3):
        for step, ref in enumerate(parts):
            turned[part(places[0] ^ step, head), :] = ref[piece * head : (piece + 1) * head].astype(F32)
        qkv_out[piece] = turned[...].T
    extra = [ref[3 * head : 3 * head + 16].astype(F32) for ref in parts]
    norm_out[...] = extra[0][:8] + extra[1][:8] + extra[2][:8] + extra[3][:8]
    lines = [[], []]
    for quarter in range(4):
        line = sum(
            jnp.where((places[0] ^ step) == quarter, extra[step][8:9], 0.0) for step in range(4)
        )
        lines[0].append(line[:, :head])
        lines[1].append(line[:, head : 2 * head])
    qv_out[...] = jnp.concatenate([jnp.concatenate(line, 1) for line in lines], 0)
    for step, ref in enumerate(parts):
        out_out[part(places[0] ^ step, head), :] = ref[3 * head + 16 :].astype(F32)


def to_far_chip(own, send):
    return (own + flip(send, "dp").astype(F32)).astype(BF)


def gather_rows(payload):
    size = lax.axis_size("row")
    return [payload] + [shift(payload, "row", step) for step in range(1, size)]


def move_rows(sums):
    return [shift(block, "row", -1 - i) for i, block in enumerate(sums)]


def spread_weights(mine, other):
    return spread_cores(mine, flip(other, "t"))


def spread_cores(mine, got):
    near = jnp.stack([mine, got])
    far = flip(near, "dp")
    return near[0], far[0], near[1], far[1]


def fast_shards(
    tokens,
    w_qkv,
    b_qv,
    w_out,
    b_out,
    norm1_gain,
    norm1_shift,
    w_up,
    b_up,
    w_down,
    b_down,
    norm2_gain,
    norm2_shift,
    cotangent,
):
    core, chip = lax.axis_index("dp"), lax.axis_index("t")
    u_index, row = lax.axis_index("u"), lax.axis_index("row")
    rows = lax.axis_size("row")
    quarter = 2 * chip + core
    other_quarter = 2 * (1 - chip) + core
    places = jnp.stack([quarter, other_quarter, u_index, core, chip, row]).astype(jnp.int32)
    feats = tokens.shape[0]
    width = 4 * feats
    half = 2 * feats
    own_rows = SEQ // 4
    swap_cores = [(2 * d + u, 2 * u + d) for d in range(2) for u in range(2)]
    head_rows = w_out.shape[0] // 4
    qkv_rows, out_rows, ff_rows = 3 * head_rows, head_rows, w_down.shape[0] // 4

    x00 = lax.ppermute(tokens, ("dp", "u"), swap_cores)

    attn_rows = qkv_rows + 16 + out_rows
    attn_keep, attn_send = kernel_call(
        prepare_attn_kernel,
        "prepare_attn",
        [((attn_rows, feats), BF)] * 2,
        places,
        w_qkv.transpose(1, 0, 2),
        b_qv,
        w_out,
        b_out,
        norm1_gain,
        norm1_shift,
        b_down,
        norm2_gain,
        norm2_shift,
        scratch=[pltpu.VMEM((3, 4 * head_rows, feats), BF)],
        vmem=60,
    )
    attn_got = flip(attn_send, "t")
    ff_keep, ff_send = kernel_call(
        prepare_ff_kernel, "prepare_ff", [((2 * ff_rows, feats), BF)] * 2, places, after(w_up, attn_send), w_down, vmem=60
    )
    ff_got = flip(ff_send, "t")
    attn_got = after(attn_got, x00)
    x10 = flip(x00, "dp")
    qkv_part = jnp.stack([attn_keep[: qkv_rows + 8], attn_got[: qkv_rows + 8]])
    cot = lax.ppermute(after(cotangent, qkv_part), ("dp", "u"), swap_cores)
    x01 = flip(after(x00, qkv_part), "t")
    x11 = flip(x01, "dp")
    cot = after(cot, x01)
    cot_parts = [cut(cot, quarter ^ j, own_rows, 1) for j in range(4)]
    cot_far = flip(jnp.stack([cot_parts[2], cot_parts[3]]), "t")
    cot_near = flip(jnp.stack([cot_parts[1], cot_far[1]]), "dp")

    ff_got = after(ff_got, qkv_part)
    qkv_own = jnp.stack(gather_rows(qkv_part))
    attn_both = in_order(chip, attn_keep[qkv_rows + 8 :], attn_got[qkv_rows + 8 :], 1)
    ff_both = in_order(chip, ff_keep, ff_got, 1)
    up_bias = lax.dynamic_index_in_dim(b_up.reshape(4, -1), quarter, 0, True)
    up_bias = jnp.pad(up_bias, ((0, 7), (0, half - ff_rows)))
    mixed_part = jnp.concatenate([attn_both, ff_both[:ff_rows], up_bias])
    mixed_pieces = gather_rows(after(mixed_part, qkv_own))
    qkv_far = flip(after(qkv_own, x01), "u")

    x_blocks = (x00, x01, x10, x11)
    pair_of_heads = rows // 2

    def attend(first, far_half):
        def of(shape):
            return pl.BlockSpec(
                shape, lambda step, places: (first + step,) + (0,) * (len(shape) - 1)
            )

        return kernel_call(
            attend_kernel,
            "attend",
            [
                ((pair_of_heads, 3, head_rows, SEQ), BF),
                ((pair_of_heads, head_rows, SEQ), F32),
                ((pair_of_heads, 1, SEQ), F32),
            ]
            + [((pair_of_heads, qkv_rows, feats), BF)] * 4,
            places,
            *x_blocks,
            qkv_own,
            far_half,
            grid=pair_of_heads,
            specs=[fixed((feats, SEQ))] * 4 + [of((1, 2, qkv_rows + 8, feats))] * 2,
            out_specs=[
                stepped((1, 3, head_rows, SEQ), 0),
                stepped((1, head_rows, SEQ), 0),
                stepped((1, 1, SEQ), 0),
            ]
            + [stepped((1, qkv_rows, feats), 0)] * 4,
            vmem=28,
            long=True,
        )

    qkv_early, attended_early, norm_early, *weight_early = attend(0, qkv_far)
    mixed_own = jnp.stack(after(mixed_pieces, norm_early, cot_near))
    down_pieces = gather_rows(after(ff_both[ff_rows:], mixed_own))
    vec_rows = 8 + out_rows
    out_own, up_own = mixed_own[:, :vec_rows], mixed_own[:, vec_rows:]
    out_far = flip(out_own, "u")
    up_far = flip(up_own, "u")
    far_late = after(qkv_far, mixed_own)
    qkv_late, attended_late, norm_late, *weight_late = attend(pair_of_heads, far_late)
    attended_late = after(attended_late, down_pieces[1], down_pieces[3:])
    bias_up = up_own[:, ff_rows, :ff_rows].reshape(1, -1).astype(F32)
    vec = in_order(u_index, out_own[0, :8], out_far[0, :8], 1).astype(F32)
    up_pair = [x[:, :ff_rows].reshape(rows * ff_rows, half) for x in (up_own, up_far)]
    up_full = in_order(u_index, *up_pair, 1)

    row_block = (own_rows, width)
    pair_outs = [(row_block, F32), (row_block, BF)]
    far_own, far_send, out_full, low_attended = kernel_call(
        out_far_kernel,
        "out_far",
        pair_outs + [((rows * head_rows, width), BF), ((rows, head_rows, SEQ), BF)],
        places,
        attended_early,
        attended_late,
        out_own,
        out_far,
    )
    sent = to_far_chip(far_own, far_send)
    near_attended = after(low_attended, sent, up_far, down_pieces)
    got = flip(sent, "t")
    near_own, near_send = kernel_call(
        out_near_kernel, "out_near", pair_outs, places, near_attended, out_full
    )
    down_own = jnp.stack(after(down_pieces, near_own))
    down_far = flip(down_own, "u").reshape(rows * ff_rows, half)
    down_full = in_order(u_index, down_own.reshape(rows * ff_rows, half), down_far, 1)
    near_got = flip(near_send, "dp")
    got = after(got, near_got, up_far, down_own)
    chunk = own_rows // 2
    row_chunk = stepped((chunk, width), 0)
    own_tokens = pl.BlockSpec((feats, chunk), lambda step, places: (0, 2 * places[0] + step))
    normed_a, low_a, normed1, scale1 = kernel_call(
        norm1_kernel,
        "norm1",
        [(row_block, F32), (row_block, BF), (row_block, F32), ((own_rows, 1), F32)],
        places,
        near_own,
        near_got,
        got,
        *x_blocks,
        vec,
        grid=2,
        specs=[row_chunk] * 3 + [own_tokens] * 4 + [fixed((8, width))],
        out_specs=[row_chunk] * 3 + [stepped((chunk, 1), 0)],
    )

    def up(rows_in):
        pre = against(rows_in, up_full) + bias_up
        cdf = 0.5 * (1.0 + lax.erf(pre * (0.5**0.5)))
        slope = cdf + pre * (jnp.exp(-0.5 * pre * pre) * 0.3989422804014327)
        return (pre * cdf).astype(BF), slope

    a0, a1, a2 = low_a, flip(low_a, "dp"), flip(low_a, "t")
    hidden_near, slope_near = up(jnp.concatenate([a0, a1]))
    a2 = after(a2, hidden_near)
    a3 = flip(a2, "dp")
    hidden_far, slope_far = up(jnp.concatenate([a2, a3]))
    far_send = matmul(hidden_far[own_rows:], down_full).astype(BF)
    sent = to_far_chip(matmul(hidden_far[:own_rows], down_full), far_send)
    near_hidden = after(hidden_near, sent)
    token_rows = kernel_call(
        turn_kernel, "turn", [((SEQ, feats), BF)] * 4, places, *after(x_blocks, near_hidden)
    )
    got = flip(sent, "t")
    near_got = flip(matmul(near_hidden[own_rows:], down_full).astype(BF), "dp")
    near_own = matmul(near_hidden[:own_rows], down_full)
    got = after(got, near_got, token_rows)
    turned_chunk = stepped((feats, chunk), 1)
    pair_chunk = stepped((2, feats, chunk), 2)
    result_here, result_send, grad_r2, low_g, sums2 = kernel_call(
        norm2_kernel,
        "norm2",
        [((2, feats, own_rows), BF)] * 2 + [(row_block, F32), (row_block, BF), ((8, width), F32)],
        places,
        near_own,
        near_got,
        got,
        normed_a,
        cot_parts[0],
        cot_far[0],
        cot_near[0],
        cot_near[1],
        vec,
        grid=2,
        specs=[row_chunk] * 4 + [turned_chunk] * 4 + [fixed((8, width))],
        out_specs=[pair_chunk] * 2 + [row_chunk] * 2 + [fixed((8, width))],
    )

    two_blocks = 2 * own_rows

    def weight_grad(near, far, blocks, extra):
        shape = (rows, ff_rows + extra, half)
        return kernel_call(
            weight_grad_kernel,
            "weight_grad",
            [(shape, BF)] * 2,
            places,
            near,
            far,
            *blocks,
            grid=rows,
            specs=[stepped((two_blocks, ff_rows), 1)] * 2 + [fixed(row_block)] * 4,
            out_specs=[stepped((1, *shape[1:]), 0)] * 2,
            scratch=[pltpu.VMEM((2, SEQ, half), BF)],
            long=True,
        )

    g0, g1, g2 = low_g, flip(low_g, "dp"), flip(low_g, "t")
    grad_pre_near = (against(jnp.concatenate([g0, g1]), down_full) * slope_near).astype(BF)
    g2 = after(g2, grad_pre_near)
    g3 = flip(g2, "dp")
    grad_pre_far = (against(jnp.concatenate([g2, g3]), down_full) * slope_far).astype(BF)
    far_send = matmul(grad_pre_far[own_rows:], up_full).astype(BF)
    sent = to_far_chip(matmul(grad_pre_far[:own_rows], up_full), far_send)
    near_pre = after(grad_pre_near, sent)
    got = flip(sent, "t")
    near_got = flip(matmul(near_pre[own_rows:], up_full).astype(BF), "dp")
    near_own = matmul(near_pre[:own_rows], up_full)
    hiddens, pres = after(((hidden_near, hidden_far), (near_pre, grad_pre_far)), near_own)
    down_mine, down_sent = weight_grad(*hiddens, (g0, g1, g2, g3), 0)
    down_got = flip(down_sent, "u")
    up_mine, up_sent = weight_grad(*pres, (a0, a1, a2, a3), 8)
    got = after(got, near_got, up_sent)
    low_r1, sums = kernel_call(
        norm1_back_kernel,
        "norm1_back",
        [(row_block, BF), ((8, width), F32)],
        places,
        near_own,
        near_got,
        got,
        grad_r2,
        normed1,
        scale1,
        vec,
        sums2,
        grid=2,
        specs=[row_chunk] * 5 + [stepped((chunk, 1), 0)] + [fixed((8, width))] * 2,
        out_specs=[row_chunk, fixed((8, width))],
    )

    d0, d1, d2 = low_r1, flip(low_r1, "dp"), flip(low_r1, "t")
    down_got = after(down_got, low_r1)
    up_sent, down_got = lax.optimization_barrier((up_sent, down_got))
    up_got = flip(up_sent, "u")
    d2 = after(d2, down_got)

    def sums_of(mine, got):
        shape = mine.shape[1:]
        return kernel_call(
            sum_kernel, "sum", [(shape, F32)] + [(shape, BF)] * (rows - 1), places, mine, got
        )

    d3 = flip(d2, "dp")
    d_blocks = (d0, d1, d2, d3)
    out_shape = (rows, 2, out_rows, feats)
    grad_att, out_mine, out_sent = kernel_call(
        out_back_kernel,
        "out_back",
        [((rows, head_rows, SEQ), BF)] + [(out_shape, BF)] * 2,
        places,
        *d_blocks,
        out_full,
        low_attended,
    )
    down_total, *down_sums = sums_of(down_mine, after(down_got, grad_att))
    grad_att = after(grad_att, down_sums)
    down_moved = move_rows(down_sums)
    extra_rows = qkv_rows + 16 + out_rows

    def attend_back(first, grad, qkv, log_norm, attended):
        def of(shape):
            return pl.BlockSpec(
                shape, lambda step, places: (first + step,) + (0,) * (len(shape) - 1)
            )

        return kernel_call(
            attend_back_kernel,
            "attend_back",
            [((pair_of_heads, qkv_rows, SEQ), BF)]
            + [((pair_of_heads, 2, extra_rows, feats), BF)] * 2,
            places,
            qkv,
            grad,
            log_norm,
            attended,
            out_mine,
            out_sent,
            *token_rows,
            sums,
            grid=pair_of_heads,
            specs=[
                stepped((1, 3, head_rows, SEQ), 0),
                of((1, head_rows, SEQ)),
                stepped((1, 1, SEQ), 0),
                stepped((1, head_rows, SEQ), 0),
                of((1, 2, out_rows, feats)),
                of((1, 2, out_rows, feats)),
            ]
            + [fixed((SEQ, feats))] * 4
            + [fixed((8, width))],
            out_specs=[stepped((1, qkv_rows, SEQ), 0)]
            + [stepped((1, 2, extra_rows, feats), 0)] * 2,
            scratch=[pltpu.VMEM((SEQ, SEQ), BF)] * 2,
            vmem=30,
            long=True,
        )

    result_far = flip(after(result_send, d3), "t")
    result_near = flip(jnp.stack([result_here[1], result_far[1]]), "dp")
    result_parts = [result_here[0], result_near[0], result_far[0], result_near[1]]

    grads_late, late_mine, late_sent = attend_back(
        pair_of_heads, grad_att, qkv_late, norm_late, attended_late
    )
    late_got = flip(late_sent, "u")
    up_total, *up_sums = sums_of(up_mine, after(up_got, late_sent))
    up_moved = move_rows(up_sums)
    early_att = after(grad_att, up_sums, down_moved, result_near)
    grads_early, early_mine, early_sent = attend_back(
        0, early_att, qkv_early, norm_early, attended_early
    )
    early_got = flip(after(early_sent, up_moved[0], up_moved[2:]), "u")
    sum_shape = (2, extra_rows, feats)
    early_own, *tail_sums = kernel_call(
        tail_sum_kernel,
        "tail_sum",
        [(sum_shape, F32)] + [(sum_shape, BF)] * (rows - 1),
        places,
        early_mine,
        early_got,
        late_mine,
        after(late_got, early_sent, up_moved),
    )
    moved = move_rows(tail_sums)

    def back_to(index, grads_early):
        pairs = ((weight_early[index], grads_early), (weight_late[index], grads_late))
        products = [
            inner_rows(w.reshape(-1, feats), grads.reshape(-1, SEQ)) for w, grads in pairs
        ]
        return products[0] + products[1]

    grads_now = after(grads_early, tail_sums)
    far_send = back_to(3, grads_now).astype(BF)
    sent = to_far_chip(back_to(1, grads_now), far_send)
    got = flip(sent, "t")
    near_own, near_send = kernel_call(
        input_near_kernel,
        "input_near",
        [((feats, SEQ), F32), ((feats, SEQ), BF)],
        places,
        weight_early[0],
        weight_late[0],
        weight_early[2],
        weight_late[2],
        after(grads_early, sent),
        grads_late,
        *d_blocks,
        vmem=24,
    )
    near_got = flip(near_send, "dp")
    result_seq = after(four_in_order(core, chip, result_parts, 1), tail_sums)
    result_out = lax.ppermute(result_seq, ("dp", "u"), swap_cores)
    ff_sums = kernel_call(
        last_ff_kernel,
        "last_ff",
        [((2 * ff_rows + 8, feats), BF)] * 2,
        places,
        after(down_total, near_own, result_out),
        *down_moved,
        up_total,
        *up_moved,
    )
    ff_got = flip(ff_sums[1], "t")
    got = after(got, moved, ff_got)
    grad_in = (near_own + near_got.astype(F32) + got.astype(F32)).astype(BF)
    grad_tokens = lax.ppermute(grad_in, ("dp", "u"), swap_cores)
    last_sums = kernel_call(
        last_sum_kernel,
        "last_sum",
        [(sum_shape[1:], BF)] * 2,
        places,
        after(early_own, grad_in),
        *moved,
    )
    last_got = flip(last_sums[1], "t")
    down_out, up_out, up_bias_out = kernel_call(
        last_ff_out_kernel,
        "last_ff_out",
        [((4 * ff_rows, feats), F32), ((feats, 4 * ff_rows), F32), ((1, 4 * ff_rows), F32)],
        places,
        *spread_cores(after(ff_sums[0], last_got), ff_got),
    )
    last_parts = spread_cores(after(last_sums[0], grad_tokens), last_got)
    grad_tokens = after(grad_tokens, last_parts[2]).astype(F32)
    qkv_out, qv_out, norm_out, out_out = kernel_call(
        last_kernel,
        "last",
        [
            ((3, feats, 4 * head_rows), F32),
            ((2, 4 * head_rows), F32),
            ((8, feats), F32),
            ((4 * out_rows, feats), F32),
        ],
        places,
        *last_parts,
        scratch=[pltpu.VMEM((4 * head_rows, feats), F32)],
    )
    return (
        result_out,
        grad_tokens,
        qkv_out.transpose(1, 0, 2),
        qv_out,
        out_out,
        norm_out[0],
        norm_out[1],
        norm_out[2],
        up_out,
        up_bias_out[0],
        down_out,
        norm_out[3],
        norm_out[4],
        norm_out[5],
    )


def solution(mesh):
    sizes = dict(mesh.shape)
    grouped = sizes["dp"] == 2 and sizes["col"] == 4 and D % (4 * sizes["row"] * HEAD_DIM) == 0
    if grouped:
        devices = mesh.devices.reshape(sizes["dp"], sizes["row"], 2, 2)
        inner_mesh, col, body = Mesh(devices, ("dp", "row", "u", "t")), ("u", "t"), fast_shards
    else:
        inner_mesh, col, body = mesh, "col", shards
    tokens_spec = P(col, ("dp", "row"))
    return jax.shard_map(
        body,
        mesh=inner_mesh,
        in_specs=(
            tokens_spec,
            P(col, None, "row"),
            P(None, "row"),
            P("row", col),
            P(col),
            P(col),
            P(col),
            P(col, "row"),
            P("row"),
            P("row", col),
            P(col),
            P(col),
            P(col),
            tokens_spec,
        ),
        out_specs=(
            tokens_spec,
            tokens_spec,
            P(col, None, "row"),
            P(None, "row"),
            P("row", col),
            P(col),
            P(col),
            P(col),
            P(col, "row"),
            P("row"),
            P("row", col),
            P(col),
            P(col),
            P(col),
        ),
        check_vma=False,
    )
```
